128 devices in a mesh: lat: 8 (over y_lo, x), lon: 16 (over y_hi, z, core).
Axes of the slice: x: 4, y: 4 (y_hi: 2, y_lo: 2; y = y_hi * 2 + y_lo), z: 4, core: 2. Of those that a mesh axis runs over, the one named last changes fastest.
Arguments:
- fine_field: bfloat16 [8, 144, 192, 192], P(None, 'lat', 'lon'), may hold values from -6 to 6
- qkv_weight: bfloat16 [2, 192, 576], replicated, may hold values from -0.4375 to 0.4375
- out_weight: bfloat16 [2, 192, 192], replicated, may hold values from -0.4375 to 0.4375
- up_weight: bfloat16 [2, 192, 768], replicated, may hold values from -0.4375 to 0.4375
- down_weight: bfloat16 [2, 768, 192], replicated, may hold values from -0.21875 to 0.21875
- norm_gain: float32 [2, 2, 192], replicated, may hold values from 0.1 to 1.9
- bias_table: float32 [2, 24, 4, 6, 3312], P(None, 'lat'), may hold values from -4 to 302
- bias_index: int32 [144, 144], replicated, may hold values from 0 to 3311, as said below
- merge_gain: float32 [768], replicated, may hold values from 0.1 to 1.9
- merge_weight: bfloat16 [768, 384], replicated, may hold values from -0.21875 to 0.21875
- column_order: int32 [768], replicated, may hold values from 0 to 767, as said below
Outputs:
- coarse_grid: bfloat16 [768, 72, 384], P('lon', 'lat')
The draws below stay inside these ranges and needn't reach their ends.
Inputs may be any that keep to these rules, and one draw needn't show every extreme that they name: `bias_index`: every one of the 3312 table entries is used by some pair. `column_order`: A permutation of the 768 coarse columns. Split into 16 blocks of 48 positions: the number of columns that a block takes at one coarse longitude depends only on that longitude modulo 6, and a block takes exactly 3 columns from every run of 6 consecutive coarse longitudes, around the globe.
All inputs are finite; a program needn't handle non-finite values.
Results may differ from the reference program's by a relative error of at most 0.02.
Values may be sent and summed in bfloat16 or wider, within the bound.
A program may use at most 128 MiB of HBM per device.

```python
import jax
import jax.numpy as jnp
from jax import lax

D = 192
HEADS = 6
FF = 768
Z = 8
WZ = 2
WLAT = 6
WLON = 12
TABLE = 3312
NLAT = 144
NLON = 192
NWLAT = 24
NWZ = 4
CLON_DEV = 6
CLON = 96
COLUMNS = 768
COLS_DEV = 48
PER_PEER = 3


def table_labels(key):
    return jax.random.permutation(jax.random.fold_in(key, 11), TABLE).astype(jnp.int32)


def draw_bias_index(key, part):
    relabel = table_labels(key)
    tokens = jnp.arange(WZ * WLAT * WLON, dtype=jnp.int32)
    level_pos = tokens // (WLAT * WLON)
    row_pos = tokens // WLON % WLAT
    col_pos = tokens % WLON
    relative = ((col_pos[:, None] - col_pos[None, :] + WLON - 1) * WLAT * WLAT + row_pos[:, None] * WLAT + row_pos[None, :]) * WZ * WZ + level_pos[:, None] * WZ + level_pos[None, :]
    return relabel[relative].astype(jnp.int32)


def draw_bias_table(key, part):
    key = jax.random.fold_in(key, 5)
    full_shape = (2, NWLAT, NWZ, HEADS, TABLE)
    base_key = jax.random.fold_in(key, 0)
    return jax.random.truncated_normal(base_key, -4.0, 4.0, full_shape, jnp.float32)


def draw_column_order(key, part):
    key = jax.random.fold_in(key, 7)
    pattern_key, level_key, rank_key = jax.random.split(key, 3)
    pattern = (jax.random.permutation(pattern_key, COLS_DEV).astype(jnp.int32) // PER_PEER).reshape(CLON_DEV, Z)
    lon_ids = jnp.arange(CLON, dtype=jnp.int32)
    level_perms = jax.vmap(lambda sub_key: jax.random.permutation(sub_key, Z))(jax.random.split(level_key, CLON)).astype(jnp.int32)
    targets = jnp.take_along_axis(pattern[lon_ids % CLON_DEV], level_perms, axis=1)
    targets = targets.T.reshape(-1)
    ranks = jax.random.permutation(rank_key, COLUMNS).astype(jnp.int32)
    return jnp.argsort(targets * COLUMNS + ranks).astype(jnp.int32)


def block_levels(rng, shape, shards, smallest, largest):
    def one(position, shards_of):
        steps = jax.random.uniform(jax.random.fold_in(jax.random.fold_in(rng, 6), position), (shards_of,), jnp.float32, smallest / len(shards), largest / len(shards))
        return jnp.repeat(jnp.exp(steps), shape[position] // shards_of).reshape((-1,) + (1,) * (len(shape) - position - 1))

    gain = one(*shards[0])
    for cut in shards[1:]:
        gain = gain * one(*cut)
    return gain


def centred(stream_key, shape, deviation, bound, pieces=(), held_as=jnp.bfloat16):
    loudness = block_levels(stream_key, shape, pieces, -0.22, 0.18) if pieces else 1.0
    values = jax.random.normal(stream_key, shape, jnp.float32) * deviation * loudness
    return jnp.minimum(jnp.maximum(values, -bound), bound).astype(held_as)


def setup_inputs(seed: int = 0) -> dict:
    seeds = jax.random.split(jax.random.key(seed), 12)
    return {
        "fine_field": centred(seeds[0], (Z, NLAT, NLON, D), 1.0, 6.0, ((1, 8), (2, 16))),
        "qkv_weight": centred(seeds[1], (2, D, 3 * D), D ** -0.5, 0.4375),
        "out_weight": centred(seeds[2], (2, D, D), D ** -0.5, 0.4375),
        "up_weight": centred(seeds[3], (2, D, FF), D ** -0.5, 0.4375),
        "down_weight": centred(seeds[4], (2, FF, D), FF ** -0.5, 0.21875),
        "norm_gain": jnp.clip(1.0 + 0.18 * jax.random.normal(seeds[5], (2, 2, D), jnp.float32), 0.1, 1.9),
        "bias_table": draw_bias_table(jax.random.fold_in(seeds[11], 71), 0),
        "bias_index": draw_bias_index(jax.random.fold_in(seeds[11], 71), 0),
        "merge_gain": jnp.clip(1.0 + 0.18 * jax.random.normal(seeds[8], (4 * D,), jnp.float32), 0.1, 1.9),
        "merge_weight": centred(seeds[9], (4 * D, 2 * D), (4 * D) ** -0.5, 0.21875),
        "column_order": draw_column_order(jax.random.fold_in(seeds[11], 71), 0),
    }


epsilon = 1e-05

def layer_norm(inputs, scale_gain):
    inputs = inputs.astype(jnp.float32)
    average = lax.optimization_barrier(jnp.mean(inputs, axis=-1, keepdims=True))
    centered = inputs - average
    variance = lax.optimization_barrier(jnp.mean(centered * centered, axis=-1, keepdims=True))
    return (centered * lax.rsqrt(variance + epsilon) * scale_gain).astype(jnp.bfloat16)

def window_block(lat_slab, tables, lat_label, level_label, qkv_mat, out_mat, up_mat, down_mat, gain_pair, pair_index):
    levels, row_count, col_count, channels = lat_slab.shape
    head_count = tables.shape[1]
    head_dim = channels // head_count
    level_wins = levels // WZ
    lon_wins = col_count // WLON
    window_tokens = WZ * row_count * WLON
    windows = lat_slab.reshape(level_wins, WZ, row_count, lon_wins, WLON, channels)
    windows = windows.transpose(0, 3, 1, 2, 4, 5).reshape(level_wins, lon_wins, window_tokens, channels)
    normed = layer_norm(windows, gain_pair[0])
    projected = jnp.einsum('altd,de->alte', normed.astype(jnp.float32), qkv_mat.astype(jnp.float32))
    projected = projected.astype(jnp.bfloat16).reshape(level_wins, lon_wins, window_tokens, 3, head_count, head_dim)
    queries = projected[:, :, :, 0].astype(jnp.float32)
    key_rows = projected[:, :, :, 1].astype(jnp.float32)
    value_rows = projected[:, :, :, 2].astype(jnp.float32)
    scores = jnp.einsum('althe,alshe->alhts', queries, key_rows) * (1.0 / head_dim ** 0.5)
    pair_bias = jnp.take(tables, pair_index, axis=2)
    scores = scores + pair_bias[:, None]
    lat_part = jnp.broadcast_to(lat_label[None, None, :, None], (level_wins, WZ, row_count, WLON))
    level_part = jnp.broadcast_to(level_label.reshape(level_wins, WZ)[:, :, None, None], (level_wins, WZ, row_count, WLON))
    region_code = (lat_part * 2 + level_part).reshape(level_wins, window_tokens)
    allowed = region_code[:, :, None] == region_code[:, None, :]
    scores = jnp.where(allowed[:, None, None], scores, jnp.float32(-1e+30))
    maxima = lax.optimization_barrier(jnp.max(scores, axis=-1, keepdims=True))
    powers = jnp.exp(scores - maxima)
    weights = (powers / lax.optimization_barrier(jnp.sum(powers, axis=-1, keepdims=True))).astype(jnp.bfloat16)
    attended = jnp.einsum('alhts,alshe->althe', weights.astype(jnp.float32), value_rows)
    attended = attended.astype(jnp.bfloat16).reshape(level_wins, lon_wins, window_tokens, channels)
    output_part = jnp.einsum('altd,de->alte', attended.astype(jnp.float32), out_mat.astype(jnp.float32))
    hidden = (windows.astype(jnp.float32) + output_part).astype(jnp.bfloat16)
    normed_two = layer_norm(hidden, gain_pair[1])
    expanded = jnp.einsum('altd,df->altf', normed_two.astype(jnp.float32), up_mat.astype(jnp.float32))
    activated = jax.nn.gelu(expanded).astype(jnp.bfloat16)
    shrunk = jnp.einsum('altf,fd->altd', activated.astype(jnp.float32), down_mat.astype(jnp.float32))
    result = (hidden.astype(jnp.float32) + shrunk).astype(jnp.bfloat16)
    result = result.reshape(level_wins, lon_wins, WZ, row_count, WLON, channels).transpose(0, 2, 3, 1, 4, 5)
    return result.reshape(levels, row_count, col_count, channels)

def reference(fine_field, qkv_weight, out_weight, up_weight, down_weight, norm_gain, bias_table, bias_index, merge_gain, merge_weight, column_order):
    levels, lat_total, lon_total, channels = fine_field.shape
    half_level = WZ // 2
    half_lat = WLAT // 2
    half_lon = WLON // 2
    current = fine_field
    for layer_index in range(2):
        if layer_index == 1:
            rolled = jnp.roll(current, (-half_level, -half_lat, -half_lon), axis=(0, 1, 2))
            lat_label = (jnp.arange(lat_total) >= lat_total - half_lat).astype(jnp.int32)
            level_label = (jnp.arange(levels) >= levels - half_level).astype(jnp.int32)
        else:
            rolled = current
            lat_label = jnp.zeros((lat_total,), jnp.int32)
            level_label = jnp.zeros((levels,), jnp.int32)
        slabs = rolled.reshape(levels, lat_total // WLAT, WLAT, lon_total, channels).transpose(1, 0, 2, 3, 4)
        labels = lat_label.reshape(lat_total // WLAT, WLAT)

        def one_slab(item, layer_index=layer_index, level_label=level_label):
            return window_block(item[0], item[1], item[2], level_label, qkv_weight[layer_index], out_weight[layer_index], up_weight[layer_index], down_weight[layer_index], norm_gain[layer_index], bias_index)
        outputs = lax.map(one_slab, (slabs, bias_table[layer_index], labels))
        current = outputs.transpose(1, 0, 2, 3, 4).reshape(levels, lat_total, lon_total, channels)
        if layer_index == 1:
            current = jnp.roll(current, (half_level, half_lat, half_lon), axis=(0, 1, 2))
    groups = current.reshape(levels, lat_total // 2, 2, lon_total // 2, 2, channels)
    joined = jnp.concatenate([groups[:, :, 0, :, 0], groups[:, :, 1, :, 0], groups[:, :, 0, :, 1], groups[:, :, 1, :, 1]], axis=-1)
    merge_norm = layer_norm(joined, merge_gain)
    merged = jnp.dot(merge_norm.reshape(-1, 4 * channels), merge_weight, preferred_element_type=jnp.float32)
    merged = merged.astype(jnp.bfloat16).reshape(levels, lat_total // 2, lon_total // 2, 2 * channels)
    columns = merged.transpose(0, 2, 1, 3).reshape(levels * (lon_total // 2), lat_total // 2, 2 * channels)
    return jnp.take(columns, column_order.astype(jnp.int32), axis=0)
```

```python
import functools
import jax
import jax.numpy as jnp
from jax import lax
from jax.experimental import pallas as pl
from jax.experimental.pallas import tpu as pltpu
from jax.sharding import PartitionSpec as P

WZ = 2
WLAT = 6
WLON = 12
epsilon = 1e-05
LOG2E = 1.4426950408889634
PITCH = 152
f32 = jnp.float32
bf16 = jnp.bfloat16


def lane_norm(x, gain):
    mean = jnp.mean(x, axis=-1, keepdims=True)
    cen = x - mean
    var = jnp.mean(cen * cen, axis=-1, keepdims=True)
    return (cen * lax.rsqrt(var + epsilon) * gain).astype(bf16)


def dot(a, b):
    return jnp.dot(a, b, preferred_element_type=f32)


def dot_t(a, b):
    return lax.dot_general(a, b, (((1,), (1,)), ((), ())), preferred_element_type=f32)


def gelu(v):
    u = v * (0.7978845608028654 + 0.035677408136300125 * (v * v))
    hv = 0.5 * v
    return hv + hv * jnp.tanh(u)


def qkv_rows(x, gain, wqkv):
    n = lane_norm(x, gain)
    p = dot(n, wqkv)
    q = (p[:, :192] * (LOG2E / 32**0.5)).astype(bf16)
    return jnp.concatenate([q, p[:, 192:].astype(bf16)], axis=1)


def attend(qkv, bias_main, bias_tail):
    q, k, v = qkv[:, :192], qkv[:, 192:384], qkv[:, 384:576]
    head = lax.broadcasted_iota(jnp.int32, (1, 192), 1) // 32
    zero = jnp.zeros((), bf16)
    group = lax.broadcasted_iota(jnp.int32, (144, 128), 1) // 16
    kt, vt = k[128:], v[128:]
    k_tail = jnp.concatenate([jnp.where(head == h, kt, zero) for h in range(6)], axis=0)
    v_all = jnp.concatenate([v[:128]] + [vt] * 8, axis=0)
    k_main = k[:128]
    tail = dot_t(q, jnp.concatenate([k_tail, jnp.zeros((32, 192), bf16)], axis=0)) + bias_tail
    mains, maxes = [], []
    for h in range(6):
        s = dot_t(jnp.where(head == h, q, zero), k_main) + bias_main(h)
        m = jnp.max(jnp.maximum(s, jnp.where(group == h, tail, -3.0e38)), axis=-1, keepdims=True)
        mains.append(s)
        maxes.append(m)
    mt = jnp.broadcast_to(maxes[0], (144, 128))
    for h in range(1, 6):
        mt = jnp.where(group == h, maxes[h], mt)
    pt = jnp.where(group < 6, jnp.exp2(tail - mt), 0.0)
    lane = lax.broadcasted_iota(jnp.int32, (144, 128), 1) // 32
    accs = [None, None]
    for h in range(6):
        p = jnp.exp2(mains[h] - maxes[h])
        ph = jnp.where(group == h, pt, 0.0)
        total = jnp.sum(p + ph, axis=-1, keepdims=True)
        lhs = jnp.concatenate([p.astype(bf16), ph.astype(bf16)], axis=1)
        half = h // 4
        rhs = v_all[:, :128] if half == 0 else v_all[:, 128:]
        o = dot(lhs, rhs) * (1.0 / total)
        if accs[half] is None:
            accs[half] = o
        else:
            accs[half] = jnp.where(lane[:, : o.shape[1]] == h - 4 * half, o, accs[half])
    return jnp.concatenate(accs, axis=1).astype(bf16)


def ffn_rows(x, att, wout, gain, wup, wdown):
    hidden = (x + dot(att, wout)).astype(bf16)
    hf = hidden.astype(f32)
    n = lane_norm(hf, gain)
    act = gelu(dot(n, wup)).astype(bf16)
    return hf + dot(act, wdown)


def passed_along(value, axis, steps):
    count = lax.axis_size(axis)
    pairs = [(source, (source + steps) % count) for source in range(count)]
    return lax.ppermute(value, axis, pairs)


def build_table(tb_ref, t_ref):
    def step(k, carry):
        k0 = pl.multiple_of(k * 128, 128)
        for b in range(2):
            blk = tb_ref[b, :, pl.ds(k0, 128)] * LOG2E
            blk = jnp.concatenate([blk, jnp.zeros((32, 128), f32)], 0)
            t_ref[pl.ds(2 * k0 + b, 128, stride=2), :] = blk.T
        return carry

    lax.fori_loop(0, 26, step, 0)


def gather_rows(idx_ref, t_ref, g_ref, t):
    for s in range(144):
        i = idx_ref.at[pl.ds(s, 20736 - 143)][t * 144]
        g_ref[pl.ds(2 * s, 2), :] = t_ref[pl.ds(pl.multiple_of(i, 2), 2), :]


def spread(g_ref, bm, bt, t, lane):
    for b in range(2):
        tr = g_ref[pl.ds(b, 128, stride=2), :].T
        for r in range(12):
            bm[b, pl.ds(r * 8 * PITCH + t, 8, stride=PITCH), :] = tr[r * 8 : r * 8 + 8]
        tail = g_ref[pl.ds(256 + b, 16, stride=2), :]
        tt = jnp.concatenate([tail] * 8, 0).T
        for half in range(2):
            acc = tt[half * 8 : half * 8 + 8]
            for h in range(1, 6):
                acc = jnp.where(lane == h, tt[h * 16 + half * 8 : h * 16 + half * 8 + 8], acc)
            bt[b, pl.ds(half * 8 * PITCH + t, 8, stride=PITCH), :] = acc


UN = 8


def expand_bias(idx_ref, tb_ref, t_ref, ga, gb, bm, bt):
    build_table(tb_ref, t_ref)
    lane = lax.broadcasted_iota(jnp.int32, (8, 128), 1) // 16
    gather_rows(idx_ref, t_ref, ga, 0)
    gs = [ga, gb]

    def step(u, carry):
        t = UN * u
        for k in range(UN):
            spread(gs[k % 2], bm, bt, t + k, lane)
            nxt = t + k + 1
            gather_rows(idx_ref, t_ref, gs[(k + 1) % 2], jnp.minimum(nxt, 143) if k == UN - 1 else nxt)
        return carry

    lax.fori_loop(0, 144 // UN, step, 0)


def mask_bias(bm, bt, last_lat):
    tok = lax.broadcasted_iota(jnp.int32, (144, 128), 0)
    key = lax.broadcasted_iota(jnp.int32, (144, 128), 1)
    key_t = 128 + key % 16

    def level(t):
        return t // 72

    def row(t):
        return ((t // 12) % 6) // 3

    def cut(w, code):
        differ = code(tok) != code(key)
        for h in range(6):
            at = pl.ds((h * 16 + w) * PITCH, 144)
            bm[1, at, :] = jnp.where(differ, -1e30, bm[1, at, :])
        at = pl.ds(w * PITCH, 144)
        bt[1, at, :] = jnp.where(code(tok) != code(key_t), -1e30, bt[1, at, :])

    for w in (3, 7, 11):
        cut(w, level)

    @pl.when(last_lat)
    def _():
        for w in (8, 9, 10, 11):
            cut(w, row)


def run_block(b, x_ref, y_ref, wq, wo, wu, wd, gains, bm, bt, bb, x3, qkv, att, ready):
    for li in range(3):
        for a in range(4):
            for zz in range(2):
                for r in range(6):
                    i = zz * 6 + r
                    x3[li * 4 + a, 12 * i : 12 * i + 12, :] = x_ref[2 * a + zz, 6 * li + r].astype(f32)

    def first(g, carry):
        x = x3[pl.ds(2 * g, 2)].reshape(288, 192)
        qkv[pl.ds(pl.multiple_of(g * 288, 288), 288), :] = qkv_rows(x, gains[b, 0:1, :], wq[b])
        return carry

    lax.fori_loop(0, 6, first, 0)
    ready()

    def second(w, carry):
        def main(h):
            return bm[bb, pl.ds(pl.multiple_of((h * 16 + w) * PITCH, 8), 144), :]

        rows = pl.ds(pl.multiple_of(w * 144, 144), 144)
        tail = bt[bb, pl.ds(pl.multiple_of(w * PITCH, 8), 144), :]
        att[rows, :] = attend(qkv[rows, :], main, tail)
        return carry

    lax.fori_loop(0, 12, second, 0)

    def third(g, carry):
        x = x3[pl.ds(2 * g, 2)].reshape(288, 192)
        rows = pl.ds(pl.multiple_of(g * 288, 288), 288)
        out = ffn_rows(x, att[rows, :], wo[b], gains[b, 1:2, :], wu[b], wd[b])
        x3[pl.ds(2 * g, 2)] = out.reshape(2, 144, 192)
        return carry

    lax.fori_loop(0, 6, third, 0)
    for li in range(3):
        for a in range(4):
            for zz in range(2):
                for r in range(6):
                    i = zz * 6 + r
                    y_ref[2 * a + zz, 6 * li + r] = x3[li * 4 + a, 12 * i : 12 * i + 12, :].astype(bf16)


def kernel_one(idx, tb, x, wq, wo, wu, wd, gains, y, bm_out, bt_out, t, ga, gb, bm, bt, x3, qkv, att, sems):
    expand_bias(idx, tb, t, ga, gb, bm, bt)
    mask_bias(bm, bt, lax.axis_index("lat") == lax.axis_size("lat") - 1)
    c1 = pltpu.make_async_copy(bm.at[1], bm_out, sems.at[0])
    c2 = pltpu.make_async_copy(bt.at[1], bt_out, sems.at[1])
    c1.start()
    c2.start()
    run_block(0, x, y, wq, wo, wu, wd, gains, bm, bt, 0, x3, qkv, att, lambda: None)
    c1.wait()
    c2.wait()


def kernel_two(bm_in, bt_in, x, wq, wo, wu, wd, gains, y, bm, bt, x3, qkv, att, sems):
    c1 = pltpu.make_async_copy(bm_in, bm.at[0], sems.at[0])
    c2 = pltpu.make_async_copy(bt_in, bt.at[0], sems.at[1])
    c1.start()
    c2.start()

    def ready():
        c1.wait()
        c2.wait()

    run_block(1, x, y, wq, wo, wu, wd, gains, bm, bt, 0, x3, qkv, att, ready)


VM = pl.BlockSpec(memory_space=pltpu.VMEM)
HB = pl.BlockSpec(memory_space=pl.ANY)
SM = pl.BlockSpec(memory_space=pltpu.SMEM)
PARAMS = pltpu.CompilerParams(vmem_limit_bytes=56 << 20)


def work_scratch(copies):
    return [
        pltpu.VMEM((copies, 96 * PITCH, 128), f32),
        pltpu.VMEM((copies, 16 * PITCH, 128), f32),
        pltpu.VMEM((12, 144, 192), f32),
        pltpu.VMEM((1728, 576), bf16),
        pltpu.VMEM((1728, 192), bf16),
        pltpu.SemaphoreType.DMA((2,)),
    ]


def block_one(idx, tables, x, wq, wo, wu, wd, gains):
    return pl.pallas_call(
        kernel_one,
        out_shape=[
            jax.ShapeDtypeStruct(x.shape, bf16),
            jax.ShapeDtypeStruct((96 * PITCH, 128), f32),
            jax.ShapeDtypeStruct((16 * PITCH, 128), f32),
        ],
        in_specs=[SM] + [VM] * 7,
        out_specs=[VM, HB, HB],
        scratch_shapes=[pltpu.VMEM((6656, 128), f32), pltpu.VMEM((288, 128), f32), pltpu.VMEM((288, 128), f32)]
        + work_scratch(2),
        compiler_params=PARAMS,
        name="bias_and_block",
    )(idx, tables, x, wq, wo, wu, wd, gains)


def block_two(bm, bt, x, wq, wo, wu, wd, gains):
    return pl.pallas_call(
        kernel_two,
        out_shape=jax.ShapeDtypeStruct(x.shape, bf16),
        in_specs=[HB, HB] + [VM] * 6,
        out_specs=VM,
        scratch_shapes=work_scratch(1),
        compiler_params=PARAMS,
        name="shifted_block",
    )(bm, bt, x, wq, wo, wu, wd, gains)


def layer_norm(inputs, scale_gain):
    inputs = inputs.astype(f32)
    average = jnp.mean(inputs, axis=-1, keepdims=True)
    centered = inputs - average
    variance = jnp.mean(centered * centered, axis=-1, keepdims=True)
    return (centered * lax.rsqrt(variance + epsilon) * scale_gain).astype(bf16)


def body(
    fine_field,
    qkv_weight,
    out_weight,
    up_weight,
    down_weight,
    norm_gain,
    bias_table,
    bias_index,
    merge_gain,
    merge_weight,
    column_order,
):
    levels, row_count, col_count, channels = fine_field.shape
    lon_count = lax.axis_size("lon")
    lon_place = lax.axis_index("lon")
    half_level = WZ // 2
    half_lat = WLAT // 2
    half_lon = WLON // 2
    tables = bias_table.reshape(2, 12, 6, 3312).transpose(0, 2, 1, 3)
    tables = jnp.pad(tables, ((0, 0), (0, 0), (0, 4), (0, 16))).reshape(2, 96, 3328)
    flat_index = (bias_index * 2).reshape(-1)
    weights = (qkv_weight, out_weight, up_weight, down_weight, norm_gain)
    one, bm, bt = block_one(flat_index, tables, fine_field, *weights)
    lon_next = passed_along(one[:, :, :half_lon], "lon", -1)
    rolled = jnp.concatenate([one[:, :, half_lon:], lon_next], axis=2)
    lat_next = passed_along(rolled[:, :half_lat], "lat", -1)
    rolled = jnp.concatenate([rolled[:, half_lat:], lat_next], axis=1)
    rolled = jnp.roll(rolled, -half_level, axis=0)
    second = block_two(bm, bt, rolled, *weights)
    second = jnp.roll(second, half_level, axis=0)
    lat_prev = passed_along(second[:, row_count - half_lat :], "lat", 1)
    second = jnp.concatenate([lat_prev, second[:, : row_count - half_lat]], axis=1)
    lat_cells = row_count // 2
    lon_cells = col_count // 2
    coarse_offset = half_lon // 2
    groups = second.reshape(levels, lat_cells, 2, lon_cells, 2, channels)
    joined = jnp.concatenate(
        [groups[:, :, 0, :, 0], groups[:, :, 1, :, 0], groups[:, :, 0, :, 1], groups[:, :, 1, :, 1]],
        axis=-1,
    )
    columns = joined.transpose(0, 2, 1, 3).reshape(levels * lon_cells, lat_cells, 4 * channels)
    merge_norm = layer_norm(columns, merge_gain)
    merged = jnp.einsum("pcf,fg->pcg", merge_norm, merge_weight, preferred_element_type=f32).astype(bf16)
    col_total = levels * lon_cells
    coarse_width = lon_cells * lon_count
    slots = jnp.arange(col_total, dtype=jnp.int32)
    local_ids = (
        slots // lon_cells * coarse_width + (lon_place * lon_cells + slots % lon_cells + coarse_offset) % coarse_width
    )
    places = jnp.arange(column_order.shape[0], dtype=jnp.int32)
    position = jnp.sum(jnp.where(column_order[:, None] == local_ids[None, :], places[:, None], 0), axis=0)
    rank = jnp.sum((position[None, :] < position[:, None]).astype(jnp.int32), axis=1)
    send = (slots[:, None] == rank[None, :]).astype(bf16)
    my_columns = lax.dynamic_slice_in_dim(column_order, lon_place * col_total, col_total)
    source = (my_columns % coarse_width - coarse_offset + coarse_width) % coarse_width // lon_cells
    order = source * col_total + slots
    placing = jnp.sum((order[None, :] < order[:, None]).astype(jnp.int32), axis=1)
    place = (slots[None, :] == placing[:, None]).astype(bf16)
    flat = merged.reshape(col_total, -1)
    outgoing = jnp.dot(send, flat, preferred_element_type=f32).astype(bf16)
    arrived = lax.all_to_all(outgoing.reshape(lon_count, -1, flat.shape[1]), "lon", split_axis=0, concat_axis=0, tiled=True)
    result = jnp.dot(place, arrived.reshape(col_total, -1), preferred_element_type=f32).astype(bf16)
    return result.reshape(col_total, lat_cells, -1)


def solution(mesh):
    in_specs = (
        P(None, "lat", "lon", None),
        P(),
        P(),
        P(),
        P(),
        P(),
        P(None, "lat", None, None, None),
        P(),
        P(),
        P(),
        P(),
    )
    out_specs = P("lon", "lat", None)
    return jax.shard_map(body, mesh=mesh, in_specs=in_specs, out_specs=out_specs, check_vma=False)
```

```python
import functools
import jax
import jax.numpy as jnp
from jax import lax
from jax.experimental import pallas as pl
from jax.experimental.pallas import tpu as pltpu
from jax.sharding import PartitionSpec as P

epsilon = 1e-05
LOG2E = 1.4426950408889634
PITCH = 152
f32 = jnp.float32
bf16 = jnp.bfloat16


def lane_norm(x, gain):
    mean = jnp.mean(x, axis=-1, keepdims=True)
    cen = x - mean
    var = jnp.mean(cen * cen, axis=-1, keepdims=True)
    return (cen * lax.rsqrt(var + epsilon) * gain).astype(bf16)


def dot(a, b):
    return jnp.dot(a, b, preferred_element_type=f32)


def dot_t(a, b):
    return lax.dot_general(a, b, (((1,), (1,)), ((), ())), preferred_element_type=f32)


def gelu(v):
    u = v * (0.7978845608028654 + 0.035677408136300125 * (v * v))
    hv = 0.5 * v
    return hv + hv * jnp.tanh(u)


def qkv_rows(x, gain, wqkv):
    n = lane_norm(x, gain)
    p = dot(n, wqkv)
    q = (p[:, :192] * (LOG2E / 32**0.5)).astype(bf16)
    return jnp.concatenate([q, p[:, 192:].astype(bf16)], axis=1)


def attend(qkv, rows, bias_main, bias_tail, k_tail, v_tail):
    head = lax.broadcasted_iota(jnp.int32, (1, 192), 1) // 32
    zero = jnp.zeros((), bf16)
    group = lax.broadcasted_iota(jnp.int32, (144, 128), 1) // 16
    rest = pl.ds(rows + 128, 16)
    kt, vt = qkv[rest, 192:384], qkv[rest, 384:576]
    for h in range(6):
        k_tail[16 * h : 16 * h + 16, :] = jnp.where(head == h, kt, zero)
        v_tail[16 * h : 16 * h + 16, :] = jnp.where(head == h, vt, zero)
    q = qkv[pl.ds(rows, 144), :192]
    k = qkv[pl.ds(rows, 128), 192:384]
    v = qkv[pl.ds(rows, 128), 384:576]
    tail = dot_t(q, k_tail[...]) + bias_tail
    mains, maxes = [], []
    for h in range(6):
        s = dot_t(jnp.where(head == h, q, zero), k) + bias_main(h)
        m = jnp.max(jnp.maximum(s, jnp.where(group == h, tail, -3.0e38)), axis=-1, keepdims=True)
        mains.append(s)
        maxes.append(m)
    mt = jnp.broadcast_to(maxes[0], (144, 128))
    for h in range(1, 6):
        mt = jnp.where(group == h, maxes[h], mt)
    pt = jnp.where(group < 6, jnp.exp2(tail - mt), 0.0)
    both = dot(pt.astype(bf16), v_tail[...])
    lane = lax.broadcasted_iota(jnp.int32, (144, 128), 1) // 32
    outs = []
    for half, heads in ((0, (0, 1, 2, 3)), (1, (4, 5))):
        at = slice(0, 128) if half == 0 else slice(128, 192)
        width = at.stop - at.start
        acc = inv = None
        for h in heads:
            p = jnp.exp2(mains[h] - maxes[h])
            r = 1.0 / jnp.sum(p + jnp.where(group == h, pt, 0.0), axis=-1, keepdims=True)
            o = dot(p.astype(bf16), v[:, at])
            if acc is None:
                acc, inv = o, jnp.broadcast_to(r, (144, width))
            else:
                mine = lane[:, :width] == h - 4 * half
                acc, inv = jnp.where(mine, o, acc), jnp.where(mine, r, inv)
        outs.append((acc + both[:, at]) * inv)
    return jnp.concatenate(outs, axis=1).astype(bf16)


def ffn_rows(x, att, wout, gain, wup, wdown_t):
    hidden = (x + dot(att, wout)).astype(bf16)
    hf = hidden.astype(f32)
    n = lane_norm(hf, gain)
    act = gelu(dot(n, wup)).astype(bf16)
    return (hf + dot_t(act, wdown_t)).astype(bf16).astype(f32)


MESH = pl.DeviceIdType.MESH
LI_ROWS = 24 * PITCH


def build_table(tb_ref, t_ref, piece):
    def rows(k0, width):
        for b in range(2):
            piece[b, :72, :width] = tb_ref[b, :, pl.ds(k0, width)] * LOG2E
            t_ref[pl.ds(2 * k0 + b, 128, stride=2), :] = piece[b].T

    def step(k, carry):
        rows(pl.multiple_of(k * 128, 128), 128)
        return carry

    piece[...] = jnp.zeros_like(piece)
    lax.fori_loop(0, 25, step, 0)
    rows(3200, 112)


def gather_rows(idx_ref, t_ref, g_ref, t):
    t3 = t_ref.reshape(3328, 2, 128)
    for s in range(144):
        i = idx_ref.at[pl.ds(s, 20736 - 143)][t * 144]
        g_ref[pl.ds(2 * s, 2), :] = t3[i]


def spread(g_ref, bm, bt, t, lane):
    for b in range(2):
        tr = g_ref[pl.ds(b, 128, stride=2), :].T
        for r in range(9):
            bm[b, pl.ds(r * 8 * PITCH + t, 8, stride=PITCH), :] = tr[r * 8 : r * 8 + 8]
        tail = g_ref[pl.ds(256 + b, 16, stride=2), :]
        tt = jnp.concatenate([tail] * 8, 0).T
        for li in range(3):
            v = [tt[(li * 3 + n) * 8 : (li * 3 + n) * 8 + 8] for n in range(3)]
            acc = jnp.where(lane < 2, v[0], jnp.where(lane < 4, v[1], v[2]))
            acc = jnp.where(lane % 2 == 0, acc, jnp.concatenate([acc[4:], acc[:4]], 0))
            bt[b, pl.ds(li * 8 * PITCH + t, 8, stride=PITCH), :] = acc


UN = 8


def expand_bias(idx_ref, tb_ref, t_ref, piece, ga, gb, bm, bt):
    build_table(tb_ref, t_ref, piece)
    lane8 = lax.broadcasted_iota(jnp.int32, (8, 128), 1) // 16
    gather_rows(idx_ref, t_ref, ga, 0)
    gs = [ga, gb]

    def step(u, carry):
        t = UN * u
        for k in range(UN):
            spread(gs[k % 2], bm, bt, t + k, lane8)
            nxt = t + k + 1
            gather_rows(idx_ref, t_ref, gs[(k + 1) % 2], jnp.minimum(nxt, 143) if k == UN - 1 else nxt)
        return carry

    lax.fori_loop(0, 144 // UN, step, 0)


def mask_bias(bm, bt, last_lat):
    tok = lax.broadcasted_iota(jnp.int32, (144, 128), 0)
    key = lax.broadcasted_iota(jnp.int32, (144, 128), 1)
    key_t = 128 + key % 16

    def level(t):
        return t // 72

    def row(t):
        return ((t // 12) % 6) // 3

    def cut(w, code):
        differ = code(tok) != code(key)
        for h in range(6):
            at = pl.ds(((w // 4) * 24 + h * 4 + w % 4) * PITCH, 144)
            bm[1, at, :] = jnp.where(differ, -1e30, bm[1, at, :])
        at = pl.ds((w // 4 * 8 + w % 4) * PITCH, 144)
        bt[1, at, :] = jnp.where(code(tok) != code(key_t), -1e30, bt[1, at, :])

    for w in (3, 7, 11):
        cut(w, level)

    @pl.when(last_lat)
    def _():
        for w in (8, 9, 10, 11):
            cut(w, row)


def block_rows(b, li, cur, ws, gains, bm, bt, qkv, att, k_tail, v_tail):
    wq, wo, wu, wd = ws

    def first(g, carry):
        x = cur[pl.ds(4 * li + 2 * g, 2)].reshape(288, 192)
        qkv[pl.ds(pl.multiple_of(g * 288, 288), 288), :] = qkv_rows(x, gains[b, 0:1, :], wq[b])
        return carry

    lax.fori_loop(0, 2, first, 0)

    def second(a, carry):
        def main(h):
            return bm[b, pl.ds(pl.multiple_of((li * 24 + h * 4 + a) * PITCH, 8), 144), :]

        start = pl.multiple_of(a * 144, 144)
        tail = bt[b, pl.ds(pl.multiple_of((li * 8 + a) * PITCH, 8), 144), :]
        att[pl.ds(start, 144), :] = attend(qkv, start, main, tail, k_tail, v_tail)
        return carry

    lax.fori_loop(0, 4, second, 0)

    def third(g, carry):
        x = cur[pl.ds(4 * li + 2 * g, 2)].reshape(288, 192)
        rows = pl.ds(pl.multiple_of(g * 288, 288), 288)
        out = ffn_rows(x, att[rows, :], wo[b], gains[b, 1:2, :], wu[b], wd[b])
        cur[pl.ds(4 * li + 2 * g, 2)] = out.reshape(2, 144, 192)
        return carry

    lax.fori_loop(0, 2, third, 0)


def split(ref, rows, x):
    ref[0, rows, :] = x[:, :128]
    ref[1, rows, :64] = x[:, 128:]


def kernel(
    idx, tb, gains, mgain, send_row, place_row, x_hbm, wq_hbm, wo_hbm, wu_hbm, wd_hbm, wm_hbm,
    out,
    table, piece, ga, gb, bm, bt, xin, xf, x3, y3, qkv, att, k_tail, v_tail, wq, wo, wu, wd, wm,
    stage, half_out, half_in, north_out, north_in, lines, back_out, back_in, back, cells, merged, fan_out, fan_in,
    load, half_s, half_r, north_s, north_r, back_s, back_r, fan_s, fan_r,
):
    lats, lons = lax.axis_size("lat"), lax.axis_size("lon")
    lat, lon = lax.axis_index("lat"), lax.axis_index("lon")
    up, down = lax.rem(lat + lats - 1, lats), lax.rem(lat + 1, lats)
    west, east = lax.rem(lon + lons - 1, lons), lax.rem(lon + 1, lons)

    barrier = pltpu.get_barrier_semaphore()
    greet = [(lat, lax.rem(lon + k, lons)) for k in range(1, 16)] + [(down, lon), (down, east), (up, lon)]
    for where in greet:
        pl.semaphore_signal(barrier, inc=1, device_id=where, device_id_type=MESH)

    pairs = [(x_hbm, xin), (wq_hbm, wq), (wo_hbm, wo), (wu_hbm, wu), (wd_hbm, wd), (wm_hbm, wm)]
    loads = [pltpu.make_async_copy(s, d, load.at[n]) for n, (s, d) in enumerate(pairs)]
    for c in loads:
        c.start()
    expand_bias(idx, tb, table, piece, ga, gb, bm, bt)
    mask_bias(bm, bt, lat == lats - 1)
    for c in loads:
        c.wait()
    pl.semaphore_wait(barrier, 18)
    ws = (wq, wo, wu, wd)

    split(xf, pl.ds(0, 1728), xin[...].reshape(1728, 192).astype(f32))
    xf[:, 1728:, :] = jnp.zeros((2, 32, 128), f32)

    def window(w, carry):
        for zz in range(2):
            for r in range(6):
                i = zz * 6 + r
                at = pl.ds((6 * (w // 4) + r) * 96 + 2 * (w % 4) + zz, 16, stride=8)
                x3[w, 12 * i : 12 * i + 12, :128] = xf[0, at, :][:12]
                x3[w, 12 * i : 12 * i + 12, 128:] = xf[1, at, :][:12, :64]
        return carry

    lax.fori_loop(0, 12, window, 0)
    stage[...] = jnp.zeros_like(stage)
    k_tail[...] = jnp.zeros_like(k_tail)
    v_tail[...] = jnp.zeros_like(v_tail)

    def half_copy(li, a, rh):
        target = jnp.where(li + rh == 0, up, lat)
        n = (li * 4 + a) * 2 + rh
        return pltpu.make_async_remote_copy(
            src_ref=half_out.at[n], dst_ref=half_in.at[n], send_sem=half_s.at[n], recv_sem=half_r.at[n],
            device_id=(target, west), device_id_type=MESH,
        )

    def north_copy(a):
        return pltpu.make_async_remote_copy(
            src_ref=north_out.at[a], dst_ref=north_in.at[a], send_sem=north_s.at[a], recv_sem=north_r.at[a],
            device_id=(up, lon), device_id_type=MESH,
        )

    def moved(a, zz):
        return (a, 0) if zz == 1 else ((a + 3) % 4, 1)

    def send_row_of_windows(li):
        for a in range(4):
            w = li * 4 + a
            for rh in range(2):
                for rr in range(3):
                    for zz in range(2):
                        at = 12 * (zz * 6 + 3 * rh + rr)
                        to = 6 * (rr * 2 + zz)
                        stage[a * 2 + rh, to : to + 6, :] = x3[w, at : at + 6, :]
                half_out[w * 2 + rh] = stage[a * 2 + rh].astype(bf16)
                half_copy(li, a, rh).start()

        @pl.when(li == 0)
        def _():
            for a in range(4):
                for rr in range(3):
                    for zz in range(2):
                        at = 12 * (zz * 6 + rr) + 6
                        to = 6 * (rr * 2 + zz)
                        stage[a, to : to + 6, :] = x3[a, at : at + 6, :]
                north_out[a] = stage[a].astype(bf16)
                north_copy(a).start()

        for a in range(4):
            for zz in range(2):
                a2, z2 = moved(a, zz)
                for r in range(3, 6):
                    at, to = 12 * (zz * 6 + r) + 6, 12 * (z2 * 6 + r - 3)
                    y3[li * 4 + a2, to : to + 6, :] = x3[li * 4 + a, at : at + 6, :]

        @pl.when(li > 0)
        def _():
            for a in range(4):
                for zz in range(2):
                    a2, z2 = moved(a, zz)
                    for r in range(3):
                        at, to = 12 * (zz * 6 + r) + 6, 12 * (z2 * 6 + r + 3)
                        y3[(li - 1) * 4 + a2, to : to + 6, :] = x3[li * 4 + a, at : at + 6, :]

    def place_half(li, block, a, rh, col):
        for rr in range(3):
            for zz in range(2):
                a2, z2 = moved(a, zz)
                to = 12 * (z2 * 6 + (rr if rh == 1 else rr + 3)) + col
                y3[li * 4 + a2, to : to + 6, :] = stage[block, 6 * (rr * 2 + zz) : 6 * (rr * 2 + zz) + 6, :]

    def receive_row_of_windows(li):
        nxt = lax.rem(li + 1, 3)
        for rh, source in ((1, li), (0, nxt)):
            for a in range(4):
                half_copy(source, a, rh).wait_recv()
                stage[a * 2 + rh] = half_in[(source * 4 + a) * 2 + rh].astype(f32)
                place_half(li, a * 2 + rh, a, rh, 6)

        @pl.when(li == 2)
        def _():
            for a in range(4):
                north_copy(a).wait_recv()
                stage[a] = north_in[a].astype(f32)
                place_half(li, a, a, 0, 0)

    def one(k, carry):
        li = lax.rem(k + 2, 3)
        block_rows(0, li, x3, ws, gains, bm, bt, qkv, att, k_tail, v_tail)
        send_row_of_windows(li)
        return carry

    lax.fori_loop(0, 3, one, 0)

    back_copy = pltpu.make_async_remote_copy(
        src_ref=back_out, dst_ref=back_in, send_sem=back_s.at[0], recv_sem=back_r.at[0],
        device_id=(down, lon), device_id_type=MESH,
    )

    def two(k, carry):
        li = lax.rem(k + 2, 3)
        receive_row_of_windows(li)
        block_rows(1, li, y3, ws, gains, bm, bt, qkv, att, k_tail, v_tail)

        @pl.when(li == 2)
        def _():
            for rr in range(3):
                for a in range(4):
                    for zz in range(2):
                        to = 12 * (rr * 8 + 2 * a + zz)
                        at = 12 * (zz * 6 + rr + 3)
                        lines[to : to + 12, :] = y3[8 + a, at : at + 12, :]
            back_out[...] = lines[...].astype(bf16)
            back_copy.start()

        return carry

    lax.fori_loop(0, 3, two, 0)
    back_copy.wait_recv()
    split(back, pl.ds(0, 288), back_in[...].astype(f32))
    for w in range(12):
        split(xf, pl.ds(w * 144, 144), y3[w])

    back[:, 288:, :] = jnp.zeros((2, 8, 128), f32)

    def line(rho, lev, par):
        if rho < 0:
            return back, pl.ds(12 * ((rho + 3) * 8 + lev) + par, 8, stride=2)
        at = ((rho // 6) * 4 + lev // 2) * 144 + 12 * ((lev % 2) * 6 + rho % 6)
        return xf, pl.ds(at + par, 8, stride=2)

    def level(z, carry):
        lev = lax.rem(z + 7, 8)
        for i in range(9):
            to = pl.ds(pl.multiple_of((i * 8 + z) * 8, 8), 8)
            for q in range(4):
                ref, at = line(2 * i - 3 + q % 2, lev, q // 2)
                cells[q, to, :128] = ref[0, at, :]
                cells[q, to, 128:] = ref[1, at, :][:, :64]
        return carry

    lax.fori_loop(0, 8, level, 0)

    def merge(g, carry):
        rows = pl.ds(pl.multiple_of(g * 144, 144), 144)
        xs = [cells[q, rows, :] for q in range(4)]
        mean = sum(jnp.sum(x, axis=-1, keepdims=True) for x in xs) * (1.0 / 768)
        cs = [x - mean for x in xs]
        var = sum(jnp.sum(c * c, axis=-1, keepdims=True) for c in cs) * (1.0 / 768)
        scale = lax.rsqrt(var + epsilon)
        total = None
        for q in range(4):
            part = dot((cs[q] * scale * mgain[q : q + 1, :]).astype(bf16), wm[q])
            total = part if total is None else total + part
        merged[rows, :] = total.astype(bf16)
        return carry

    lax.fori_loop(0, 4, merge, 0)

    pick = lax.broadcasted_iota(jnp.int32, (512, 576), 0) == send_row[...]
    fan = dot(jnp.where(pick, 1.0, 0.0).astype(bf16), merged[...])
    fan_out[...] = fan.astype(bf16).reshape(16, 32, 384)

    def fan_copy(k):
        peer = lax.rem(lon + k, lons)
        return pltpu.make_async_remote_copy(
            src_ref=fan_out.at[peer], dst_ref=fan_in.at[lon], send_sem=fan_s.at[k], recv_sem=fan_r.at[k],
            device_id=(lat, peer), device_id_type=MESH,
        )

    for k in range(1, 16):
        fan_copy(k).start()
    fan_in[lon] = fan_out[lon]
    for k in range(1, 16):
        fan_copy(k).wait_recv()
    slots = lax.broadcasted_iota(jnp.int32, (432, 512), 1) == place_row[...]
    out[...] = dot(jnp.where(slots, 1.0, 0.0).astype(bf16), fan_in[...].reshape(512, 384)).astype(bf16).reshape(9, 48, 384)

    for n in range(24):
        half_copy(n // 8, (n // 2) % 4, n % 2).wait_send()
    for a in range(4):
        north_copy(a).wait_send()
    back_copy.wait_send()
    for k in range(1, 16):
        fan_copy(k).wait_send()


VM = pl.BlockSpec(memory_space=pltpu.VMEM)
HB = pl.BlockSpec(memory_space=pl.ANY)
SM = pl.BlockSpec(memory_space=pltpu.SMEM)


def whole(idx, tables, gains, mgain, send_row, place_row, x, wq, wo, wu, wd, wm):
    v = pltpu.VMEM
    dma = pltpu.SemaphoreType.DMA
    return pl.pallas_call(
        kernel,
        out_shape=jax.ShapeDtypeStruct((9, 48, 384), bf16),
        in_specs=[SM] + [VM] * 5 + [HB] * 6,
        out_specs=VM,
        scratch_shapes=[
            v((6656, 128), f32),
            v((2, 128, 128), f32),
            v((288, 128), f32),
            v((288, 128), f32),
            v((2, 72 * PITCH, 128), f32),
            v((2, 24 * PITCH, 128), f32),
            v(x.shape, bf16),
            v((2, 1760, 128), f32),
            v((12, 144, 192), f32),
            v((12, 144, 192), f32),
            v((576, 576), bf16),
            v((576, 192), bf16),
            v((128, 192), bf16),
            v((128, 192), bf16),
            v(wq.shape, bf16),
            v(wo.shape, bf16),
            v(wu.shape, bf16),
            v(wd.shape, bf16),
            v(wm.shape, bf16),
            v((8, 48, 192), f32),
            v((24, 48, 192), bf16),
            v((24, 48, 192), bf16),
            v((4, 48, 192), bf16),
            v((4, 48, 192), bf16),
            v((288, 192), f32),
            v((288, 192), bf16),
            v((288, 192), bf16),
            v((2, 296, 128), f32),
            v((4, 576, 192), f32),
            v((576, 384), bf16),
            v((16, 32, 384), bf16),
            v((16, 32, 384), bf16),
            dma((6,)),
            dma((24,)),
            dma((24,)),
            dma((4,)),
            dma((4,)),
            dma((1,)),
            dma((1,)),
            dma((16,)),
            dma((16,)),
        ],
        compiler_params=pltpu.CompilerParams(vmem_limit_bytes=60 << 20, collective_id=0, has_side_effects=True),
        name="whole_pair",
    )(idx, tables, gains, mgain, send_row, place_row, x, wq, wo, wu, wd, wm)


def body(
    fine_field,
    qkv_weight,
    out_weight,
    up_weight,
    down_weight,
    norm_gain,
    bias_table,
    bias_index,
    merge_gain,
    merge_weight,
    column_order,
):
    lon_count = lax.axis_size("lon")
    lon_place = lax.axis_index("lon")
    cells, coarse, offset = 6, 96, 3
    col_total = 48
    slots = jnp.arange(col_total, dtype=jnp.int32)
    local_ids = slots // cells * coarse + (lon_place * cells + slots % cells + offset) % coarse
    places = jnp.arange(column_order.shape[0], dtype=jnp.int32)
    position = jnp.sum(jnp.where(column_order[:, None] == local_ids[None, :], places[:, None], 0), axis=0)
    rank = jnp.sum((position[None, :] < position[:, None]).astype(jnp.int32), axis=1)
    send_at = rank // 3 * 32 + rank % 3
    rows = 3 * jnp.arange(9, dtype=jnp.int32)
    send_at = jnp.pad(send_at.reshape(8, 6), ((0, 0), (0, 2)), constant_values=-1000).reshape(-1)
    send_row = (rows[:, None] + send_at[None, :]).reshape(1, 576)
    my_columns = lax.dynamic_slice_in_dim(column_order, lon_place * col_total, col_total)
    source = (my_columns % coarse - offset + coarse) % coarse // cells
    order = source * col_total + slots
    placing = jnp.sum((order[None, :] < order[:, None]).astype(jnp.int32), axis=1)
    place_at = placing // 3 * 32 + placing % 3
    place_row = (rows[:, None] + place_at[None, :]).reshape(432, 1)
    result = whole(
        bias_index.reshape(-1),
        bias_table.transpose(0, 1, 3, 2, 4).reshape(2, 72, 3312),
        norm_gain,
        merge_gain.reshape(4, 192),
        send_row,
        place_row,
        fine_field.transpose(1, 2, 0, 3),
        qkv_weight,
        out_weight,
        up_weight,
        down_weight.transpose(0, 2, 1),
        merge_weight.reshape(4, 192, 384),
    )
    return result.transpose(1, 0, 2)


def solution(mesh):
    in_specs = (
        P(None, "lat", "lon", None),
        P(),
        P(),
        P(),
        P(),
        P(),
        P(None, "lat", None, None, None),
        P(),
        P(),
        P(),
        P(),
    )
    out_specs = P("lon", "lat", None)
    return jax.shard_map(body, mesh=mesh, in_specs=in_specs, out_specs=out_specs, check_vma=False)
```

```python
import functools
import jax
import jax.numpy as jnp
from jax import lax
from jax.experimental import pallas as pl
from jax.experimental.pallas import tpu as pltpu
from jax.sharding import PartitionSpec as P

epsilon = 1e-05
LOG2E = 1.4426950408889634
PITCH = 152
f32 = jnp.float32
bf16 = jnp.bfloat16


def lane_norm(x, gain):
    mean = jnp.mean(x, axis=-1, keepdims=True)
    cen = x - mean
    var = jnp.mean(cen * cen, axis=-1, keepdims=True)
    return (cen * lax.rsqrt(var + epsilon) * gain).astype(bf16)


def dot(a, b):
    return jnp.dot(a, b, preferred_element_type=f32)


def dot_t(a, b):
    return lax.dot_general(a, b, (((1,), (1,)), ((), ())), preferred_element_type=f32)


def gelu(v):
    u = v * (0.7978845608028654 + 0.035677408136300125 * (v * v))
    hv = 0.5 * v
    return hv + hv * jnp.tanh(u)


def qkv_rows(x, gain, wqkv):
    n = lane_norm(x, gain)
    p = dot(n, wqkv)
    q = (p[:, :192] * (LOG2E / 32**0.5)).astype(bf16)
    return jnp.concatenate([q, p[:, 192:].astype(bf16)], axis=1)


def attend(qkv, rows, bias_main, bias_tail, k_tail, v_tail):
    head = lax.broadcasted_iota(jnp.int32, (1, 192), 1) // 32
    zero = jnp.zeros((), bf16)
    group = lax.broadcasted_iota(jnp.int32, (144, 128), 1) // 16
    rest = pl.ds(rows + 128, 16)
    kt, vt = qkv[rest, 192:384], qkv[rest, 384:576]
    for h in range(6):
        k_tail[16 * h : 16 * h + 16, :] = jnp.where(head == h, kt, zero)
        v_tail[16 * h : 16 * h + 16, :] = jnp.where(head == h, vt, zero)
    q = qkv[pl.ds(rows, 144), :192]
    k = qkv[pl.ds(rows, 128), 192:384]
    v = qkv[pl.ds(rows, 128), 384:576]
    tail = dot_t(q, k_tail[...]) + bias_tail
    mains, maxes = [], []
    for h in range(6):
        s = dot_t(jnp.where(head == h, q, zero), k) + bias_main(h)
        m = jnp.max(jnp.maximum(s, jnp.where(group == h, tail, -3.0e38)), axis=-1, keepdims=True)
        mains.append(s)
        maxes.append(m)
    mt = jnp.broadcast_to(maxes[0], (144, 128))
    for h in range(1, 6):
        mt = jnp.where(group == h, maxes[h], mt)
    pt = jnp.where(group < 6, jnp.exp2(tail - mt), 0.0)
    both = dot(pt.astype(bf16), v_tail[...])
    lane = lax.broadcasted_iota(jnp.int32, (144, 128), 1) // 32
    outs = []
    for half, heads in ((0, (0, 1, 2, 3)), (1, (4, 5))):
        at = slice(0, 128) if half == 0 else slice(128, 192)
        width = at.stop - at.start
        acc = inv = None
        for h in heads:
            p = jnp.exp2(mains[h] - maxes[h])
            r = 1.0 / jnp.sum(p + jnp.where(group == h, pt, 0.0), axis=-1, keepdims=True)
            o = dot(p.astype(bf16), v[:, at])
            if acc is None:
                acc, inv = o, jnp.broadcast_to(r, (144, width))
            else:
                mine = lane[:, :width] == h - 4 * half
                acc, inv = jnp.where(mine, o, acc), jnp.where(mine, r, inv)
        outs.append((acc + both[:, at]) * inv)
    return jnp.concatenate(outs, axis=1).astype(bf16)


def ffn_rows(x, att, wout, gain, wup, wdown_t):
    hidden = (x + dot(att, wout)).astype(bf16)
    hf = hidden.astype(f32)
    n = lane_norm(hf, gain)
    act = gelu(dot(n, wup)).astype(bf16)
    return (hf + dot_t(act, wdown_t)).astype(bf16).astype(f32)


MESH = pl.DeviceIdType.MESH
LI_ROWS = 24 * PITCH


def build_table(tb_ref, t_ref, piece):
    def rows(k0, width):
        for b in range(2):
            for n in range(18):
                piece[b, 4 * n : 4 * n + 4, :width] = tb_ref[b, n // 6, n % 6, :, pl.ds(k0, width)]
            t_ref[pl.ds(2 * k0 + b, 128, stride=2), :] = (piece[b] * LOG2E).T

    def step(k, carry):
        rows(pl.multiple_of(k * 128, 128), 128)
        return carry

    piece[...] = jnp.zeros_like(piece)
    lax.fori_loop(0, 25, step, 0)
    rows(3200, 112)


def gather_rows(idx_ref, t_ref, g_ref, t):
    t3 = t_ref.reshape(3328, 2, 128)
    for s in range(144):
        i = idx_ref.at[pl.ds(s, 20736 - 143)][t * 144]
        g_ref[pl.ds(2 * s, 2), :] = t3[i]


def spread(g_ref, bm, bt, t, lane):
    for b in range(2):
        tr = g_ref[pl.ds(b, 128, stride=2), :].T
        for r in range(9):
            bm[b, pl.ds(r * 8 * PITCH + t, 8, stride=PITCH), :] = tr[r * 8 : r * 8 + 8]
        tail = g_ref[pl.ds(256 + b, 16, stride=2), :]
        tt = jnp.concatenate([tail] * 8, 0).T
        for li in range(3):
            v = [tt[(li * 3 + n) * 8 : (li * 3 + n) * 8 + 8] for n in range(3)]
            acc = jnp.where(lane < 2, v[0], jnp.where(lane < 4, v[1], v[2]))
            acc = jnp.where(lane % 2 == 0, acc, jnp.concatenate([acc[4:], acc[:4]], 0))
            bt[b, pl.ds(li * 8 * PITCH + t, 8, stride=PITCH), :] = acc


UN = 8


def expand_bias(idx_ref, tb_ref, t_ref, piece, ga, gb, bm, bt):
    build_table(tb_ref, t_ref, piece)
    lane8 = lax.broadcasted_iota(jnp.int32, (8, 128), 1) // 16
    gather_rows(idx_ref, t_ref, ga, 0)
    gs = [ga, gb]

    def step(u, carry):
        t = UN * u
        for k in range(UN):
            spread(gs[k % 2], bm, bt, t + k, lane8)
            nxt = t + k + 1
            gather_rows(idx_ref, t_ref, gs[(k + 1) % 2], jnp.minimum(nxt, 143) if k == UN - 1 else nxt)
        return carry

    lax.fori_loop(0, 144 // UN, step, 0)


def mask_bias(bm, bt, last_lat):
    tok = lax.broadcasted_iota(jnp.int32, (144, 128), 0)
    key = lax.broadcasted_iota(jnp.int32, (144, 128), 1)
    key_t = 128 + key % 16

    def level(t):
        return t // 72

    def row(t):
        return ((t // 12) % 6) // 3

    def cut(w, code):
        differ = code(tok) != code(key)
        for h in range(6):
            at = pl.ds(((w // 4) * 24 + h * 4 + w % 4) * PITCH, 144)
            bm[1, at, :] = jnp.where(differ, -1e30, bm[1, at, :])
        at = pl.ds((w // 4 * 8 + w % 4) * PITCH, 144)
        bt[1, at, :] = jnp.where(code(tok) != code(key_t), -1e30, bt[1, at, :])

    for w in (3, 7, 11):
        cut(w, level)

    @pl.when(last_lat)
    def _():
        for w in (8, 9, 10, 11):
            cut(w, row)


def block_rows(b, li, cur, ws, gains, bm, bt, qkv, att, k_tail, v_tail):
    wq, wo, wu, wd = ws

    def first(g, carry):
        x = cur[pl.ds(4 * li + 2 * g, 2)].reshape(288, 192)
        qkv[pl.ds(pl.multiple_of(g * 288, 288), 288), :] = qkv_rows(x, gains[b, 0:1, :], wq[b])
        return carry

    lax.fori_loop(0, 2, first, 0)

    def second(a, carry):
        def main(h):
            return bm[b, pl.ds(pl.multiple_of((li * 24 + h * 4 + a) * PITCH, 8), 144), :]

        start = pl.multiple_of(a * 144, 144)
        tail = bt[b, pl.ds(pl.multiple_of((li * 8 + a) * PITCH, 8), 144), :]
        att[pl.ds(start, 144), :] = attend(qkv, start, main, tail, k_tail, v_tail)
        return carry

    lax.fori_loop(0, 4, second, 0)

    def third(g, carry):
        x = cur[pl.ds(4 * li + 2 * g, 2)].reshape(288, 192)
        rows = pl.ds(pl.multiple_of(g * 288, 288), 288)
        out = ffn_rows(x, att[rows, :], wo[b], gains[b, 1:2, :], wu[b], wd[b])
        cur[pl.ds(4 * li + 2 * g, 2)] = out.reshape(2, 144, 192)
        return carry

    lax.fori_loop(0, 2, third, 0)


PARTS = ((0, 1, 2, 3, 8), (4, 5, 6, 7))


def less(a, b, axis):
    return jnp.sum(jnp.where(a < b, 1.0, 0.0), axis=axis, keepdims=True)


def thirds(rank):
    peer = jnp.floor((rank + 0.5) * (1.0 / 3))
    return 13.0 * peer + rank


def column_places(order_ref, lon, send_ref, place_ref):
    order = order_ref[...].astype(f32)
    row = lax.broadcasted_iota(jnp.int32, (128, 1), 0)
    lane = lax.broadcasted_iota(jnp.int32, (128, 768), 1)
    level, col = (row % 64) // 8, row % 8
    wide = lon * 6 + col + 3
    ids = level * 96 + jnp.where(wide >= 96, wide - 96, wide)
    hit = order == ids.astype(f32)
    place = jnp.sum(jnp.where(hit, lane.astype(f32), 0.0), axis=1, keepdims=True)
    place = jnp.where(col < 6, place, 1e6)
    across = jnp.broadcast_to(place, (128, 128))
    send_ref[...] = jnp.broadcast_to(thirds(less(across[:64], across.T[:1], 0)), (8, 128))
    mine = jnp.sum(jnp.where(lane == lon * 48 + row, order, 0.0), axis=1, keepdims=True)
    east = mine - 96.0 * jnp.floor((mine + 0.5) * (1.0 / 96)) - 3.0
    east = jnp.where(east < 0.0, east + 96.0, east)
    key = jnp.floor((east + 0.5) * (1.0 / 6)) * 48.0 + row.astype(f32)
    key = jnp.where(row < 48, key, 1e6)
    across = jnp.broadcast_to(key, (128, 128))
    at = thirds(less(across.T[:1], key, 1))
    place_ref[...] = jnp.broadcast_to(at[:48], (48, 128))


def split(ref, rows, x):
    ref[0, rows, :] = x[:, :128]
    ref[1, rows, :64] = x[:, 128:]


def kernel(
    idx, tb, gains, mgain, order, x_hbm, wq_hbm, wo_hbm, wu_hbm, wd_hbm, wm_hbm,
    out,
    table, piece, ga, gb, bm, bt, xin, xf, x3, y3, qkv, att, k_tail, v_tail, wq, wo, wu, wd, wm,
    stage, half_out, half_in, north_out, north_in, lines, back_out, back_in, back, cells, merged, fan_out, fan_in, send_at, place_at,
    load, half_s, half_r, north_s, north_r, back_s, back_r, fan_s, fan_r,
):
    lats, lons = lax.axis_size("lat"), lax.axis_size("lon")
    lat, lon = lax.axis_index("lat"), lax.axis_index("lon")
    up, down = lax.rem(lat + lats - 1, lats), lax.rem(lat + 1, lats)
    west, east = lax.rem(lon + lons - 1, lons), lax.rem(lon + 1, lons)

    barrier = pltpu.get_barrier_semaphore()
    greet = [(lat, lax.rem(lon + k, lons)) for k in range(1, 16)] + [(down, lon), (down, east), (up, lon)]
    for where in greet:
        pl.semaphore_signal(barrier, inc=1, device_id=where, device_id_type=MESH)

    pairs = [(x_hbm, xin), (wq_hbm, wq), (wo_hbm, wo), (wu_hbm, wu), (wd_hbm, wd), (wm_hbm, wm)]
    loads = [pltpu.make_async_copy(s, d, load.at[n]) for n, (s, d) in enumerate(pairs)]
    for c in loads:
        c.start()
    column_places(order, lon, send_at, place_at)
    expand_bias(idx, tb, table, piece, ga, gb, bm, bt)
    mask_bias(bm, bt, lat == lats - 1)
    for c in loads:
        c.wait()
    pl.semaphore_wait(barrier, 18)
    ws = (wq, wo, wu, wd)

    split(xf, pl.ds(0, 1728), xin[...].reshape(1728, 192).astype(f32))
    def window(w, carry):
        for zz in range(2):
            for r in range(6):
                i = zz * 6 + r
                at = pl.ds((6 * (w // 4) + r) * 96 + 2 * (w % 4) + zz, 16, stride=8)
                x3[w, 12 * i : 12 * i + 12, :128] = xf[0, at, :][:12]
                x3[w, 12 * i : 12 * i + 12, 128:] = xf[1, at, :][:12, :64]
        return carry

    lax.fori_loop(0, 12, window, 0)
    stage[...] = jnp.zeros_like(stage)
    k_tail[...] = jnp.zeros_like(k_tail)
    v_tail[...] = jnp.zeros_like(v_tail)

    def half_copy(li, a, rh):
        target = jnp.where(li + rh == 0, up, lat)
        n = (li * 4 + a) * 2 + rh
        return pltpu.make_async_remote_copy(
            src_ref=half_out.at[n], dst_ref=half_in.at[n], send_sem=half_s.at[n], recv_sem=half_r.at[n],
            device_id=(target, west), device_id_type=MESH,
        )

    def north_copy(a):
        return pltpu.make_async_remote_copy(
            src_ref=north_out.at[a], dst_ref=north_in.at[a], send_sem=north_s.at[a], recv_sem=north_r.at[a],
            device_id=(up, lon), device_id_type=MESH,
        )

    def moved(a, zz):
        return (a, 0) if zz == 1 else ((a + 3) % 4, 1)

    def send_row_of_windows(li):
        for a in range(4):
            w = li * 4 + a
            for rh in range(2):
                for rr in range(3):
                    for zz in range(2):
                        at = 12 * (zz * 6 + 3 * rh + rr)
                        to = 6 * (rr * 2 + zz)
                        stage[a * 2 + rh, to : to + 6, :] = x3[w, at : at + 6, :]
                half_out[w * 2 + rh] = stage[a * 2 + rh].astype(bf16)
                half_copy(li, a, rh).start()

        @pl.when(li == 0)
        def _():
            for a in range(4):
                for rr in range(3):
                    for zz in range(2):
                        at = 12 * (zz * 6 + rr) + 6
                        to = 6 * (rr * 2 + zz)
                        stage[a, to : to + 6, :] = x3[a, at : at + 6, :]
                north_out[a] = stage[a].astype(bf16)
                north_copy(a).start()

        for a in range(4):
            for zz in range(2):
                a2, z2 = moved(a, zz)
                for r in range(3, 6):
                    at, to = 12 * (zz * 6 + r) + 6, 12 * (z2 * 6 + r - 3)
                    y3[li * 4 + a2, to : to + 6, :] = x3[li * 4 + a, at : at + 6, :]

        @pl.when(li > 0)
        def _():
            for a in range(4):
                for zz in range(2):
                    a2, z2 = moved(a, zz)
                    for r in range(3):
                        at, to = 12 * (zz * 6 + r) + 6, 12 * (z2 * 6 + r + 3)
                        y3[(li - 1) * 4 + a2, to : to + 6, :] = x3[li * 4 + a, at : at + 6, :]

    def place_half(li, block, a, rh, col):
        for rr in range(3):
            for zz in range(2):
                a2, z2 = moved(a, zz)
                to = 12 * (z2 * 6 + (rr if rh == 1 else rr + 3)) + col
                y3[li * 4 + a2, to : to + 6, :] = stage[block, 6 * (rr * 2 + zz) : 6 * (rr * 2 + zz) + 6, :]

    def receive_row_of_windows(li):
        nxt = lax.rem(li + 1, 3)
        for rh, source in ((1, li), (0, nxt)):
            for a in range(4):
                half_copy(source, a, rh).wait_recv()
                stage[a * 2 + rh] = half_in[(source * 4 + a) * 2 + rh].astype(f32)
                place_half(li, a * 2 + rh, a, rh, 6)

        @pl.when(li == 2)
        def _():
            for a in range(4):
                north_copy(a).wait_recv()
                stage[a] = north_in[a].astype(f32)
                place_half(li, a, a, 0, 0)

    def one(k, carry):
        li = lax.rem(k + 2, 3)
        block_rows(0, li, x3, ws, gains, bm, bt, qkv, att, k_tail, v_tail)
        send_row_of_windows(li)
        return carry

    lax.fori_loop(0, 3, one, 0)

    back_copy = pltpu.make_async_remote_copy(
        src_ref=back_out, dst_ref=back_in, send_sem=back_s.at[0], recv_sem=back_r.at[0],
        device_id=(down, lon), device_id_type=MESH,
    )

    def two(k, carry):
        li = lax.rem(k + 2, 3)
        receive_row_of_windows(li)
        block_rows(1, li, y3, ws, gains, bm, bt, qkv, att, k_tail, v_tail)

        @pl.when(li == 2)
        def _():
            for rr in range(3):
                for a in range(4):
                    for zz in range(2):
                        to = 12 * (rr * 8 + 2 * a + zz)
                        at = 12 * (zz * 6 + rr + 3)
                        lines[to : to + 12, :] = y3[8 + a, at : at + 12, :]
            back_out[...] = lines[...].astype(bf16)
            back_copy.start()

        for a in range(4):
            w = li * 4 + a
            split(xf, pl.ds(pl.multiple_of(w * 144, 144), 144), y3[w])

        @pl.when(li == 0)
        def _():
            back_copy.wait_recv()
            split(back, pl.ds(0, 288), back_in[...].astype(f32))
            flush(0)

        return carry

    def line(rho, lev, par):
        if rho < 0:
            return back, pl.ds(12 * ((rho + 3) * 8 + lev) + par, 8, stride=2)
        at = ((rho // 6) * 4 + lev // 2) * 144 + 12 * ((lev % 2) * 6 + rho % 6)
        return xf, pl.ds(at + par, 8, stride=2)

    def fan_copy(part, k):
        peer = lax.rem(lon + k, lons)
        return pltpu.make_async_remote_copy(
            src_ref=fan_out.at[part, peer], dst_ref=fan_in.at[part, lon],
            send_sem=fan_s.at[part, k], recv_sem=fan_r.at[part, k],
            device_id=(lat, peer), device_id_type=MESH,
        )

    def flush(part):
        ready = PARTS[part]
        base, size = 64 * 5 * part, 64 * len(ready)

        def level(z, carry):
            lev = lax.rem(z + 7, 8)
            for n, i in enumerate(ready):
                to = pl.ds(pl.multiple_of(base + (n * 8 + z) * 8, 8), 8)
                for q in range(4):
                    ref, at = line(2 * i - 3 + q % 2, lev, q // 2)
                    cells[q, to, :128] = ref[0, at, :]
                    cells[q, to, 128:] = ref[1, at, :][:, :64]
            return carry

        lax.fori_loop(0, 8, level, 0)

        def merge(g, carry):
            rows = pl.ds(pl.multiple_of(base + g * (size // 2), 16), size // 2)
            xs = [cells[q, rows, :] for q in range(4)]
            mean = sum(jnp.sum(x, axis=-1, keepdims=True) for x in xs) * (1.0 / 768)
            cs = [x - mean for x in xs]
            var = sum(jnp.sum(c * c, axis=-1, keepdims=True) for c in cs) * (1.0 / 768)
            scale = lax.rsqrt(var + epsilon)
            gain = mgain[...]
            total = None
            for q in range(4):
                piece_gain = gain[:, 192 * q : 192 * q + 192]
                part_sum = dot((cs[q] * scale * piece_gain).astype(bf16), wm[q])
                total = part_sum if total is None else total + part_sum
            merged[rows, :] = total.astype(bf16)
            return carry

        lax.fori_loop(0, 2, merge, 0)
        lane = lax.broadcasted_iota(jnp.int32, (1, 128), 1)
        blocks = [send_at[0:1, :] + (3 * (2 * m + lane // 64)).astype(f32) for m in range((len(ready) + 1) // 2)]
        where = jnp.concatenate(blocks, axis=1)[:, :size]
        pick = lax.broadcasted_iota(jnp.int32, (256, size), 0).astype(f32) == where
        fan = dot(jnp.where(pick, 1.0, 0.0).astype(bf16), merged[base : base + size, :])
        fan_out[part] = fan.astype(bf16).reshape(16, 16, 384)
        for k in range(1, 16):
            fan_copy(part, k).start()
        fan_in[part, lon] = fan_out[part, lon]

    xf[:, 1728:, :] = jnp.zeros((2, 32, 128), f32)
    back[:, 288:, :] = jnp.zeros((2, 8, 128), f32)
    lax.fori_loop(0, 3, two, 0)
    flush(1)

    for part in range(2):
        for k in range(1, 16):
            fan_copy(part, k).wait_recv()
        arrived = fan_in[part].reshape(256, 384)
        slot = lax.broadcasted_iota(jnp.int32, (48, 256), 1).astype(f32)
        picks = [
            jnp.where(slot == place_at[...][:, :1] + 3.0 * n, 1.0, 0.0).astype(bf16) for n in range(len(PARTS[part]))
        ]
        rows = dot(jnp.concatenate(picks, axis=0), arrived).astype(bf16)
        for n, i in enumerate(PARTS[part]):
            out[i] = rows[48 * n : 48 * n + 48]

    for n in range(24):
        half_copy(n // 8, (n // 2) % 4, n % 2).wait_send()
    for a in range(4):
        north_copy(a).wait_send()
    back_copy.wait_send()
    for part in range(2):
        for k in range(1, 16):
            fan_copy(part, k).wait_send()


VM = pl.BlockSpec(memory_space=pltpu.VMEM)
HB = pl.BlockSpec(memory_space=pl.ANY)
SM = pl.BlockSpec(memory_space=pltpu.SMEM)


def whole(idx, tables, gains, mgain, order, x, wq, wo, wu, wd, wm):
    v = pltpu.VMEM
    dma = pltpu.SemaphoreType.DMA
    return pl.pallas_call(
        kernel,
        out_shape=jax.ShapeDtypeStruct((9, 48, 384), bf16),
        in_specs=[SM] + [VM] * 4 + [HB] * 6,
        out_specs=VM,
        scratch_shapes=[
            v((6656, 128), f32),
            v((2, 128, 128), f32),
            v((288, 128), f32),
            v((288, 128), f32),
            v((2, 72 * PITCH, 128), f32),
            v((2, 24 * PITCH, 128), f32),
            v(x.shape, bf16),
            v((2, 1760, 128), f32),
            v((12, 144, 192), f32),
            v((12, 144, 192), f32),
            v((576, 576), bf16),
            v((576, 192), bf16),
            v((128, 192), bf16),
            v((128, 192), bf16),
            v(wq.shape, bf16),
            v(wo.shape, bf16),
            v(wu.shape, bf16),
            v(wd.shape, bf16),
            v(wm.shape, bf16),
            v((8, 48, 192), f32),
            v((24, 48, 192), bf16),
            v((24, 48, 192), bf16),
            v((4, 48, 192), bf16),
            v((4, 48, 192), bf16),
            v((288, 192), f32),
            v((288, 192), bf16),
            v((288, 192), bf16),
            v((2, 296, 128), f32),
            v((4, 576, 192), f32),
            v((576, 384), bf16),
            v((2, 16, 16, 384), bf16),
            v((2, 16, 16, 384), bf16),
            v((8, 128), f32),
            v((48, 128), f32),
            dma((6,)),
            dma((24,)),
            dma((24,)),
            dma((4,)),
            dma((4,)),
            dma((1,)),
            dma((1,)),
            dma((2, 16)),
            dma((2, 16)),
        ],
        compiler_params=pltpu.CompilerParams(vmem_limit_bytes=60 << 20, collective_id=0, has_side_effects=True),
        name="whole_pair",
    )(idx, tables, gains, mgain, order, x, wq, wo, wu, wd, wm)


def body(
    fine_field,
    qkv_weight,
    out_weight,
    up_weight,
    down_weight,
    norm_gain,
    bias_table,
    bias_index,
    merge_gain,
    merge_weight,
    column_order,
):
    result = whole(
        bias_index.reshape(-1),
        bias_table.transpose(0, 1, 3, 2, 4),
        norm_gain,
        merge_gain.reshape(1, 768),
        column_order.reshape(1, 768),
        fine_field.transpose(1, 2, 0, 3),
        qkv_weight,
        out_weight,
        up_weight,
        down_weight.transpose(0, 2, 1),
        merge_weight.reshape(4, 192, 384),
    )
    return result.transpose(1, 0, 2)


def solution(mesh):
    in_specs = (
        P(None, "lat", "lon", None),
        P(),
        P(),
        P(),
        P(),
        P(),
        P(None, "lat", None, None, None),
        P(),
        P(),
        P(),
        P(),
    )
    out_specs = P("lon", "lat", None)
    return jax.shard_map(body, mesh=mesh, in_specs=in_specs, out_specs=out_specs, check_vma=False)
```

```python
import functools
import jax
import jax.numpy as jnp
from jax import lax
from jax.experimental import pallas as pl
from jax.experimental.pallas import tpu as pltpu
from jax.sharding import PartitionSpec as P

epsilon = 1e-05
LOG2E = 1.4426950408889634
PITCH = 152
f32 = jnp.float32
bf16 = jnp.bfloat16


def lane_norm(x, gain):
    mean = jnp.mean(x, axis=-1, keepdims=True)
    cen = x - mean
    var = jnp.mean(cen * cen, axis=-1, keepdims=True)
    return (cen * lax.rsqrt(var + epsilon) * gain).astype(bf16)


def dot(a, b):
    return jnp.dot(a, b, preferred_element_type=f32)


def dot_t(a, b):
    return lax.dot_general(a, b, (((1,), (1,)), ((), ())), preferred_element_type=f32)


def gelu(v):
    u = v * (0.7978845608028654 + 0.035677408136300125 * (v * v))
    hv = 0.5 * v
    return hv + hv * jnp.tanh(u)


def qkv_rows(x, gain, wqkv):
    n = lane_norm(x, gain)
    p = dot(n, wqkv)
    q = (p[:, :192] * (LOG2E / 32**0.5)).astype(bf16)
    return jnp.concatenate([q, p[:, 192:].astype(bf16)], axis=1)


def attend(qkv, rows, bias_main, bias_tail, k_tail, v_tail):
    head = lax.broadcasted_iota(jnp.int32, (1, 192), 1) // 32
    zero = jnp.zeros((), bf16)
    group = lax.broadcasted_iota(jnp.int32, (144, 128), 1) // 16
    rest = pl.ds(rows + 128, 16)
    kt, vt = qkv[rest, 192:384], qkv[rest, 384:576]
    for h in range(6):
        k_tail[16 * h : 16 * h + 16, :] = jnp.where(head == h, kt, zero)
        v_tail[16 * h : 16 * h + 16, :] = jnp.where(head == h, vt, zero)
    q = qkv[pl.ds(rows, 144), :192]
    k = qkv[pl.ds(rows, 128), 192:384]
    v = qkv[pl.ds(rows, 128), 384:576]
    tail = dot_t(q, k_tail[...]) + bias_tail
    mains, maxes = [], []
    for h in range(6):
        s = dot_t(jnp.where(head == h, q, zero), k) + bias_main(h)
        m = jnp.max(jnp.maximum(s, jnp.where(group == h, tail, -3.0e38)), axis=-1, keepdims=True)
        mains.append(s)
        maxes.append(m)
    mt = jnp.broadcast_to(maxes[0], (144, 128))
    for h in range(1, 6):
        mt = jnp.where(group == h, maxes[h], mt)
    pt = jnp.where(group < 6, jnp.exp2(tail - mt), 0.0)
    both = dot(pt.astype(bf16), v_tail[...])
    lane = lax.broadcasted_iota(jnp.int32, (144, 128), 1) // 32
    outs = []
    for half, heads in ((0, (0, 1, 2, 3)), (1, (4, 5))):
        at = slice(0, 128) if half == 0 else slice(128, 192)
        width = at.stop - at.start
        acc = inv = None
        for h in heads:
            p = jnp.exp2(mains[h] - maxes[h])
            r = 1.0 / jnp.sum(p + jnp.where(group == h, pt, 0.0), axis=-1, keepdims=True)
            o = dot(p.astype(bf16), v[:, at])
            if acc is None:
                acc, inv = o, jnp.broadcast_to(r, (144, width))
            else:
                mine = lane[:, :width] == h - 4 * half
                acc, inv = jnp.where(mine, o, acc), jnp.where(mine, r, inv)
        outs.append((acc + both[:, at]) * inv)
    return jnp.concatenate(outs, axis=1).astype(bf16)


def ffn_rows(x, att, wout, gain, wup, wdown_t):
    hidden = (x + dot(att, wout)).astype(bf16)
    hf = hidden.astype(f32)
    n = lane_norm(hf, gain)
    act = gelu(dot(n, wup)).astype(bf16)
    return (hf + dot_t(act, wdown_t)).astype(bf16).astype(f32)


MESH = pl.DeviceIdType.MESH
LI_ROWS = 24 * PITCH


def build_table(tb_ref, t_ref, piece):
    def rows(k0, width):
        for b in range(2):
            for n in range(18):
                piece[b, 4 * n : 4 * n + 4, :width] = tb_ref[b, n // 6, n % 6, :, pl.ds(k0, width)]
            t_ref[pl.ds(2 * k0 + b, 128, stride=2), :] = (piece[b] * LOG2E).T

    def step(k, carry):
        rows(pl.multiple_of(k * 128, 128), 128)
        return carry

    piece[...] = jnp.zeros_like(piece)
    lax.fori_loop(0, 25, step, 0)
    rows(3200, 112)


def gather_rows(idx_ref, t_ref, g_ref, t):
    t3 = t_ref.reshape(3328, 2, 128)
    for s in range(144):
        i = idx_ref.at[pl.ds(s, 20736 - 143)][t * 144]
        g_ref[pl.ds(2 * s, 2), :] = t3[i]


def spread(g_ref, bm, bt, t, lane):
    for b in range(2):
        tr = g_ref[pl.ds(b, 128, stride=2), :].T
        for r in range(9):
            bm[b, pl.ds(r * 8 * PITCH + t, 8, stride=PITCH), :] = tr[r * 8 : r * 8 + 8]
        tail = g_ref[pl.ds(256 + b, 16, stride=2), :]
        tt = jnp.concatenate([tail] * 8, 0).T
        for li in range(3):
            v = [tt[(li * 3 + n) * 8 : (li * 3 + n) * 8 + 8] for n in range(3)]
            acc = jnp.where(lane < 2, v[0], jnp.where(lane < 4, v[1], v[2]))
            acc = jnp.where(lane % 2 == 0, acc, jnp.concatenate([acc[4:], acc[:4]], 0))
            bt[b, pl.ds(li * 8 * PITCH + t, 8, stride=PITCH), :] = acc


UN = 8


def expand_bias(idx_ref, tb_ref, t_ref, piece, ga, gb, bm, bt):
    build_table(tb_ref, t_ref, piece)
    lane8 = lax.broadcasted_iota(jnp.int32, (8, 128), 1) // 16
    gather_rows(idx_ref, t_ref, ga, 0)
    gs = [ga, gb]

    def step(u, carry):
        t = UN * u
        for k in range(UN):
            spread(gs[k % 2], bm, bt, t + k, lane8)
            nxt = t + k + 1
            gather_rows(idx_ref, t_ref, gs[(k + 1) % 2], jnp.minimum(nxt, 143) if k == UN - 1 else nxt)
        return carry

    lax.fori_loop(0, 144 // UN, step, 0)


def mask_bias(bm, bt, last_lat):
    tok = lax.broadcasted_iota(jnp.int32, (144, 128), 0)
    key = lax.broadcasted_iota(jnp.int32, (144, 128), 1)
    key_t = 128 + key % 16

    def level(t):
        return t // 72

    def row(t):
        return ((t // 12) % 6) // 3

    def cut(lo, hi, window, code):
        differ = code(tok) != code(key)
        differ_t = code(tok) != code(key_t)

        def step(n, carry):
            li, a = window(n)
            for h in range(6):
                at = pl.ds(pl.multiple_of((li * 24 + h * 4 + a) * PITCH, 8), 144)
                bm[1, at, :] = jnp.where(differ, -1e30, bm[1, at, :])
            at = pl.ds(pl.multiple_of((li * 8 + a) * PITCH, 8), 144)
            bt[1, at, :] = jnp.where(differ_t, -1e30, bt[1, at, :])
            return carry

        lax.fori_loop(lo, hi, step, 0)

    cut(0, 3, lambda n: (n, 3), level)

    @pl.when(last_lat)
    def _():
        cut(0, 4, lambda n: (2, n), row)


def block_rows(b, li, cur, ws, gains, bm, bt, qkv, att, k_tail, v_tail):
    wq, wo, wu, wd = ws

    def first(g, carry):
        x = cur[b, pl.ds(4 * li + 2 * g, 2)].reshape(288, 192)
        qkv[pl.ds(pl.multiple_of(g * 288, 288), 288), :] = qkv_rows(x, gains[b, 0:1, :], wq[b])
        return carry

    lax.fori_loop(0, 2, first, 0)

    def second(a, carry):
        def main(h):
            return bm[b, pl.ds(pl.multiple_of((li * 24 + h * 4 + a) * PITCH, 8), 144), :]

        start = pl.multiple_of(a * 144, 144)
        tail = bt[b, pl.ds(pl.multiple_of((li * 8 + a) * PITCH, 8), 144), :]
        att[pl.ds(start, 144), :] = attend(qkv, start, main, tail, k_tail, v_tail)
        return carry

    lax.fori_loop(0, 4, second, 0, unroll=2)

    def third(g, carry):
        x = cur[b, pl.ds(4 * li + 2 * g, 2)].reshape(288, 192)
        rows = pl.ds(pl.multiple_of(g * 288, 288), 288)
        out = ffn_rows(x, att[rows, :], wo[b], gains[b, 1:2, :], wu[b], wd[b])
        cur[b, pl.ds(4 * li + 2 * g, 2)] = out.reshape(2, 144, 192)
        return carry

    lax.fori_loop(0, 2, third, 0)


PARTS = ((0, 1, 2, 3, 8), (4, 5, 6, 7))


def less(a, b, axis):
    return jnp.sum(jnp.where(a < b, 1.0, 0.0), axis=axis, keepdims=True)


def thirds(rank):
    peer = jnp.floor((rank + 0.5) * (1.0 / 3))
    return 13.0 * peer + rank


def column_places(order_ref, lon, send_ref, place_ref):
    order = order_ref[...].astype(f32).reshape(1, 768)
    row = lax.broadcasted_iota(jnp.int32, (128, 1), 0)
    lane = lax.broadcasted_iota(jnp.int32, (128, 768), 1)
    level, col = (row % 64) // 8, row % 8
    wide = lon * 6 + col + 3
    ids = level * 96 + jnp.where(wide >= 96, wide - 96, wide)
    hit = order == ids.astype(f32)
    place = jnp.sum(jnp.where(hit, lane.astype(f32), 0.0), axis=1, keepdims=True)
    place = jnp.where(col < 6, place, 1e6)
    across = jnp.broadcast_to(place, (128, 128))
    send_ref[...] = jnp.broadcast_to(thirds(less(across[:64], across.T[:1], 0)), (8, 128))
    mine = jnp.sum(jnp.where(lane == lon * 48 + row, order, 0.0), axis=1, keepdims=True)
    east = mine - 96.0 * jnp.floor((mine + 0.5) * (1.0 / 96)) - 3.0
    east = jnp.where(east < 0.0, east + 96.0, east)
    key = jnp.floor((east + 0.5) * (1.0 / 6)) * 48.0 + row.astype(f32)
    key = jnp.where(row < 48, key, 1e6)
    across = jnp.broadcast_to(key, (128, 128))
    at = thirds(less(across.T[:1], key, 1))
    place_ref[...] = jnp.broadcast_to(at[:48], (48, 128))


def split(ref, rows, x):
    ref[0, rows, :] = x[:, :128]
    ref[1, rows, :64] = x[:, 128:]


def kernel(
    idx, tb, gains, mgain, order, x_hbm, wq_hbm, wo_hbm, wu_hbm, wd_hbm, wm_hbm,
    out,
    table, piece, ga, gb, bm, bt, xin, xf, xy, qkv, att, k_tail, v_tail, wq, wo, wu, wd, wm,
    stage, half_out, half_in, north_out, north_in, lines, back_out, back_in, back, cells, merged, fan_out, fan_in, send_at, place_at,
    load, half_s, half_r, north_s, north_r, back_s, back_r, fan_s, fan_r,
):
    lats, lons = lax.axis_size("lat"), lax.axis_size("lon")
    lat, lon = lax.axis_index("lat"), lax.axis_index("lon")
    up, down = lax.rem(lat + lats - 1, lats), lax.rem(lat + 1, lats)
    west, east = lax.rem(lon + lons - 1, lons), lax.rem(lon + 1, lons)

    barrier = pltpu.get_barrier_semaphore()
    greet = [(lat, lax.rem(lon + k, lons)) for k in range(1, 16)] + [(down, lon), (down, east), (up, lon)]
    for where in greet:
        pl.semaphore_signal(barrier, inc=1, device_id=where, device_id_type=MESH)

    pairs = [(x_hbm, xin), (wq_hbm, wq), (wo_hbm, wo), (wu_hbm, wu), (wd_hbm, wd), (wm_hbm, wm)]
    loads = [pltpu.make_async_copy(s, d, load.at[n]) for n, (s, d) in enumerate(pairs)]
    for c in loads:
        c.start()
    column_places(order, lon, send_at, place_at)
    expand_bias(idx, tb, table, piece, ga, gb, bm, bt)
    mask_bias(bm, bt, lat == lats - 1)
    for c in loads:
        c.wait()
    pl.semaphore_wait(barrier, 18)
    ws = (wq, wo, wu, wd)
    x3, y3 = xy.at[0], xy.at[1]

    split(xf, pl.ds(0, 1728), xin[...].reshape(1728, 192).astype(f32))
    def window(w, carry):
        for zz in range(2):
            for r in range(6):
                i = zz * 6 + r
                at = pl.ds((6 * (w // 4) + r) * 96 + 2 * (w % 4) + zz, 16, stride=8)
                x3[w, 12 * i : 12 * i + 12, :128] = xf[0, at, :][:12]
                x3[w, 12 * i : 12 * i + 12, 128:] = xf[1, at, :][:12, :64]
        return carry

    lax.fori_loop(0, 12, window, 0)
    stage[...] = jnp.zeros_like(stage)
    k_tail[...] = jnp.zeros_like(k_tail)
    v_tail[...] = jnp.zeros_like(v_tail)

    def half_copy(li, a, rh):
        target = jnp.where(li + rh == 0, up, lat)
        n = (li * 4 + a) * 2 + rh
        return pltpu.make_async_remote_copy(
            src_ref=half_out.at[n], dst_ref=half_in.at[n], send_sem=half_s.at[n], recv_sem=half_r.at[n],
            device_id=(target, west), device_id_type=MESH,
        )

    def north_copy(a):
        return pltpu.make_async_remote_copy(
            src_ref=north_out.at[a], dst_ref=north_in.at[a], send_sem=north_s.at[a], recv_sem=north_r.at[a],
            device_id=(up, lon), device_id_type=MESH,
        )

    def moved(a, zz):
        return (a, 0) if zz == 1 else ((a + 3) % 4, 1)

    def send_row_of_windows(li):
        for a in range(4):
            w = li * 4 + a
            for rh in range(2):
                for rr in range(3):
                    for zz in range(2):
                        at = 12 * (zz * 6 + 3 * rh + rr)
                        to = 6 * (rr * 2 + zz)
                        stage[a * 2 + rh, to : to + 6, :] = x3[w, at : at + 6, :]
                half_out[w * 2 + rh] = stage[a * 2 + rh].astype(bf16)
                half_copy(li, a, rh).start()

        @pl.when(li == 0)
        def _():
            for a in range(4):
                for rr in range(3):
                    for zz in range(2):
                        at = 12 * (zz * 6 + rr) + 6
                        to = 6 * (rr * 2 + zz)
                        stage[a, to : to + 6, :] = x3[a, at : at + 6, :]
                north_out[a] = stage[a].astype(bf16)
                north_copy(a).start()

        for a in range(4):
            for zz in range(2):
                a2, z2 = moved(a, zz)
                for r in range(3, 6):
                    at, to = 12 * (zz * 6 + r) + 6, 12 * (z2 * 6 + r - 3)
                    y3[li * 4 + a2, to : to + 6, :] = x3[li * 4 + a, at : at + 6, :]

        @pl.when(li > 0)
        def _():
            for a in range(4):
                for zz in range(2):
                    a2, z2 = moved(a, zz)
                    for r in range(3):
                        at, to = 12 * (zz * 6 + r) + 6, 12 * (z2 * 6 + r + 3)
                        y3[(li - 1) * 4 + a2, to : to + 6, :] = x3[li * 4 + a, at : at + 6, :]

    def place_half(li, block, a, rh, col):
        for rr in range(3):
            for zz in range(2):
                a2, z2 = moved(a, zz)
                to = 12 * (z2 * 6 + (rr if rh == 1 else rr + 3)) + col
                y3[li * 4 + a2, to : to + 6, :] = stage[block, 6 * (rr * 2 + zz) : 6 * (rr * 2 + zz) + 6, :]

    def receive_row_of_windows(li):
        nxt = lax.rem(li + 1, 3)
        for rh, source in ((1, li), (0, nxt)):
            for a in range(4):
                half_copy(source, a, rh).wait_recv()
                stage[a * 2 + rh] = half_in[(source * 4 + a) * 2 + rh].astype(f32)
                place_half(li, a * 2 + rh, a, rh, 6)

        @pl.when(li == 2)
        def _():
            for a in range(4):
                north_copy(a).wait_recv()
                stage[a] = north_in[a].astype(f32)
                place_half(li, a, a, 0, 0)

    back_copy = pltpu.make_async_remote_copy(
        src_ref=back_out, dst_ref=back_in, send_sem=back_s.at[0], recv_sem=back_r.at[0],
        device_id=(down, lon), device_id_type=MESH,
    )

    def step(k, carry):
        li = lax.rem(k + 2, 3)
        b = k // 3

        @pl.when(b == 1)
        def _():
            receive_row_of_windows(li)

        block_rows(b, li, xy, ws, gains, bm, bt, qkv, att, k_tail, v_tail)

        @pl.when(b == 0)
        def _():
            send_row_of_windows(li)

        @pl.when(b == 1)
        def _():
            finish(li)

        return carry

    def finish(li):
        @pl.when(li == 2)
        def _():
            for rr in range(3):
                for a in range(4):
                    for zz in range(2):
                        to = 12 * (rr * 8 + 2 * a + zz)
                        at = 12 * (zz * 6 + rr + 3)
                        lines[to : to + 12, :] = y3[8 + a, at : at + 12, :]
            back_out[...] = lines[...].astype(bf16)
            back_copy.start()

        for a in range(4):
            w = li * 4 + a
            split(xf, pl.ds(pl.multiple_of(w * 144, 144), 144), y3[w])

        @pl.when(li == 0)
        def _():
            back_copy.wait_recv()
            split(back, pl.ds(0, 288), back_in[...].astype(f32))
            flush(0)

    def line(rho, lev, par):
        if rho < 0:
            return back, pl.ds(12 * ((rho + 3) * 8 + lev) + par, 8, stride=2)
        at = ((rho // 6) * 4 + lev // 2) * 144 + 12 * ((lev % 2) * 6 + rho % 6)
        return xf, pl.ds(at + par, 8, stride=2)

    def fan_copy(part, k):
        peer = lax.rem(lon + k, lons)
        return pltpu.make_async_remote_copy(
            src_ref=fan_out.at[part, peer], dst_ref=fan_in.at[part, lon],
            send_sem=fan_s.at[part, k], recv_sem=fan_r.at[part, k],
            device_id=(lat, peer), device_id_type=MESH,
        )

    def flush(part):
        ready = PARTS[part]
        base, size = 64 * 5 * part, 64 * len(ready)

        def level(z, carry):
            lev = lax.rem(z + 7, 8)
            for n, i in enumerate(ready):
                to = pl.ds(pl.multiple_of(base + (n * 8 + z) * 8, 8), 8)
                for q in range(4):
                    ref, at = line(2 * i - 3 + q % 2, lev, q // 2)
                    cells[q, to, :128] = ref[0, at, :]
                    cells[q, to, 128:] = ref[1, at, :][:, :64]
            return carry

        lax.fori_loop(0, 8, level, 0)

        def merge(g, carry):
            rows = pl.ds(pl.multiple_of(base + g * (size // 2), 16), size // 2)
            xs = [cells[q, rows, :] for q in range(4)]
            mean = sum(jnp.sum(x, axis=-1, keepdims=True) for x in xs) * (1.0 / 768)
            cs = [x - mean for x in xs]
            var = sum(jnp.sum(c * c, axis=-1, keepdims=True) for c in cs) * (1.0 / 768)
            scale = lax.rsqrt(var + epsilon)
            gain = mgain[...].reshape(1, 768)
            total = None
            for q in range(4):
                piece_gain = gain[:, 192 * q : 192 * q + 192]
                part_sum = dot((cs[q] * scale * piece_gain).astype(bf16), wm[q])
                total = part_sum if total is None else total + part_sum
            merged[rows, :] = total.astype(bf16)
            return carry

        lax.fori_loop(0, 2, merge, 0)
        lane = lax.broadcasted_iota(jnp.int32, (1, 128), 1)
        blocks = [send_at[0:1, :] + (3 * (2 * m + lane // 64)).astype(f32) for m in range((len(ready) + 1) // 2)]
        where = jnp.concatenate(blocks, axis=1)[:, :size]
        pick = lax.broadcasted_iota(jnp.int32, (256, size), 0).astype(f32) == where
        fan = dot(jnp.where(pick, 1.0, 0.0).astype(bf16), merged[base : base + size, :])
        fan_out[part] = fan.astype(bf16).reshape(16, 16, 384)
        for k in range(1, 16):
            fan_copy(part, k).start()
        fan_in[part, lon] = fan_out[part, lon]

    xf[:, 1728:, :] = jnp.zeros((2, 32, 128), f32)
    back[:, 288:, :] = jnp.zeros((2, 8, 128), f32)
    lax.fori_loop(0, 6, step, 0)
    flush(1)

    for part in range(2):
        for k in range(1, 16):
            fan_copy(part, k).wait_recv()
        arrived = fan_in[part].reshape(256, 384)
        slot = lax.broadcasted_iota(jnp.int32, (48, 256), 1).astype(f32)
        picks = [
            jnp.where(slot == place_at[...][:, :1] + 3.0 * n, 1.0, 0.0).astype(bf16) for n in range(len(PARTS[part]))
        ]
        rows = dot(jnp.concatenate(picks, axis=0), arrived).astype(bf16)
        for n, i in enumerate(PARTS[part]):
            out[i] = rows[48 * n : 48 * n + 48]

    for n in range(24):
        half_copy(n // 8, (n // 2) % 4, n % 2).wait_send()
    for a in range(4):
        north_copy(a).wait_send()
    back_copy.wait_send()
    for part in range(2):
        for k in range(1, 16):
            fan_copy(part, k).wait_send()


VM = pl.BlockSpec(memory_space=pltpu.VMEM)
HB = pl.BlockSpec(memory_space=pl.ANY)
SM = pl.BlockSpec(memory_space=pltpu.SMEM)


def whole(idx, tables, gains, mgain, order, x, wq, wo, wu, wd, wm):
    v = pltpu.VMEM
    dma = pltpu.SemaphoreType.DMA
    return pl.pallas_call(
        kernel,
        out_shape=jax.ShapeDtypeStruct((9, 48, 384), bf16),
        in_specs=[SM] + [VM] * 4 + [HB] * 6,
        out_specs=VM,
        scratch_shapes=[
            v((6656, 128), f32),
            v((2, 128, 128), f32),
            v((288, 128), f32),
            v((288, 128), f32),
            v((2, 72 * PITCH, 128), f32),
            v((2, 24 * PITCH, 128), f32),
            v(x.shape, bf16),
            v((2, 1760, 128), f32),
            v((2, 12, 144, 192), f32),
            v((576, 576), bf16),
            v((576, 192), bf16),
            v((128, 192), bf16),
            v((128, 192), bf16),
            v(wq.shape, bf16),
            v(wo.shape, bf16),
            v(wu.shape, bf16),
            v(wd.shape, bf16),
            v(wm.shape, bf16),
            v((8, 48, 192), f32),
            v((24, 48, 192), bf16),
            v((24, 48, 192), bf16),
            v((4, 48, 192), bf16),
            v((4, 48, 192), bf16),
            v((288, 192), f32),
            v((288, 192), bf16),
            v((288, 192), bf16),
            v((2, 296, 128), f32),
            v((4, 576, 192), f32),
            v((576, 384), bf16),
            v((2, 16, 16, 384), bf16),
            v((2, 16, 16, 384), bf16),
            v((8, 128), f32),
            v((48, 128), f32),
            dma((6,)),
            dma((24,)),
            dma((24,)),
            dma((4,)),
            dma((4,)),
            dma((1,)),
            dma((1,)),
            dma((2, 16)),
            dma((2, 16)),
        ],
        compiler_params=pltpu.CompilerParams(vmem_limit_bytes=60 << 20, collective_id=0, has_side_effects=True),
        name="whole_pair",
    )(idx, tables, gains, mgain, order, x, wq, wo, wu, wd, wm)


def body(
    fine_field,
    qkv_weight,
    out_weight,
    up_weight,
    down_weight,
    norm_gain,
    bias_table,
    bias_index,
    merge_gain,
    merge_weight,
    column_order,
):
    result = whole(
        bias_index.reshape(-1),
        bias_table.transpose(0, 1, 3, 2, 4),
        norm_gain,
        merge_gain,
        column_order,
        fine_field.transpose(1, 2, 0, 3),
        qkv_weight,
        out_weight,
        up_weight,
        down_weight.transpose(0, 2, 1),
        merge_weight.reshape(4, 192, 384),
    )
    return result.transpose(1, 0, 2)


def solution(mesh):
    in_specs = (
        P(None, "lat", "lon", None),
        P(),
        P(),
        P(),
        P(),
        P(),
        P(None, "lat", None, None, None),
        P(),
        P(),
        P(),
        P(),
    )
    out_specs = P("lon", "lat", None)
    return jax.shard_map(body, mesh=mesh, in_specs=in_specs, out_specs=out_specs, check_vma=False)
```

```python
import functools
import jax
import jax.numpy as jnp
from jax import lax
from jax.experimental import pallas as pl
from jax.experimental.pallas import tpu as pltpu
from jax.sharding import PartitionSpec as P

epsilon = 1e-05
LOG2E = 1.4426950408889634
PITCH = 152
f32 = jnp.float32
bf16 = jnp.bfloat16


def lane_norm(x, gain):
    mean = jnp.mean(x, axis=-1, keepdims=True)
    cen = x - mean
    var = jnp.mean(cen * cen, axis=-1, keepdims=True)
    return (cen * lax.rsqrt(var + epsilon) * gain).astype(bf16)


def dot(a, b):
    return jnp.dot(a, b, preferred_element_type=f32)


def dot_t(a, b):
    return lax.dot_general(a, b, (((1,), (1,)), ((), ())), preferred_element_type=f32)


def gelu(v):
    u = v * (0.7978845608028654 + 0.035677408136300125 * (v * v))
    hv = 0.5 * v
    return hv + hv * jnp.tanh(u)


def qkv_rows(x, gain, wqkv):
    n = lane_norm(x, gain)
    p = dot(n, wqkv)
    q = (p[:, :192] * (LOG2E / 32**0.5)).astype(bf16)
    return jnp.concatenate([q, p[:, 192:].astype(bf16)], axis=1)


def attend(qkv, rows, bias_main, bias_tail, k_tail, v_tail):
    head = lax.broadcasted_iota(jnp.int32, (1, 192), 1) // 32
    zero = jnp.zeros((), bf16)
    group = lax.broadcasted_iota(jnp.int32, (144, 128), 1) // 16
    rest = pl.ds(rows + 128, 16)
    kt, vt = qkv[rest, 192:384], qkv[rest, 384:576]
    for h in range(6):
        k_tail[16 * h : 16 * h + 16, :] = jnp.where(head == h, kt, zero)
        v_tail[16 * h : 16 * h + 16, :] = jnp.where(head == h, vt, zero)
    q = qkv[pl.ds(rows, 144), :192]
    k = qkv[pl.ds(rows, 128), 192:384]
    v = qkv[pl.ds(rows, 128), 384:576]
    tail = dot_t(q, k_tail[...]) + bias_tail
    mains, maxes = [], []
    for h in range(6):
        s = dot_t(jnp.where(head == h, q, zero), k) + bias_main(h)
        m = jnp.max(jnp.maximum(s, jnp.where(group == h, tail, -3.0e38)), axis=-1, keepdims=True)
        mains.append(s)
        maxes.append(m)
    mt = jnp.broadcast_to(maxes[0], (144, 128))
    for h in range(1, 6):
        mt = jnp.where(group == h, maxes[h], mt)
    pt = jnp.where(group < 6, jnp.exp2(tail - mt), 0.0)
    both = dot(pt.astype(bf16), v_tail[...])
    lane = lax.broadcasted_iota(jnp.int32, (144, 128), 1) // 32
    outs = []
    for half, heads in ((0, (0, 1, 2, 3)), (1, (4, 5))):
        at = slice(0, 128) if half == 0 else slice(128, 192)
        width = at.stop - at.start
        acc = total = None
        for h in heads:
            p = jnp.exp2(mains[h] - maxes[h])
            d = jnp.sum(p + jnp.where(group == h, pt, 0.0), axis=-1, keepdims=True)
            o = dot(p.astype(bf16), v[:, at])
            if acc is None:
                acc, total = o, jnp.broadcast_to(d, (144, width))
            else:
                mine = lane[:, :width] == h - 4 * half
                acc, total = jnp.where(mine, o, acc), jnp.where(mine, d, total)
        outs.append((acc + both[:, at]) * (1.0 / total))
    return jnp.concatenate(outs, axis=1).astype(bf16)


def ffn_rows(x, att, wout, gain, wup, wdown_t):
    hidden = (x + dot(att, wout)).astype(bf16)
    hf = hidden.astype(f32)
    n = lane_norm(hf, gain)
    act = gelu(dot(n, wup)).astype(bf16)
    return (hf + dot_t(act, wdown_t)).astype(bf16).astype(f32)


MESH = pl.DeviceIdType.MESH
LI_ROWS = 24 * PITCH


BIAS_LOW = -4.0
BIAS_STEP = 306.0 / 65535.0


def unpacked(word):
    parts = (lax.shift_right_logical(word, 16), word & 65535)
    return [p.astype(f32) * (BIAS_STEP * LOG2E) for p in parts]


def build_table(tb_ref, t_ref, piece):
    def rows(k0, width):
        for b in range(2):
            for n in range(18):
                piece[b, 4 * n : 4 * n + 4, :width] = tb_ref[b, n // 6, n % 6, :, pl.ds(k0, width)]
        fixed = [jnp.floor((piece[b] - BIAS_LOW) * (1.0 / BIAS_STEP) + 0.5).astype(jnp.int32) for b in range(2)]
        t_ref[pl.ds(k0, 128), :] = ((fixed[0] << 16) | fixed[1]).T

    def step(k, carry):
        rows(pl.multiple_of(k * 128, 128), 128)
        return carry

    piece[...] = jnp.zeros_like(piece)
    lax.fori_loop(0, 25, step, 0)
    rows(3200, 112)


def gather_rows(idx_ref, t_ref, g_ref, t):
    t3 = t_ref.reshape(3328, 1, 128)
    for s in range(144):
        i = idx_ref.at[pl.ds(s, 20736 - 143)][t * 144]
        g_ref[pl.ds(s, 1), :] = t3[i]


def spread(g_ref, bm, bt, t, lane):
    tr = g_ref[:128, :].T
    for r in range(9):
        for b, x in enumerate(unpacked(tr[r * 8 : r * 8 + 8])):
            bm[b, pl.ds(r * 8 * PITCH + t, 8, stride=PITCH), :] = x
    tt = jnp.concatenate([g_ref[128:144, :]] * 8, 0).T
    for li in range(3):
        v = [tt[(li * 3 + n) * 8 : (li * 3 + n) * 8 + 8] for n in range(3)]
        acc = jnp.where(lane < 2, v[0], jnp.where(lane < 4, v[1], v[2]))
        acc = jnp.where(lane % 2 == 0, acc, jnp.concatenate([acc[4:], acc[:4]], 0))
        for b, x in enumerate(unpacked(acc)):
            bt[b, pl.ds(li * 8 * PITCH + t, 8, stride=PITCH), :] = x


UN = 8


def expand_bias(idx_ref, tb_ref, t_ref, piece, ga, gb, bm, bt):
    build_table(tb_ref, t_ref, piece)
    lane8 = lax.broadcasted_iota(jnp.int32, (8, 128), 1) // 16
    gather_rows(idx_ref, t_ref, ga, 0)
    gs = [ga, gb]

    def step(u, carry):
        t = UN * u
        for k in range(UN):
            spread(gs[k % 2], bm, bt, t + k, lane8)
            nxt = t + k + 1
            gather_rows(idx_ref, t_ref, gs[(k + 1) % 2], jnp.minimum(nxt, 143) if k == UN - 1 else nxt)
        return carry

    lax.fori_loop(0, 144 // UN, step, 0)


def mask_bias(bm, bt, last_lat):
    tok = lax.broadcasted_iota(jnp.int32, (144, 128), 0)
    key = lax.broadcasted_iota(jnp.int32, (144, 128), 1)
    key_t = 128 + key % 16

    def level(t):
        return t // 72

    def row(t):
        return ((t // 12) % 6) // 3

    def cut(lo, hi, window, code):
        differ = code(tok) != code(key)
        differ_t = code(tok) != code(key_t)

        def step(n, carry):
            li, a = window(n)
            for h in range(6):
                at = pl.ds(pl.multiple_of((li * 24 + h * 4 + a) * PITCH, 8), 144)
                bm[1, at, :] = jnp.where(differ, -1e30, bm[1, at, :])
            at = pl.ds(pl.multiple_of((li * 8 + a) * PITCH, 8), 144)
            bt[1, at, :] = jnp.where(differ_t, -1e30, bt[1, at, :])
            return carry

        lax.fori_loop(lo, hi, step, 0)

    cut(0, 3, lambda n: (n, 3), level)

    @pl.when(last_lat)
    def _():
        cut(0, 4, lambda n: (2, n), row)


def block_rows(b, li, cur, ws, gains, bm, bt, qkv, att, k_tail, v_tail):
    wq, wo, wu, wd = ws

    def first(g, carry):
        x = cur[b, pl.ds(4 * li + 2 * g, 2)].reshape(288, 192)
        qkv[pl.ds(pl.multiple_of(g * 288, 288), 288), :] = qkv_rows(x, gains[b, 0:1, :], wq[b])
        return carry

    lax.fori_loop(0, 2, first, 0)

    def second(a, carry):
        def main(h):
            return bm[b, pl.ds(pl.multiple_of((li * 24 + h * 4 + a) * PITCH, 8), 144), :]

        start = pl.multiple_of(a * 144, 144)
        tail = bt[b, pl.ds(pl.multiple_of((li * 8 + a) * PITCH, 8), 144), :]
        att[pl.ds(start, 144), :] = attend(qkv, start, main, tail, k_tail, v_tail)
        return carry

    lax.fori_loop(0, 4, second, 0, unroll=2)

    def third(g, carry):
        x = cur[b, pl.ds(4 * li + 2 * g, 2)].reshape(288, 192)
        rows = pl.ds(pl.multiple_of(g * 288, 288), 288)
        out = ffn_rows(x, att[rows, :], wo[b], gains[b, 1:2, :], wu[b], wd[b])
        cur[b, pl.ds(4 * li + 2 * g, 2)] = out.reshape(2, 144, 192)
        return carry

    lax.fori_loop(0, 2, third, 0)


PARTS = ((0, 1, 2, 3, 8), (4, 5, 6, 7))


def less(a, b, axis):
    return jnp.sum(jnp.where(a < b, 1.0, 0.0), axis=axis, keepdims=True)


def thirds(rank):
    peer = jnp.floor((rank + 0.5) * (1.0 / 3))
    return 13.0 * peer + rank


def column_places(order_ref, lon, send_ref, place_ref):
    order = order_ref[...].astype(f32).reshape(1, 768)
    row = lax.broadcasted_iota(jnp.int32, (128, 1), 0)
    lane = lax.broadcasted_iota(jnp.int32, (128, 768), 1)
    level, col = (row % 64) // 8, row % 8
    wide = lon * 6 + col + 3
    ids = level * 96 + jnp.where(wide >= 96, wide - 96, wide)
    hit = order == ids.astype(f32)
    place = jnp.sum(jnp.where(hit, lane.astype(f32), 0.0), axis=1, keepdims=True)
    place = jnp.where(col < 6, place, 1e6)
    across = jnp.broadcast_to(place, (128, 128))
    send_ref[...] = jnp.broadcast_to(thirds(less(across[:64], across.T[:1], 0)), (8, 128))
    mine = jnp.sum(jnp.where(lane == lon * 48 + row, order, 0.0), axis=1, keepdims=True)
    east = mine - 96.0 * jnp.floor((mine + 0.5) * (1.0 / 96)) - 3.0
    east = jnp.where(east < 0.0, east + 96.0, east)
    key = jnp.floor((east + 0.5) * (1.0 / 6)) * 48.0 + row.astype(f32)
    key = jnp.where(row < 48, key, 1e6)
    across = jnp.broadcast_to(key, (128, 128))
    at = thirds(less(across.T[:1], key, 1))
    place_ref[...] = jnp.broadcast_to(at[:48], (48, 128))


def split(ref, rows, x):
    ref[0, rows, :] = x[:, :128]
    ref[1, rows, :64] = x[:, 128:]


def kernel(
    idx, tb, gains, mgain, order, x_hbm, wq_hbm, wo_hbm, wu_hbm, wd_hbm, wm_hbm,
    out,
    table, piece, ga, gb, bm, bt, xin, xf, xy, qkv, att, k_tail, v_tail, wq, wo, wu, wd, wm,
    stage, half_out, half_in, north_out, north_in, lines, back_out, back_in, back, cells, merged, fan_out, fan_in, send_at, place_at,
    load, half_s, half_r, north_s, north_r, back_s, back_r, fan_s, fan_r,
):
    lats, lons = lax.axis_size("lat"), lax.axis_size("lon")
    lat, lon = lax.axis_index("lat"), lax.axis_index("lon")
    up, down = lax.rem(lat + lats - 1, lats), lax.rem(lat + 1, lats)
    west, east = lax.rem(lon + lons - 1, lons), lax.rem(lon + 1, lons)

    barrier = pltpu.get_barrier_semaphore()
    greet = [(lat, lax.rem(lon + k, lons)) for k in range(1, 16)] + [(down, lon), (down, east), (up, lon)]
    for where in greet:
        pl.semaphore_signal(barrier, inc=1, device_id=where, device_id_type=MESH)

    pairs = [(x_hbm, xin), (wq_hbm, wq), (wo_hbm, wo), (wu_hbm, wu), (wd_hbm, wd), (wm_hbm, wm)]
    loads = [pltpu.make_async_copy(s, d, load.at[n]) for n, (s, d) in enumerate(pairs)]
    for c in loads:
        c.start()
    column_places(order, lon, send_at, place_at)
    expand_bias(idx, tb, table, piece, ga, gb, bm, bt)
    mask_bias(bm, bt, lat == lats - 1)
    for c in loads:
        c.wait()
    pl.semaphore_wait(barrier, 18)
    ws = (wq, wo, wu, wd)
    x3, y3 = xy.at[0], xy.at[1]

    split(xf, pl.ds(0, 1728), xin[...].reshape(1728, 192).astype(f32))
    def window(w, carry):
        for zz in range(2):
            for r in range(6):
                i = zz * 6 + r
                at = pl.ds((6 * (w // 4) + r) * 96 + 2 * (w % 4) + zz, 16, stride=8)
                x3[w, 12 * i : 12 * i + 12, :128] = xf[0, at, :][:12]
                x3[w, 12 * i : 12 * i + 12, 128:] = xf[1, at, :][:12, :64]
        return carry

    lax.fori_loop(0, 12, window, 0)
    stage[...] = jnp.zeros_like(stage)
    k_tail[...] = jnp.zeros_like(k_tail)
    v_tail[...] = jnp.zeros_like(v_tail)

    def half_copy(li, a, rh):
        target = jnp.where(li + rh == 0, up, lat)
        n = (li * 4 + a) * 2 + rh
        return pltpu.make_async_remote_copy(
            src_ref=half_out.at[n], dst_ref=half_in.at[n], send_sem=half_s.at[n], recv_sem=half_r.at[n],
            device_id=(target, west), device_id_type=MESH,
        )

    def north_copy(a):
        return pltpu.make_async_remote_copy(
            src_ref=north_out.at[a], dst_ref=north_in.at[a], send_sem=north_s.at[a], recv_sem=north_r.at[a],
            device_id=(up, lon), device_id_type=MESH,
        )

    def moved(a, zz):
        return (a, 0) if zz == 1 else ((a + 3) % 4, 1)

    def send_row_of_windows(li):
        for a in range(4):
            w = li * 4 + a
            for rh in range(2):
                for rr in range(3):
                    for zz in range(2):
                        at = 12 * (zz * 6 + 3 * rh + rr)
                        to = 6 * (rr * 2 + zz)
                        stage[a * 2 + rh, to : to + 6, :] = x3[w, at : at + 6, :]
                half_out[w * 2 + rh] = stage[a * 2 + rh].astype(bf16)
                half_copy(li, a, rh).start()

        @pl.when(li == 0)
        def _():
            for a in range(4):
                for rr in range(3):
                    for zz in range(2):
                        at = 12 * (zz * 6 + rr) + 6
                        to = 6 * (rr * 2 + zz)
                        stage[a, to : to + 6, :] = x3[a, at : at + 6, :]
                north_out[a] = stage[a].astype(bf16)
                north_copy(a).start()

        for a in range(4):
            for zz in range(2):
                a2, z2 = moved(a, zz)
                for r in range(3, 6):
                    at, to = 12 * (zz * 6 + r) + 6, 12 * (z2 * 6 + r - 3)
                    y3[li * 4 + a2, to : to + 6, :] = x3[li * 4 + a, at : at + 6, :]

        @pl.when(li > 0)
        def _():
            for a in range(4):
                for zz in range(2):
                    a2, z2 = moved(a, zz)
                    for r in range(3):
                        at, to = 12 * (zz * 6 + r) + 6, 12 * (z2 * 6 + r + 3)
                        y3[(li - 1) * 4 + a2, to : to + 6, :] = x3[li * 4 + a, at : at + 6, :]

    def place_half(li, block, a, rh, col):
        for rr in range(3):
            for zz in range(2):
                a2, z2 = moved(a, zz)
                to = 12 * (z2 * 6 + (rr if rh == 1 else rr + 3)) + col
                y3[li * 4 + a2, to : to + 6, :] = stage[block, 6 * (rr * 2 + zz) : 6 * (rr * 2 + zz) + 6, :]

    def receive_row_of_windows(li):
        nxt = lax.rem(li + 1, 3)
        for rh, source in ((1, li), (0, nxt)):
            for a in range(4):
                half_copy(source, a, rh).wait_recv()
                stage[a * 2 + rh] = half_in[(source * 4 + a) * 2 + rh].astype(f32)
                place_half(li, a * 2 + rh, a, rh, 6)

        @pl.when(li == 2)
        def _():
            for a in range(4):
                north_copy(a).wait_recv()
                stage[a] = north_in[a].astype(f32)
                place_half(li, a, a, 0, 0)

    back_copy = pltpu.make_async_remote_copy(
        src_ref=back_out, dst_ref=back_in, send_sem=back_s.at[0], recv_sem=back_r.at[0],
        device_id=(down, lon), device_id_type=MESH,
    )

    def step(k, carry):
        li = lax.rem(k + 2, 3)
        b = k // 3

        @pl.when(b == 1)
        def _():
            receive_row_of_windows(li)

        block_rows(b, li, xy, ws, gains, bm, bt, qkv, att, k_tail, v_tail)

        @pl.when(b == 0)
        def _():
            send_row_of_windows(li)

        @pl.when(b == 1)
        def _():
            finish(li)

        return carry

    def finish(li):
        @pl.when(li == 2)
        def _():
            for rr in range(3):
                for a in range(4):
                    for zz in range(2):
                        to = 12 * (rr * 8 + 2 * a + zz)
                        at = 12 * (zz * 6 + rr + 3)
                        lines[to : to + 12, :] = y3[8 + a, at : at + 12, :]
            back_out[...] = lines[...].astype(bf16)
            back_copy.start()

        for a in range(4):
            w = li * 4 + a
            split(xf, pl.ds(pl.multiple_of(w * 144, 144), 144), y3[w])

        @pl.when(li == 0)
        def _():
            back_copy.wait_recv()
            split(back, pl.ds(0, 288), back_in[...].astype(f32))
            flush(0)

    def line(rho, lev, par):
        if rho < 0:
            return back, pl.ds(12 * ((rho + 3) * 8 + lev) + par, 8, stride=2)
        at = ((rho // 6) * 4 + lev // 2) * 144 + 12 * ((lev % 2) * 6 + rho % 6)
        return xf, pl.ds(at + par, 8, stride=2)

    def fan_copy(part, k):
        peer = lax.rem(lon + k, lons)
        return pltpu.make_async_remote_copy(
            src_ref=fan_out.at[part, peer], dst_ref=fan_in.at[part, lon],
            send_sem=fan_s.at[part, k], recv_sem=fan_r.at[part, k],
            device_id=(lat, peer), device_id_type=MESH,
        )

    def flush(part):
        ready = PARTS[part]
        base, size = 64 * 5 * part, 64 * len(ready)

        def level(z, carry):
            lev = lax.rem(z + 7, 8)
            for n, i in enumerate(ready):
                to = pl.ds(pl.multiple_of(base + (n * 8 + z) * 8, 8), 8)
                for q in range(4):
                    ref, at = line(2 * i - 3 + q % 2, lev, q // 2)
                    cells[q, to, :128] = ref[0, at, :]
                    cells[q, to, 128:] = ref[1, at, :][:, :64]
            return carry

        lax.fori_loop(0, 8, level, 0)

        def merge(g, carry):
            rows = pl.ds(pl.multiple_of(base + g * (size // 2), 16), size // 2)
            xs = [cells[q, rows, :] for q in range(4)]
            mean = sum(jnp.sum(x, axis=-1, keepdims=True) for x in xs) * (1.0 / 768)
            cs = [x - mean for x in xs]
            var = sum(jnp.sum(c * c, axis=-1, keepdims=True) for c in cs) * (1.0 / 768)
            scale = lax.rsqrt(var + epsilon)
            gain = mgain[...].reshape(1, 768)
            total = None
            for q in range(4):
                piece_gain = gain[:, 192 * q : 192 * q + 192]
                part_sum = dot((cs[q] * scale * piece_gain).astype(bf16), wm[q])
                total = part_sum if total is None else total + part_sum
            merged[rows, :] = total.astype(bf16)
            return carry

        lax.fori_loop(0, 2, merge, 0)
        lane = lax.broadcasted_iota(jnp.int32, (1, 128), 1)
        blocks = [send_at[0:1, :] + (3 * (2 * m + lane // 64)).astype(f32) for m in range((len(ready) + 1) // 2)]
        where = jnp.concatenate(blocks, axis=1)[:, :size]
        pick = lax.broadcasted_iota(jnp.int32, (256, size), 0).astype(f32) == where
        fan = dot(jnp.where(pick, 1.0, 0.0).astype(bf16), merged[base : base + size, :])
        fan_out[part] = fan.astype(bf16).reshape(16, 16, 384)
        for k in range(1, 16):
            fan_copy(part, k).start()
        fan_in[part, lon] = fan_out[part, lon]

    xf[:, 1728:, :] = jnp.zeros((2, 32, 128), f32)
    back[:, 288:, :] = jnp.zeros((2, 8, 128), f32)
    lax.fori_loop(0, 6, step, 0)
    flush(1)

    for part in range(2):
        for k in range(1, 16):
            fan_copy(part, k).wait_recv()
        arrived = fan_in[part].reshape(256, 384)
        slot = lax.broadcasted_iota(jnp.int32, (48, 256), 1).astype(f32)
        picks = [
            jnp.where(slot == place_at[...][:, :1] + 3.0 * n, 1.0, 0.0).astype(bf16) for n in range(len(PARTS[part]))
        ]
        rows = dot(jnp.concatenate(picks, axis=0), arrived).astype(bf16)
        for n, i in enumerate(PARTS[part]):
            out[i] = rows[48 * n : 48 * n + 48]

    for n in range(24):
        half_copy(n // 8, (n // 2) % 4, n % 2).wait_send()
    for a in range(4):
        north_copy(a).wait_send()
    back_copy.wait_send()
    for part in range(2):
        for k in range(1, 16):
            fan_copy(part, k).wait_send()


VM = pl.BlockSpec(memory_space=pltpu.VMEM)
HB = pl.BlockSpec(memory_space=pl.ANY)
SM = pl.BlockSpec(memory_space=pltpu.SMEM)


def whole(idx, tables, gains, mgain, order, x, wq, wo, wu, wd, wm):
    v = pltpu.VMEM
    dma = pltpu.SemaphoreType.DMA
    return pl.pallas_call(
        kernel,
        out_shape=jax.ShapeDtypeStruct((9, 48, 384), bf16),
        in_specs=[SM] + [VM] * 4 + [HB] * 6,
        out_specs=VM,
        scratch_shapes=[
            v((3328, 128), jnp.int32),
            v((2, 128, 128), f32),
            v((144, 128), jnp.int32),
            v((144, 128), jnp.int32),
            v((2, 72 * PITCH, 128), f32),
            v((2, 24 * PITCH, 128), f32),
            v(x.shape, bf16),
            v((2, 1760, 128), f32),
            v((2, 12, 144, 192), f32),
            v((576, 576), bf16),
            v((576, 192), bf16),
            v((128, 192), bf16),
            v((128, 192), bf16),
            v(wq.shape, bf16),
            v(wo.shape, bf16),
            v(wu.shape, bf16),
            v(wd.shape, bf16),
            v(wm.shape, bf16),
            v((8, 48, 192), f32),
            v((24, 48, 192), bf16),
            v((24, 48, 192), bf16),
            v((4, 48, 192), bf16),
            v((4, 48, 192), bf16),
            v((288, 192), f32),
            v((288, 192), bf16),
            v((288, 192), bf16),
            v((2, 296, 128), f32),
            v((4, 576, 192), f32),
            v((576, 384), bf16),
            v((2, 16, 16, 384), bf16),
            v((2, 16, 16, 384), bf16),
            v((8, 128), f32),
            v((48, 128), f32),
            dma((6,)),
            dma((24,)),
            dma((24,)),
            dma((4,)),
            dma((4,)),
            dma((1,)),
            dma((1,)),
            dma((2, 16)),
            dma((2, 16)),
        ],
        compiler_params=pltpu.CompilerParams(vmem_limit_bytes=60 << 20, collective_id=0, has_side_effects=True),
        name="whole_pair",
    )(idx, tables, gains, mgain, order, x, wq, wo, wu, wd, wm)


def body(
    fine_field,
    qkv_weight,
    out_weight,
    up_weight,
    down_weight,
    norm_gain,
    bias_table,
    bias_index,
    merge_gain,
    merge_weight,
    column_order,
):
    result = whole(
        bias_index.reshape(-1),
        bias_table.transpose(0, 1, 3, 2, 4),
        norm_gain,
        merge_gain,
        column_order,
        fine_field.transpose(1, 2, 0, 3),
        qkv_weight,
        out_weight,
        up_weight,
        down_weight.transpose(0, 2, 1),
        merge_weight.reshape(4, 192, 384),
    )
    return result.transpose(1, 0, 2)


def solution(mesh):
    in_specs = (
        P(None, "lat", "lon", None),
        P(),
        P(),
        P(),
        P(),
        P(),
        P(None, "lat", None, None, None),
        P(),
        P(),
        P(),
        P(),
    )
    out_specs = P("lon", "lat", None)
    return jax.shard_map(body, mesh=mesh, in_specs=in_specs, out_specs=out_specs, check_vma=False)
```

```python
import functools
import jax
import jax.numpy as jnp
from jax import lax
from jax.experimental import pallas as pl
from jax.experimental.pallas import tpu as pltpu
from jax.sharding import PartitionSpec as P

epsilon = 1e-05
LOG2E = 1.4426950408889634
PITCH = 152
f32 = jnp.float32
bf16 = jnp.bfloat16


def lane_norm(x, gain):
    mean = jnp.mean(x, axis=-1, keepdims=True)
    cen = x - mean
    var = jnp.mean(cen * cen, axis=-1, keepdims=True)
    return (cen * lax.rsqrt(var + epsilon) * gain).astype(bf16)


def dot(a, b):
    return jnp.dot(a, b, preferred_element_type=f32)


def dot_t(a, b):
    return lax.dot_general(a, b, (((1,), (1,)), ((), ())), preferred_element_type=f32)


def gelu_twice(v):
    u = v * (0.7978845608028654 + 0.035677408136300125 * (v * v))
    return v + v * jnp.tanh(u)


def qkv_rows(x, gain, wqkv):
    n = lane_norm(x, gain)
    p = dot(n, wqkv)
    q = (p[:, :192] * (LOG2E / 32**0.5)).astype(bf16)
    return jnp.concatenate([q, p[:, 192:].astype(bf16)], axis=1)


def attend(qkv, rows, bias_main, bias_tail, k_tail, v_tail, v_pair):
    head = lax.broadcasted_iota(jnp.int32, (1, 192), 1) // 32
    zero = jnp.zeros((), bf16)
    group = lax.broadcasted_iota(jnp.int32, (144, 128), 1) // 16
    rest = pl.ds(rows + 128, 16)
    kt, vt = qkv[rest, 192:384], qkv[rest, 384:576]
    for h in range(6):
        k_tail[16 * h : 16 * h + 16, :] = jnp.where(head == h, kt, zero)
        v_tail[16 * h : 16 * h + 16, :] = jnp.where(head == h, vt, zero)
    q = qkv[pl.ds(rows, 144), :192]
    k = qkv[pl.ds(rows, 128), 192:384]
    for h in range(6):
        v_pair[128 * h : 128 * h + 128, :] = jnp.where(head == h, qkv[pl.ds(rows, 128), 384:576], zero)
    tail = dot_t(q, k_tail[...]) + bias_tail
    mains, maxes = [], []
    for h in range(6):
        s = dot_t(jnp.where(head == h, q, zero), k) + bias_main(h)
        m = jnp.max(jnp.maximum(s, jnp.where(group == h, tail, -3.0e38)), axis=-1, keepdims=True)
        mains.append(s)
        maxes.append(m)
    mt = jnp.broadcast_to(maxes[0], (144, 128))
    for h in range(1, 6):
        mt = jnp.where(group == h, maxes[h], mt)
    pt = jnp.where(group < 6, jnp.exp2(tail - mt), 0.0)
    both = dot(pt.astype(bf16), v_tail[...])
    lane = lax.broadcasted_iota(jnp.int32, (144, 128), 1) // 32
    outs = []
    for half, heads in ((0, (0, 1, 2, 3)), (1, (4, 5))):
        at = slice(0, 128) if half == 0 else slice(128, 192)
        width = at.stop - at.start
        acc, total, held = both[:, at], None, None
        for h in heads:
            p = jnp.exp2(mains[h] - maxes[h])
            d = jnp.sum(p + jnp.where(group == h, pt, 0.0), axis=-1, keepdims=True)
            if h % 2 == 0:
                held = p.astype(bf16)
            else:
                lhs = jnp.concatenate([held, p.astype(bf16)], axis=1)
                acc = acc + dot(lhs, v_pair[128 * h - 128 : 128 * h + 128, at])
            if total is None:
                total = jnp.broadcast_to(d, (144, width))
            else:
                total = jnp.where(lane[:, :width] == h - 4 * half, d, total)
        outs.append(acc * (1.0 / total))
    return jnp.concatenate(outs, axis=1).astype(bf16)


def ffn_rows(x, att, wout, gain, wup, wdown_t):
    hidden = (x + dot(att, wout)).astype(bf16)
    hf = hidden.astype(f32)
    n = lane_norm(hf, gain)
    act = gelu_twice(dot(n, wup)).astype(bf16)
    return (hf + 0.5 * dot_t(act, wdown_t)).astype(bf16).astype(f32)


MESH = pl.DeviceIdType.MESH
LI_ROWS = 24 * PITCH


BIAS_LOW = -4.0
BIAS_STEP = 306.0 / 65535.0


def unpacked(word):
    parts = (lax.shift_right_logical(word, 16), word & 65535)
    return [p.astype(f32) * (BIAS_STEP * LOG2E) for p in parts]


def build_table(tb_ref, t_ref, piece):
    def rows(k0, width):
        for b in range(2):
            for n in range(18):
                piece[b, 4 * n : 4 * n + 4, :width] = tb_ref[b, n // 6, n % 6, :, pl.ds(k0, width)]
        fixed = [
            jnp.clip(jnp.floor((piece[b] - BIAS_LOW) * (1.0 / BIAS_STEP) + 0.5), 0.0, 65535.0).astype(jnp.int32)
            for b in range(2)
        ]
        t_ref[pl.ds(k0, 128), :] = ((fixed[0] << 16) | fixed[1]).T

    def step(k, carry):
        rows(pl.multiple_of(k * 128, 128), 128)
        return carry

    piece[...] = jnp.zeros_like(piece)
    lax.fori_loop(0, 25, step, 0)
    rows(3200, 112)


def gather_rows(idx_ref, t_ref, g_ref, t):
    t3 = t_ref.reshape(3328, 1, 128)
    for s in range(144):
        i = idx_ref.at[pl.ds(s, 20736 - 143)][t * 144]
        g_ref[pl.ds(s, 1), :] = t3[i]


def spread(g_ref, bm, bt, t, lane):
    tr = g_ref[:128, :].T
    for r in range(9):
        for b, x in enumerate(unpacked(tr[r * 8 : r * 8 + 8])):
            bm[b, pl.ds(r * 8 * PITCH + t, 8, stride=PITCH), :] = x
    tt = jnp.concatenate([g_ref[128:144, :]] * 8, 0).T
    for li in range(3):
        v = [tt[(li * 3 + n) * 8 : (li * 3 + n) * 8 + 8] for n in range(3)]
        acc = jnp.where(lane < 2, v[0], jnp.where(lane < 4, v[1], v[2]))
        acc = jnp.where(lane % 2 == 0, acc, jnp.concatenate([acc[4:], acc[:4]], 0))
        for b, x in enumerate(unpacked(acc)):
            bt[b, pl.ds(li * 8 * PITCH + t, 8, stride=PITCH), :] = x


UN = 8


def expand_bias(idx_ref, tb_ref, t_ref, piece, ga, gb, bm, bt):
    build_table(tb_ref, t_ref, piece)
    lane8 = lax.broadcasted_iota(jnp.int32, (8, 128), 1) // 16
    gather_rows(idx_ref, t_ref, ga, 0)
    gs = [ga, gb]

    def step(u, carry):
        t = UN * u
        for k in range(UN):
            spread(gs[k % 2], bm, bt, t + k, lane8)
            nxt = t + k + 1
            gather_rows(idx_ref, t_ref, gs[(k + 1) % 2], jnp.minimum(nxt, 143) if k == UN - 1 else nxt)
        return carry

    lax.fori_loop(0, 144 // UN, step, 0)


def mask_bias(bm, bt, last_lat):
    tok = lax.broadcasted_iota(jnp.int32, (144, 128), 0)
    key = lax.broadcasted_iota(jnp.int32, (144, 128), 1)
    key_t = 128 + key % 16

    def level(t):
        return t // 72

    def row(t):
        return ((t // 12) % 6) // 3

    def cut(lo, hi, window, code):
        differ = code(tok) != code(key)
        differ_t = code(tok) != code(key_t)

        def step(n, carry):
            li, a = window(n)
            for h in range(6):
                at = pl.ds(pl.multiple_of((li * 24 + h * 4 + a) * PITCH, 8), 144)
                bm[1, at, :] = jnp.where(differ, -1e30, bm[1, at, :])
            at = pl.ds(pl.multiple_of((li * 8 + a) * PITCH, 8), 144)
            bt[1, at, :] = jnp.where(differ_t, -1e30, bt[1, at, :])
            return carry

        lax.fori_loop(lo, hi, step, 0)

    cut(0, 3, lambda n: (n, 3), level)

    @pl.when(last_lat)
    def _():
        cut(0, 4, lambda n: (2, n), row)


def block_rows(b, li, cur, ws, gains, bm, bt, qkv, att, k_tail, v_tail, v_pair):
    wq, wo, wu, wd = ws

    def first(g, carry):
        x = cur[b, pl.ds(4 * li + 2 * g, 2)].reshape(288, 192)
        qkv[pl.ds(pl.multiple_of(g * 288, 288), 288), :] = qkv_rows(x, gains[b, 0:1, :], wq[b])
        return carry

    lax.fori_loop(0, 2, first, 0)

    def second(a, carry):
        def main(h):
            return bm[b, pl.ds(pl.multiple_of((li * 24 + h * 4 + a) * PITCH, 8), 144), :]

        start = pl.multiple_of(a * 144, 144)
        tail = bt[b, pl.ds(pl.multiple_of((li * 8 + a) * PITCH, 8), 144), :]
        att[pl.ds(start, 144), :] = attend(qkv, start, main, tail, k_tail, v_tail, v_pair)
        return carry

    lax.fori_loop(0, 4, second, 0, unroll=2)

    def third(g, carry):
        x = cur[b, pl.ds(4 * li + 2 * g, 2)].reshape(288, 192)
        rows = pl.ds(pl.multiple_of(g * 288, 288), 288)
        out = ffn_rows(x, att[rows, :], wo[b], gains[b, 1:2, :], wu[b], wd[b])
        cur[b, pl.ds(4 * li + 2 * g, 2)] = out.reshape(2, 144, 192)
        return carry

    lax.fori_loop(0, 2, third, 0)


PARTS = ((0, 1, 2, 3, 8), (4, 5, 6, 7))
FAR_FIRST = (8, 7, 9, 6, 10, 5, 11, 4, 12, 3, 13, 2, 14, 1, 15)


def less(a, b, axis):
    return jnp.sum(jnp.where(a < b, 1.0, 0.0), axis=axis, keepdims=True)


def thirds(rank):
    peer = jnp.floor((rank + 0.5) * (1.0 / 3))
    return 13.0 * peer + rank


def column_places(order_ref, lon, send_ref, place_ref):
    order = order_ref[...].astype(f32).reshape(1, 768)
    row = lax.broadcasted_iota(jnp.int32, (128, 1), 0)
    lane = lax.broadcasted_iota(jnp.int32, (128, 768), 1)
    level, col = (row % 64) // 8, row % 8
    wide = lon * 6 + col + 3
    ids = level * 96 + jnp.where(wide >= 96, wide - 96, wide)
    hit = order == ids.astype(f32)
    place = jnp.sum(jnp.where(hit, lane.astype(f32), 0.0), axis=1, keepdims=True)
    place = jnp.where(col < 6, place, 1e6)
    across = jnp.broadcast_to(place, (128, 128))
    send_ref[...] = jnp.broadcast_to(thirds(less(across[:64], across.T[:1], 0)), (8, 128))
    mine = jnp.sum(jnp.where(lane == lon * 48 + row, order, 0.0), axis=1, keepdims=True)
    east = mine - 96.0 * jnp.floor((mine + 0.5) * (1.0 / 96)) - 3.0
    east = jnp.where(east < 0.0, east + 96.0, east)
    key = jnp.floor((east + 0.5) * (1.0 / 6)) * 48.0 + row.astype(f32)
    key = jnp.where(row < 48, key, 1e6)
    across = jnp.broadcast_to(key, (128, 128))
    at = thirds(less(across.T[:1], key, 1))
    place_ref[...] = jnp.broadcast_to(at[:48], (48, 128))


def split(ref, rows, x):
    ref[0, rows, :] = x[:, :128]
    ref[1, rows, :64] = x[:, 128:]


def kernel(
    idx, tb, gains, mgain, order, x_hbm, wq_hbm, wo_hbm, wu_hbm, wd_hbm, wm_hbm,
    out,
    table, piece, ga, gb, bm, bt, xin, xf, xy, qkv, att, k_tail, v_tail, v_pair, wq, wo, wu, wd, wm,
    stage, half_out, half_in, north_out, north_in, lines, back_out, back_in, back, cells, merged, fan_out, fan_in, send_at, place_at,
    load, half_s, half_r, north_s, north_r, back_s, back_r, fan_s, fan_r,
):
    lats, lons = lax.axis_size("lat"), lax.axis_size("lon")
    lat, lon = lax.axis_index("lat"), lax.axis_index("lon")
    up, down = lax.rem(lat + lats - 1, lats), lax.rem(lat + 1, lats)
    west, east = lax.rem(lon + lons - 1, lons), lax.rem(lon + 1, lons)

    barrier = pltpu.get_barrier_semaphore()
    greet = [(lat, lax.rem(lon + k, lons)) for k in range(1, 16)] + [(down, lon), (down, east), (up, lon)]
    for where in greet:
        pl.semaphore_signal(barrier, inc=1, device_id=where, device_id_type=MESH)

    pairs = [(x_hbm, xin), (wq_hbm, wq), (wo_hbm, wo), (wu_hbm, wu), (wd_hbm, wd), (wm_hbm, wm)]
    loads = [pltpu.make_async_copy(s, d, load.at[n]) for n, (s, d) in enumerate(pairs)]
    for c in loads:
        c.start()
    column_places(order, lon, send_at, place_at)
    expand_bias(idx, tb, table, piece, ga, gb, bm, bt)
    mask_bias(bm, bt, lat == lats - 1)
    for c in loads:
        c.wait()
    pl.semaphore_wait(barrier, 18)
    ws = (wq, wo, wu, wd)
    x3, y3 = xy.at[0], xy.at[1]

    split(xf, pl.ds(0, 1728), xin[...].reshape(1728, 192).astype(f32))
    def window(w, carry):
        for zz in range(2):
            for r in range(6):
                i = zz * 6 + r
                at = pl.ds((6 * (w // 4) + r) * 96 + 2 * (w % 4) + zz, 16, stride=8)
                x3[w, 12 * i : 12 * i + 12, :128] = xf[0, at, :][:12]
                x3[w, 12 * i : 12 * i + 12, 128:] = xf[1, at, :][:12, :64]
        return carry

    lax.fori_loop(0, 12, window, 0)
    stage[...] = jnp.zeros_like(stage)
    k_tail[...] = jnp.zeros_like(k_tail)
    v_tail[...] = jnp.zeros_like(v_tail)

    def half_copy(li, a, rh):
        target = jnp.where(li + rh == 0, up, lat)
        n = (li * 4 + a) * 2 + rh
        return pltpu.make_async_remote_copy(
            src_ref=half_out.at[n], dst_ref=half_in.at[n], send_sem=half_s.at[n], recv_sem=half_r.at[n],
            device_id=(target, west), device_id_type=MESH,
        )

    def north_copy(a):
        return pltpu.make_async_remote_copy(
            src_ref=north_out.at[a], dst_ref=north_in.at[a], send_sem=north_s.at[a], recv_sem=north_r.at[a],
            device_id=(up, lon), device_id_type=MESH,
        )

    def moved(a, zz):
        return (a, 0) if zz == 1 else ((a + 3) % 4, 1)

    def send_row_of_windows(li):
        for a in range(4):
            w = li * 4 + a
            for rh in range(2):
                for rr in range(3):
                    for zz in range(2):
                        at = 12 * (zz * 6 + 3 * rh + rr)
                        to = 6 * (rr * 2 + zz)
                        stage[a * 2 + rh, to : to + 6, :] = x3[w, at : at + 6, :]
                half_out[w * 2 + rh] = stage[a * 2 + rh].astype(bf16)
                half_copy(li, a, rh).start()

        @pl.when(li == 0)
        def _():
            for a in range(4):
                for rr in range(3):
                    for zz in range(2):
                        at = 12 * (zz * 6 + rr) + 6
                        to = 6 * (rr * 2 + zz)
                        stage[a, to : to + 6, :] = x3[a, at : at + 6, :]
                north_out[a] = stage[a].astype(bf16)
                north_copy(a).start()

        for a in range(4):
            for zz in range(2):
                a2, z2 = moved(a, zz)
                for r in range(3, 6):
                    at, to = 12 * (zz * 6 + r) + 6, 12 * (z2 * 6 + r - 3)
                    y3[li * 4 + a2, to : to + 6, :] = x3[li * 4 + a, at : at + 6, :]

        @pl.when(li > 0)
        def _():
            for a in range(4):
                for zz in range(2):
                    a2, z2 = moved(a, zz)
                    for r in range(3):
                        at, to = 12 * (zz * 6 + r) + 6, 12 * (z2 * 6 + r + 3)
                        y3[(li - 1) * 4 + a2, to : to + 6, :] = x3[li * 4 + a, at : at + 6, :]

    def place_half(li, block, a, rh, col):
        for rr in range(3):
            for zz in range(2):
                a2, z2 = moved(a, zz)
                to = 12 * (z2 * 6 + (rr if rh == 1 else rr + 3)) + col
                y3[li * 4 + a2, to : to + 6, :] = stage[block, 6 * (rr * 2 + zz) : 6 * (rr * 2 + zz) + 6, :]

    def receive_row_of_windows(li):
        nxt = lax.rem(li + 1, 3)
        for rh, source in ((1, li), (0, nxt)):
            for a in range(4):
                half_copy(source, a, rh).wait_recv()
                stage[a * 2 + rh] = half_in[(source * 4 + a) * 2 + rh].astype(f32)
                place_half(li, a * 2 + rh, a, rh, 6)

        @pl.when(li == 2)
        def _():
            for a in range(4):
                north_copy(a).wait_recv()
                stage[a] = north_in[a].astype(f32)
                place_half(li, a, a, 0, 0)

    back_copy = pltpu.make_async_remote_copy(
        src_ref=back_out, dst_ref=back_in, send_sem=back_s.at[0], recv_sem=back_r.at[0],
        device_id=(down, lon), device_id_type=MESH,
    )

    def step(k, carry):
        li = lax.rem(k + 2, 3)
        b = k // 3

        @pl.when(b == 1)
        def _():
            receive_row_of_windows(li)

        block_rows(b, li, xy, ws, gains, bm, bt, qkv, att, k_tail, v_tail, v_pair)

        @pl.when(b == 0)
        def _():
            send_row_of_windows(li)

        @pl.when(b == 1)
        def _():
            finish(li)

        return carry

    def finish(li):
        @pl.when(li == 2)
        def _():
            for rr in range(3):
                for a in range(4):
                    for zz in range(2):
                        to = 12 * (rr * 8 + 2 * a + zz)
                        at = 12 * (zz * 6 + rr + 3)
                        lines[to : to + 12, :] = y3[8 + a, at : at + 12, :]
            back_out[...] = lines[...].astype(bf16)
            back_copy.start()

        for a in range(4):
            w = li * 4 + a
            split(xf, pl.ds(pl.multiple_of(w * 144, 144), 144), y3[w])

        @pl.when(li == 0)
        def _():
            back_copy.wait_recv()
            split(back, pl.ds(0, 288), back_in[...].astype(f32))
            flush(0)

    def line(rho, lev, par):
        if rho < 0:
            return back, pl.ds(12 * ((rho + 3) * 8 + lev) + par, 8, stride=2)
        at = ((rho // 6) * 4 + lev // 2) * 144 + 12 * ((lev % 2) * 6 + rho % 6)
        return xf, pl.ds(at + par, 8, stride=2)

    def fan_copy(part, k):
        peer = lax.rem(lon + k, lons)
        return pltpu.make_async_remote_copy(
            src_ref=fan_out.at[part, peer], dst_ref=fan_in.at[part, lon],
            send_sem=fan_s.at[part, k], recv_sem=fan_r.at[part, k],
            device_id=(lat, peer), device_id_type=MESH,
        )

    def flush(part):
        ready = PARTS[part]
        base, size = 64 * 5 * part, 64 * len(ready)

        def level(z, carry):
            lev = lax.rem(z + 7, 8)
            for n, i in enumerate(ready):
                to = pl.ds(pl.multiple_of(base + (n * 8 + z) * 8, 8), 8)
                for q in range(4):
                    ref, at = line(2 * i - 3 + q % 2, lev, q // 2)
                    cells[q, to, :128] = ref[0, at, :]
                    cells[q, to, 128:] = ref[1, at, :][:, :64]
            return carry

        lax.fori_loop(0, 8, level, 0)

        def merge(g, carry):
            rows = pl.ds(pl.multiple_of(base + g * (size // 2), 16), size // 2)
            xs = [cells[q, rows, :] for q in range(4)]
            mean = sum(jnp.sum(x, axis=-1, keepdims=True) for x in xs) * (1.0 / 768)
            cs = [x - mean for x in xs]
            var = sum(jnp.sum(c * c, axis=-1, keepdims=True) for c in cs) * (1.0 / 768)
            scale = lax.rsqrt(var + epsilon)
            gain = mgain[...].reshape(1, 768)
            total = None
            for q in range(4):
                piece_gain = gain[:, 192 * q : 192 * q + 192]
                part_sum = dot((cs[q] * scale * piece_gain).astype(bf16), wm[q])
                total = part_sum if total is None else total + part_sum
            merged[rows, :] = total.astype(bf16)
            return carry

        lax.fori_loop(0, 2, merge, 0)
        lane = lax.broadcasted_iota(jnp.int32, (1, 128), 1)
        blocks = [send_at[0:1, :] + (3 * (2 * m + lane // 64)).astype(f32) for m in range((len(ready) + 1) // 2)]
        where = jnp.concatenate(blocks, axis=1)[:, :size]
        pick = lax.broadcasted_iota(jnp.int32, (256, size), 0).astype(f32) == where
        fan = dot(jnp.where(pick, 1.0, 0.0).astype(bf16), merged[base : base + size, :])
        fan_out[part] = fan.astype(bf16).reshape(16, 16, 384)
        for k in FAR_FIRST:
            fan_copy(part, k).start()
        fan_in[part, lon] = fan_out[part, lon]

    xf[:, 1728:, :] = jnp.zeros((2, 32, 128), f32)
    back[:, 288:, :] = jnp.zeros((2, 8, 128), f32)
    lax.fori_loop(0, 6, step, 0)
    flush(1)

    for part in range(2):
        for k in FAR_FIRST:
            fan_copy(part, k).wait_recv()
        arrived = fan_in[part].reshape(256, 384)
        slot = lax.broadcasted_iota(jnp.int32, (48, 256), 1).astype(f32)
        picks = [
            jnp.where(slot == place_at[...][:, :1] + 3.0 * n, 1.0, 0.0).astype(bf16) for n in range(len(PARTS[part]))
        ]
        rows = dot(jnp.concatenate(picks, axis=0), arrived).astype(bf16)
        for n, i in enumerate(PARTS[part]):
            out[i] = rows[48 * n : 48 * n + 48]

    for n in range(24):
        half_copy(n // 8, (n // 2) % 4, n % 2).wait_send()
    for a in range(4):
        north_copy(a).wait_send()
    back_copy.wait_send()
    for part in range(2):
        for k in FAR_FIRST:
            fan_copy(part, k).wait_send()


VM = pl.BlockSpec(memory_space=pltpu.VMEM)
HB = pl.BlockSpec(memory_space=pl.ANY)
SM = pl.BlockSpec(memory_space=pltpu.SMEM)


def whole(idx, tables, gains, mgain, order, x, wq, wo, wu, wd, wm):
    v = pltpu.VMEM
    dma = pltpu.SemaphoreType.DMA
    return pl.pallas_call(
        kernel,
        out_shape=jax.ShapeDtypeStruct((9, 48, 384), bf16),
        in_specs=[SM] + [VM] * 4 + [HB] * 6,
        out_specs=VM,
        scratch_shapes=[
            v((3328, 128), jnp.int32),
            v((2, 128, 128), f32),
            v((144, 128), jnp.int32),
            v((144, 128), jnp.int32),
            v((2, 72 * PITCH, 128), f32),
            v((2, 24 * PITCH, 128), f32),
            v(x.shape, bf16),
            v((2, 1760, 128), f32),
            v((2, 12, 144, 192), f32),
            v((576, 576), bf16),
            v((576, 192), bf16),
            v((128, 192), bf16),
            v((128, 192), bf16),
            v((768, 192), bf16),
            v(wq.shape, bf16),
            v(wo.shape, bf16),
            v(wu.shape, bf16),
            v(wd.shape, bf16),
            v(wm.shape, bf16),
            v((8, 48, 192), f32),
            v((24, 48, 192), bf16),
            v((24, 48, 192), bf16),
            v((4, 48, 192), bf16),
            v((4, 48, 192), bf16),
            v((288, 192), f32),
            v((288, 192), bf16),
            v((288, 192), bf16),
            v((2, 296, 128), f32),
            v((4, 576, 192), f32),
            v((576, 384), bf16),
            v((2, 16, 16, 384), bf16),
            v((2, 16, 16, 384), bf16),
            v((8, 128), f32),
            v((48, 128), f32),
            dma((6,)),
            dma((24,)),
            dma((24,)),
            dma((4,)),
            dma((4,)),
            dma((1,)),
            dma((1,)),
            dma((2, 16)),
            dma((2, 16)),
        ],
        compiler_params=pltpu.CompilerParams(vmem_limit_bytes=60 << 20, collective_id=0, has_side_effects=True),
        name="whole_pair",
    )(idx, tables, gains, mgain, order, x, wq, wo, wu, wd, wm)


def body(
    fine_field,
    qkv_weight,
    out_weight,
    up_weight,
    down_weight,
    norm_gain,
    bias_table,
    bias_index,
    merge_gain,
    merge_weight,
    column_order,
):
    result = whole(
        bias_index.reshape(-1),
        bias_table.transpose(0, 1, 3, 2, 4),
        norm_gain,
        merge_gain,
        column_order,
        fine_field.transpose(1, 2, 0, 3),
        qkv_weight,
        out_weight,
        up_weight,
        down_weight.transpose(0, 2, 1),
        merge_weight.reshape(4, 192, 384),
    )
    return result.transpose(1, 0, 2)


def solution(mesh):
    in_specs = (
        P(None, "lat", "lon", None),
        P(),
        P(),
        P(),
        P(),
        P(),
        P(None, "lat", None, None, None),
        P(),
        P(),
        P(),
        P(),
    )
    out_specs = P("lon", "lat", None)
    return jax.shard_map(body, mesh=mesh, in_specs=in_specs, out_specs=out_specs, check_vma=False)
```

```python
import functools
import jax
import jax.numpy as jnp
from jax import lax
from jax.experimental import pallas as pl
from jax.experimental.pallas import tpu as pltpu
from jax.sharding import PartitionSpec as P

epsilon = 1e-05
LOG2E = 1.4426950408889634
PITCH = 152
f32 = jnp.float32
bf16 = jnp.bfloat16


def lane_norm(x, gain):
    mean = jnp.mean(x, axis=-1, keepdims=True)
    cen = x - mean
    var = jnp.mean(cen * cen, axis=-1, keepdims=True)
    return (cen * lax.rsqrt(var + epsilon) * gain).astype(bf16)


def dot(a, b):
    return jnp.dot(a, b, preferred_element_type=f32)


def dot_t(a, b):
    return lax.dot_general(a, b, (((1,), (1,)), ((), ())), preferred_element_type=f32)


def gelu_twice(v):
    u = v * (0.7978845608028654 + 0.035677408136300125 * (v * v))
    return v + v * jnp.tanh(u)


def qkv_rows(x, gain, wqkv):
    n = lane_norm(x, gain)
    p = dot(n, wqkv)
    q = (p[:, :192] * (LOG2E / 32**0.5)).astype(bf16)
    return jnp.concatenate([q, p[:, 192:].astype(bf16)], axis=1)


def attend(qkv, rows, bias_main, bias_tail, k_tail, v_tail, v_pair):
    head = lax.broadcasted_iota(jnp.int32, (1, 192), 1) // 32
    zero = jnp.zeros((), bf16)
    group = lax.broadcasted_iota(jnp.int32, (144, 128), 1) // 16
    rest = pl.ds(rows + 128, 16)
    kt, vt = qkv[rest, 192:384], qkv[rest, 384:576]
    for h in range(6):
        k_tail[16 * h : 16 * h + 16, :] = jnp.where(head == h, kt, zero)
        v_tail[16 * h : 16 * h + 16, :] = jnp.where(head == h, vt, zero)
    q = qkv[pl.ds(rows, 144), :192]
    k = qkv[pl.ds(rows, 128), 192:384]
    for h in range(6):
        v_pair[128 * h : 128 * h + 128, :] = jnp.where(head == h, qkv[pl.ds(rows, 128), 384:576], zero)
    tail = dot_t(q, k_tail[...]) + bias_tail
    mains, maxes = [], []
    for h in range(6):
        s = dot_t(jnp.where(head == h, q, zero), k) + bias_main(h)
        m = jnp.max(jnp.maximum(s, jnp.where(group == h, tail, -3.0e38)), axis=-1, keepdims=True)
        mains.append(s)
        maxes.append(m)
    mt = jnp.broadcast_to(maxes[0], (144, 128))
    for h in range(1, 6):
        mt = jnp.where(group == h, maxes[h], mt)
    pt = jnp.where(group < 6, jnp.exp2(tail - mt), 0.0)
    both = dot(pt.astype(bf16), v_tail[...])
    lane = lax.broadcasted_iota(jnp.int32, (144, 128), 1) // 32
    outs = []
    for half, heads in ((0, (0, 1, 2, 3)), (1, (4, 5))):
        at = slice(0, 128) if half == 0 else slice(128, 192)
        width = at.stop - at.start
        acc, total, held = both[:, at], None, None
        for h in heads:
            p = jnp.exp2(mains[h] - maxes[h])
            d = jnp.sum(p + jnp.where(group == h, pt, 0.0), axis=-1, keepdims=True)
            if h % 2 == 0:
                held = p.astype(bf16)
            else:
                lhs = jnp.concatenate([held, p.astype(bf16)], axis=1)
                acc = acc + dot(lhs, v_pair[128 * h - 128 : 128 * h + 128, at])
            if total is None:
                total = jnp.broadcast_to(d, (144, width))
            else:
                total = jnp.where(lane[:, :width] == h - 4 * half, d, total)
        outs.append(acc * (1.0 / total))
    return jnp.concatenate(outs, axis=1).astype(bf16)


def ffn_rows(x, att, wout, gain, wup, wdown_t):
    hidden = (x + dot(att, wout)).astype(bf16)
    hf = hidden.astype(f32)
    n = lane_norm(hf, gain)
    act = gelu_twice(dot(n, wup)).astype(bf16)
    return (hf + 0.5 * dot_t(act, wdown_t)).astype(bf16).astype(f32)


MESH = pl.DeviceIdType.MESH
LI_ROWS = 24 * PITCH


BIAS_LOW = -4.0
BIAS_STEP = 306.0 / 65535.0


def unpacked(word):
    parts = (lax.shift_right_logical(word, 16), word & 65535)
    return [p.astype(f32) * (BIAS_STEP * LOG2E) for p in parts]


def build_table(tb_ref, t_ref, piece):
    def rows(k0, width):
        for b in range(2):
            for n in range(18):
                piece[b, 4 * n : 4 * n + 4, :width] = tb_ref[b, n // 6, n % 6, :, pl.ds(k0, width)]
        fixed = [
            jnp.clip(jnp.floor((piece[b] - BIAS_LOW) * (1.0 / BIAS_STEP) + 0.5), 0.0, 65535.0).astype(jnp.int32)
            for b in range(2)
        ]
        t_ref[pl.ds(k0, 128), :] = ((fixed[0] << 16) | fixed[1]).T

    def step(k, carry):
        rows(pl.multiple_of(k * 128, 128), 128)
        return carry

    piece[...] = jnp.zeros_like(piece)
    lax.fori_loop(0, 25, step, 0)
    rows(3200, 112)


def gather_rows(idx_ref, t_ref, g_ref, t):
    t3 = t_ref.reshape(3328, 1, 128)
    for s in range(144):
        i = idx_ref.at[pl.ds(s, 20736 - 143)][t * 144]
        g_ref[pl.ds(s, 1), :] = t3[i]


def spread(g_ref, bm, bt, t, lane):
    tr = g_ref[:128, :].T
    for r in range(9):
        for b, x in enumerate(unpacked(tr[r * 8 : r * 8 + 8])):
            bm[b, pl.ds(r * 8 * PITCH + t, 8, stride=PITCH), :] = x
    tt = jnp.concatenate([g_ref[128:144, :]] * 8, 0).T
    for li in range(3):
        v = [tt[(li * 3 + n) * 8 : (li * 3 + n) * 8 + 8] for n in range(3)]
        acc = jnp.where(lane < 2, v[0], jnp.where(lane < 4, v[1], v[2]))
        acc = jnp.where(lane % 2 == 0, acc, jnp.concatenate([acc[4:], acc[:4]], 0))
        for b, x in enumerate(unpacked(acc)):
            bt[b, pl.ds(li * 8 * PITCH + t, 8, stride=PITCH), :] = x


UN = 8


def expand_bias(idx_ref, tb_ref, t_ref, piece, ga, gb, bm, bt):
    build_table(tb_ref, t_ref, piece)
    lane8 = lax.broadcasted_iota(jnp.int32, (8, 128), 1) // 16
    gather_rows(idx_ref, t_ref, ga, 0)
    gs = [ga, gb]

    def step(u, carry):
        t = UN * u
        for k in range(UN):
            spread(gs[k % 2], bm, bt, t + k, lane8)
            nxt = t + k + 1
            gather_rows(idx_ref, t_ref, gs[(k + 1) % 2], jnp.minimum(nxt, 143) if k == UN - 1 else nxt)
        return carry

    lax.fori_loop(0, 144 // UN, step, 0)


def mask_bias(bm, bt, last_lat):
    tok = lax.broadcasted_iota(jnp.int32, (144, 128), 0)
    key = lax.broadcasted_iota(jnp.int32, (144, 128), 1)
    key_t = 128 + key % 16

    def level(t):
        return t // 72

    def row(t):
        return ((t // 12) % 6) // 3

    def cut(lo, hi, window, code):
        differ = code(tok) != code(key)
        differ_t = code(tok) != code(key_t)

        def step(n, carry):
            li, a = window(n)
            for h in range(6):
                at = pl.ds(pl.multiple_of((li * 24 + h * 4 + a) * PITCH, 8), 144)
                bm[1, at, :] = jnp.where(differ, -1e30, bm[1, at, :])
            at = pl.ds(pl.multiple_of((li * 8 + a) * PITCH, 8), 144)
            bt[1, at, :] = jnp.where(differ_t, -1e30, bt[1, at, :])
            return carry

        lax.fori_loop(lo, hi, step, 0)

    cut(0, 3, lambda n: (n, 3), level)

    @pl.when(last_lat)
    def _():
        cut(0, 4, lambda n: (2, n), row)


def block_rows(b, li, cur, ws, gains, bm, bt, qkv, att, k_tail, v_tail, v_pair):
    wq, wo, wu, wd = ws

    def first(g, carry):
        x = cur[b, pl.ds(4 * li + 2 * g, 2)].reshape(288, 192)
        qkv[pl.ds(pl.multiple_of(g * 288, 288), 288), :] = qkv_rows(x, gains[b, 0:1, :], wq[b])
        return carry

    lax.fori_loop(0, 2, first, 0, unroll=2)

    def second(a, carry):
        def main(h):
            return bm[b, pl.ds(pl.multiple_of((li * 24 + h * 4 + a) * PITCH, 8), 144), :]

        start = pl.multiple_of(a * 144, 144)
        tail = bt[b, pl.ds(pl.multiple_of((li * 8 + a) * PITCH, 8), 144), :]
        att[pl.ds(start, 144), :] = attend(qkv, start, main, tail, k_tail, v_tail, v_pair)
        return carry

    lax.fori_loop(0, 4, second, 0, unroll=4)

    def third(g, carry):
        x = cur[b, pl.ds(4 * li + 2 * g, 2)].reshape(288, 192)
        rows = pl.ds(pl.multiple_of(g * 288, 288), 288)
        out = ffn_rows(x, att[rows, :], wo[b], gains[b, 1:2, :], wu[b], wd[b])
        cur[b, pl.ds(4 * li + 2 * g, 2)] = out.reshape(2, 144, 192)
        return carry

    lax.fori_loop(0, 2, third, 0, unroll=2)


PARTS = ((0, 1, 2, 3, 8), (4, 5, 6, 7))
FAR_FIRST = (8, 7, 9, 6, 10, 5, 11, 4, 12, 3, 13, 2, 14, 1, 15)


def less(a, b, axis):
    return jnp.sum(jnp.where(a < b, 1.0, 0.0), axis=axis, keepdims=True)


def thirds(rank):
    peer = jnp.floor((rank + 0.5) * (1.0 / 3))
    return 13.0 * peer + rank


def column_places(order_ref, lon, send_ref, place_ref):
    order = order_ref[...].astype(f32).reshape(1, 768)
    row = lax.broadcasted_iota(jnp.int32, (128, 1), 0)
    lane = lax.broadcasted_iota(jnp.int32, (128, 768), 1)
    level, col = (row % 64) // 8, row % 8
    wide = lon * 6 + col + 3
    ids = level * 96 + jnp.where(wide >= 96, wide - 96, wide)
    hit = order == ids.astype(f32)
    place = jnp.sum(jnp.where(hit, lane.astype(f32), 0.0), axis=1, keepdims=True)
    place = jnp.where(col < 6, place, 1e6)
    across = jnp.broadcast_to(place, (128, 128))
    send_ref[...] = jnp.broadcast_to(thirds(less(across[:64], across.T[:1], 0)), (8, 128))
    mine = jnp.sum(jnp.where(lane == lon * 48 + row, order, 0.0), axis=1, keepdims=True)
    east = mine - 96.0 * jnp.floor((mine + 0.5) * (1.0 / 96)) - 3.0
    east = jnp.where(east < 0.0, east + 96.0, east)
    key = jnp.floor((east + 0.5) * (1.0 / 6)) * 48.0 + row.astype(f32)
    key = jnp.where(row < 48, key, 1e6)
    across = jnp.broadcast_to(key, (128, 128))
    at = thirds(less(across.T[:1], key, 1))
    place_ref[...] = jnp.broadcast_to(at[:48], (48, 128))


def split(ref, rows, x):
    ref[0, rows, :] = x[:, :128]
    ref[1, rows, :64] = x[:, 128:]


def kernel(
    idx, tb, gains, mgain, order, x_hbm, wq_hbm, wo_hbm, wu_hbm, wd_hbm, wm_hbm,
    out,
    table, piece, ga, gb, bm, bt, xin, xf, xy, qkv, att, k_tail, v_tail, v_pair, wq, wo, wu, wd, wm,
    stage, half_out, half_in, north_out, north_in, lines, back_out, back_in, back, cells, merged, fan_out, fan_in, send_at, place_at,
    load, half_s, half_r, north_s, north_r, back_s, back_r, fan_s, fan_r,
):
    lats, lons = lax.axis_size("lat"), lax.axis_size("lon")
    lat, lon = lax.axis_index("lat"), lax.axis_index("lon")
    up, down = lax.rem(lat + lats - 1, lats), lax.rem(lat + 1, lats)
    west, east = lax.rem(lon + lons - 1, lons), lax.rem(lon + 1, lons)

    barrier = pltpu.get_barrier_semaphore()
    greet = [(lat, lax.rem(lon + k, lons)) for k in range(1, 16)] + [(down, lon), (down, east), (up, lon)]
    for where in greet:
        pl.semaphore_signal(barrier, inc=1, device_id=where, device_id_type=MESH)

    pairs = [(x_hbm, xin), (wq_hbm, wq), (wo_hbm, wo), (wu_hbm, wu), (wd_hbm, wd), (wm_hbm, wm)]
    loads = [pltpu.make_async_copy(s, d, load.at[n]) for n, (s, d) in enumerate(pairs)]
    for c in loads:
        c.start()
    column_places(order, lon, send_at, place_at)
    expand_bias(idx, tb, table, piece, ga, gb, bm, bt)
    mask_bias(bm, bt, lat == lats - 1)
    for c in loads:
        c.wait()
    pl.semaphore_wait(barrier, 18)
    ws = (wq, wo, wu, wd)
    x3, y3 = xy.at[0], xy.at[1]

    split(xf, pl.ds(0, 1728), xin[...].reshape(1728, 192).astype(f32))
    def window(w, carry):
        for zz in range(2):
            for r in range(6):
                i = zz * 6 + r
                at = pl.ds((6 * (w // 4) + r) * 96 + 2 * (w % 4) + zz, 16, stride=8)
                x3[w, 12 * i : 12 * i + 12, :128] = xf[0, at, :][:12]
                x3[w, 12 * i : 12 * i + 12, 128:] = xf[1, at, :][:12, :64]
        return carry

    lax.fori_loop(0, 12, window, 0)
    stage[...] = jnp.zeros_like(stage)
    k_tail[...] = jnp.zeros_like(k_tail)
    v_tail[...] = jnp.zeros_like(v_tail)

    def half_copy(li, a, rh):
        target = jnp.where(li + rh == 0, up, lat)
        n = (li * 4 + a) * 2 + rh
        return pltpu.make_async_remote_copy(
            src_ref=half_out.at[n], dst_ref=half_in.at[n], send_sem=half_s.at[n], recv_sem=half_r.at[n],
            device_id=(target, west), device_id_type=MESH,
        )

    def north_copy(a):
        return pltpu.make_async_remote_copy(
            src_ref=north_out.at[a], dst_ref=north_in.at[a], send_sem=north_s.at[a], recv_sem=north_r.at[a],
            device_id=(up, lon), device_id_type=MESH,
        )

    def moved(a, zz):
        return (a, 0) if zz == 1 else ((a + 3) % 4, 1)

    def send_row_of_windows(li):
        for a in range(4):
            w = li * 4 + a
            for rh in range(2):
                for rr in range(3):
                    for zz in range(2):
                        at = 12 * (zz * 6 + 3 * rh + rr)
                        to = 6 * (rr * 2 + zz)
                        stage[a * 2 + rh, to : to + 6, :] = x3[w, at : at + 6, :]
                half_out[w * 2 + rh] = stage[a * 2 + rh].astype(bf16)
                half_copy(li, a, rh).start()

        @pl.when(li == 0)
        def _():
            for a in range(4):
                for rr in range(3):
                    for zz in range(2):
                        at = 12 * (zz * 6 + rr) + 6
                        to = 6 * (rr * 2 + zz)
                        stage[a, to : to + 6, :] = x3[a, at : at + 6, :]
                north_out[a] = stage[a].astype(bf16)
                north_copy(a).start()

        for a in range(4):
            for zz in range(2):
                a2, z2 = moved(a, zz)
                for r in range(3, 6):
                    at, to = 12 * (zz * 6 + r) + 6, 12 * (z2 * 6 + r - 3)
                    y3[li * 4 + a2, to : to + 6, :] = x3[li * 4 + a, at : at + 6, :]

        @pl.when(li > 0)
        def _():
            for a in range(4):
                for zz in range(2):
                    a2, z2 = moved(a, zz)
                    for r in range(3):
                        at, to = 12 * (zz * 6 + r) + 6, 12 * (z2 * 6 + r + 3)
                        y3[(li - 1) * 4 + a2, to : to + 6, :] = x3[li * 4 + a, at : at + 6, :]

    def place_half(li, block, a, rh, col):
        for rr in range(3):
            for zz in range(2):
                a2, z2 = moved(a, zz)
                to = 12 * (z2 * 6 + (rr if rh == 1 else rr + 3)) + col
                y3[li * 4 + a2, to : to + 6, :] = stage[block, 6 * (rr * 2 + zz) : 6 * (rr * 2 + zz) + 6, :]

    def receive_row_of_windows(li):
        nxt = lax.rem(li + 1, 3)
        for rh, source in ((1, li), (0, nxt)):
            for a in range(4):
                half_copy(source, a, rh).wait_recv()
                stage[a * 2 + rh] = half_in[(source * 4 + a) * 2 + rh].astype(f32)
                place_half(li, a * 2 + rh, a, rh, 6)

        @pl.when(li == 2)
        def _():
            for a in range(4):
                north_copy(a).wait_recv()
                stage[a] = north_in[a].astype(f32)
                place_half(li, a, a, 0, 0)

    back_copy = pltpu.make_async_remote_copy(
        src_ref=back_out, dst_ref=back_in, send_sem=back_s.at[0], recv_sem=back_r.at[0],
        device_id=(down, lon), device_id_type=MESH,
    )

    def step(k, carry):
        li = lax.rem(k + 2, 3)
        b = k // 3

        @pl.when(b == 1)
        def _():
            receive_row_of_windows(li)

        block_rows(b, li, xy, ws, gains, bm, bt, qkv, att, k_tail, v_tail, v_pair)

        @pl.when(b == 0)
        def _():
            send_row_of_windows(li)

        @pl.when(b == 1)
        def _():
            finish(li)

        return carry

    def finish(li):
        @pl.when(li == 2)
        def _():
            for rr in range(3):
                for a in range(4):
                    for zz in range(2):
                        to = 12 * (rr * 8 + 2 * a + zz)
                        at = 12 * (zz * 6 + rr + 3)
                        lines[to : to + 12, :] = y3[8 + a, at : at + 12, :]
            back_out[...] = lines[...].astype(bf16)
            back_copy.start()

        for a in range(4):
            w = li * 4 + a
            split(xf, pl.ds(pl.multiple_of(w * 144, 144), 144), y3[w])

        @pl.when(li == 0)
        def _():
            back_copy.wait_recv()
            split(back, pl.ds(0, 288), back_in[...].astype(f32))
            flush(0)

    def line(rho, lev, par):
        if rho < 0:
            return back, pl.ds(12 * ((rho + 3) * 8 + lev) + par, 8, stride=2)
        at = ((rho // 6) * 4 + lev // 2) * 144 + 12 * ((lev % 2) * 6 + rho % 6)
        return xf, pl.ds(at + par, 8, stride=2)

    def fan_copy(part, k):
        peer = lax.rem(lon + k, lons)
        return pltpu.make_async_remote_copy(
            src_ref=fan_out.at[part, peer], dst_ref=fan_in.at[part, lon],
            send_sem=fan_s.at[part, k], recv_sem=fan_r.at[part, k],
            device_id=(lat, peer), device_id_type=MESH,
        )

    def flush(part):
        ready = PARTS[part]
        base, size = 64 * 5 * part, 64 * len(ready)

        def level(z, carry):
            lev = lax.rem(z + 7, 8)
            for n, i in enumerate(ready):
                to = pl.ds(pl.multiple_of(base + (n * 8 + z) * 8, 8), 8)
                for q in range(4):
                    ref, at = line(2 * i - 3 + q % 2, lev, q // 2)
                    cells[q, to, :128] = ref[0, at, :]
                    cells[q, to, 128:] = ref[1, at, :][:, :64]
            return carry

        lax.fori_loop(0, 8, level, 0)

        def merge(g, carry):
            rows = pl.ds(pl.multiple_of(base + g * (size // 2), 16), size // 2)
            xs = [cells[q, rows, :] for q in range(4)]
            mean = sum(jnp.sum(x, axis=-1, keepdims=True) for x in xs) * (1.0 / 768)
            cs = [x - mean for x in xs]
            var = sum(jnp.sum(c * c, axis=-1, keepdims=True) for c in cs) * (1.0 / 768)
            scale = lax.rsqrt(var + epsilon)
            gain = mgain[...].reshape(1, 768)
            total = None
            for q in range(4):
                piece_gain = gain[:, 192 * q : 192 * q + 192]
                part_sum = dot((cs[q] * scale * piece_gain).astype(bf16), wm[q])
                total = part_sum if total is None else total + part_sum
            merged[rows, :] = total.astype(bf16)
            return carry

        lax.fori_loop(0, 2, merge, 0)
        lane = lax.broadcasted_iota(jnp.int32, (1, 128), 1)
        blocks = [send_at[0:1, :] + (3 * (2 * m + lane // 64)).astype(f32) for m in range((len(ready) + 1) // 2)]
        where = jnp.concatenate(blocks, axis=1)[:, :size]
        pick = lax.broadcasted_iota(jnp.int32, (256, size), 0).astype(f32) == where
        fan = dot(jnp.where(pick, 1.0, 0.0).astype(bf16), merged[base : base + size, :])
        fan_out[part] = fan.astype(bf16).reshape(16, 16, 384)
        for k in FAR_FIRST:
            fan_copy(part, k).start()
        fan_in[part, lon] = fan_out[part, lon]

    xf[:, 1728:, :] = jnp.zeros((2, 32, 128), f32)
    back[:, 288:, :] = jnp.zeros((2, 8, 128), f32)
    lax.fori_loop(0, 6, step, 0)
    flush(1)

    for part in range(2):
        for k in FAR_FIRST:
            fan_copy(part, k).wait_recv()
        arrived = fan_in[part].reshape(256, 384)
        slot = lax.broadcasted_iota(jnp.int32, (48, 256), 1).astype(f32)
        picks = [
            jnp.where(slot == place_at[...][:, :1] + 3.0 * n, 1.0, 0.0).astype(bf16) for n in range(len(PARTS[part]))
        ]
        rows = dot(jnp.concatenate(picks, axis=0), arrived).astype(bf16)
        for n, i in enumerate(PARTS[part]):
            out[i] = rows[48 * n : 48 * n + 48]

    for n in range(24):
        half_copy(n // 8, (n // 2) % 4, n % 2).wait_send()
    for a in range(4):
        north_copy(a).wait_send()
    back_copy.wait_send()
    for part in range(2):
        for k in FAR_FIRST:
            fan_copy(part, k).wait_send()


VM = pl.BlockSpec(memory_space=pltpu.VMEM)
HB = pl.BlockSpec(memory_space=pl.ANY)
SM = pl.BlockSpec(memory_space=pltpu.SMEM)


def whole(idx, tables, gains, mgain, order, x, wq, wo, wu, wd, wm):
    v = pltpu.VMEM
    dma = pltpu.SemaphoreType.DMA
    return pl.pallas_call(
        kernel,
        out_shape=jax.ShapeDtypeStruct((9, 48, 384), bf16),
        in_specs=[SM] + [VM] * 4 + [HB] * 6,
        out_specs=VM,
        scratch_shapes=[
            v((3328, 128), jnp.int32),
            v((2, 128, 128), f32),
            v((144, 128), jnp.int32),
            v((144, 128), jnp.int32),
            v((2, 72 * PITCH, 128), f32),
            v((2, 24 * PITCH, 128), f32),
            v(x.shape, bf16),
            v((2, 1760, 128), f32),
            v((2, 12, 144, 192), f32),
            v((576, 576), bf16),
            v((576, 192), bf16),
            v((128, 192), bf16),
            v((128, 192), bf16),
            v((768, 192), bf16),
            v(wq.shape, bf16),
            v(wo.shape, bf16),
            v(wu.shape, bf16),
            v(wd.shape, bf16),
            v(wm.shape, bf16),
            v((8, 48, 192), f32),
            v((24, 48, 192), bf16),
            v((24, 48, 192), bf16),
            v((4, 48, 192), bf16),
            v((4, 48, 192), bf16),
            v((288, 192), f32),
            v((288, 192), bf16),
            v((288, 192), bf16),
            v((2, 296, 128), f32),
            v((4, 576, 192), f32),
            v((576, 384), bf16),
            v((2, 16, 16, 384), bf16),
            v((2, 16, 16, 384), bf16),
            v((8, 128), f32),
            v((48, 128), f32),
            dma((6,)),
            dma((24,)),
            dma((24,)),
            dma((4,)),
            dma((4,)),
            dma((1,)),
            dma((1,)),
            dma((2, 16)),
            dma((2, 16)),
        ],
        compiler_params=pltpu.CompilerParams(vmem_limit_bytes=60 << 20, collective_id=0, has_side_effects=True),
        name="whole_pair",
    )(idx, tables, gains, mgain, order, x, wq, wo, wu, wd, wm)


def body(
    fine_field,
    qkv_weight,
    out_weight,
    up_weight,
    down_weight,
    norm_gain,
    bias_table,
    bias_index,
    merge_gain,
    merge_weight,
    column_order,
):
    result = whole(
        bias_index.reshape(-1),
        bias_table.transpose(0, 1, 3, 2, 4),
        norm_gain,
        merge_gain,
        column_order,
        fine_field.transpose(1, 2, 0, 3),
        qkv_weight,
        out_weight,
        up_weight,
        down_weight.transpose(0, 2, 1),
        merge_weight.reshape(4, 192, 384),
    )
    return result.transpose(1, 0, 2)


def solution(mesh):
    in_specs = (
        P(None, "lat", "lon", None),
        P(),
        P(),
        P(),
        P(),
        P(),
        P(None, "lat", None, None, None),
        P(),
        P(),
        P(),
        P(),
    )
    out_specs = P("lon", "lat", None)
    return jax.shard_map(body, mesh=mesh, in_specs=in_specs, out_specs=out_specs, check_vma=False)
```

```python
import functools
import jax
import jax.numpy as jnp
from jax import lax
from jax.experimental import pallas as pl
from jax.experimental.pallas import tpu as pltpu
from jax.sharding import PartitionSpec as P

epsilon = 1e-05
LOG2E = 1.4426950408889634
PITCH = 152
f32 = jnp.float32
bf16 = jnp.bfloat16


def lane_norm(x, gain):
    mean = jnp.mean(x, axis=-1, keepdims=True)
    cen = x - mean
    var = jnp.mean(cen * cen, axis=-1, keepdims=True)
    return (cen * lax.rsqrt(var + epsilon) * gain).astype(bf16)


def dot(a, b):
    return jnp.dot(a, b, preferred_element_type=f32)


def dot_t(a, b):
    return lax.dot_general(a, b, (((1,), (1,)), ((), ())), preferred_element_type=f32)


def gelu_twice(v):
    u = v * (0.7978845608028654 + 0.035677408136300125 * (v * v))
    return v + v * jnp.tanh(u)


def qkv_rows(x, gain, wqkv):
    n = lane_norm(x, gain)
    p = dot(n, wqkv)
    q = (p[:, :192] * (LOG2E / 32**0.5)).astype(bf16)
    return jnp.concatenate([q, p[:, 192:].astype(bf16)], axis=1)


def attend(qkv, rows, bias_main, bias_tail, k_tail, v_tail, v_pair):
    head = lax.broadcasted_iota(jnp.int32, (1, 192), 1) // 32
    zero = jnp.zeros((), bf16)
    group = lax.broadcasted_iota(jnp.int32, (144, 128), 1) // 16
    rest = pl.ds(rows + 128, 16)
    kt, vt = qkv[rest, 192:384], qkv[rest, 384:576]
    for h in range(6):
        k_tail[16 * h : 16 * h + 16, :] = jnp.where(head == h, kt, zero)
        v_tail[16 * h : 16 * h + 16, :] = jnp.where(head == h, vt, zero)
    q = qkv[pl.ds(rows, 144), :192]
    k = qkv[pl.ds(rows, 128), 192:384]
    for h in range(6):
        v_pair[128 * h : 128 * h + 128, :] = jnp.where(head == h, qkv[pl.ds(rows, 128), 384:576], zero)
    tail = dot_t(q, k_tail[...]) + bias_tail
    mains, maxes = [], []
    for h in range(6):
        s = dot_t(jnp.where(head == h, q, zero), k) + bias_main(h)
        m = jnp.max(jnp.maximum(s, jnp.where(group == h, tail, -3.0e38)), axis=-1, keepdims=True)
        mains.append(s)
        maxes.append(m)
    mt = jnp.broadcast_to(maxes[0], (144, 128))
    for h in range(1, 6):
        mt = jnp.where(group == h, maxes[h], mt)
    pt = jnp.where(group < 6, jnp.exp2(tail - mt), 0.0)
    both = dot(pt.astype(bf16), v_tail[...])
    lane = lax.broadcasted_iota(jnp.int32, (144, 128), 1) // 32
    outs = []
    for half, heads in ((0, (0, 1, 2, 3)), (1, (4, 5))):
        at = slice(0, 128) if half == 0 else slice(128, 192)
        width = at.stop - at.start
        acc, total, held = both[:, at], None, None
        for h in heads:
            p = jnp.exp2(mains[h] - maxes[h])
            d = jnp.sum(p + jnp.where(group == h, pt, 0.0), axis=-1, keepdims=True)
            if h % 2 == 0:
                held = p.astype(bf16)
            else:
                lhs = jnp.concatenate([held, p.astype(bf16)], axis=1)
                acc = acc + dot(lhs, v_pair[128 * h - 128 : 128 * h + 128, at])
            if total is None:
                total = jnp.broadcast_to(d, (144, width))
            else:
                total = jnp.where(lane[:, :width] == h - 4 * half, d, total)
        outs.append(acc * (1.0 / total))
    return jnp.concatenate(outs, axis=1).astype(bf16)


def ffn_rows(x, att, wout, gain, wup, wdown_t):
    hidden = (x + dot(att, wout)).astype(bf16)
    hf = hidden.astype(f32)
    n = lane_norm(hf, gain)
    act = gelu_twice(dot(n, wup)).astype(bf16)
    return (hf + 0.5 * dot_t(act, wdown_t)).astype(bf16).astype(f32)


MESH = pl.DeviceIdType.MESH
LI_ROWS = 24 * PITCH


BIAS_LOW = -4.0
BIAS_STEP = 306.0 / 65535.0


def unpacked(word):
    parts = (lax.shift_right_logical(word, 16), word & 65535)
    return [p.astype(f32) * (BIAS_STEP * LOG2E) for p in parts]


def build_table(tb_ref, t_ref, piece):
    def rows(k0, width):
        for b in range(2):
            for n in range(18):
                piece[b, 4 * n : 4 * n + 4, :width] = tb_ref[b, n // 6, n % 6, :, pl.ds(k0, width)]
        fixed = [
            jnp.clip(jnp.floor((piece[b] - BIAS_LOW) * (1.0 / BIAS_STEP) + 0.5), 0.0, 65535.0).astype(jnp.int32)
            for b in range(2)
        ]
        t_ref[pl.ds(k0, 128), :] = ((fixed[0] << 16) | fixed[1]).T

    def step(k, carry):
        rows(pl.multiple_of(k * 128, 128), 128)
        return carry

    piece[...] = jnp.zeros_like(piece)
    lax.fori_loop(0, 25, step, 0, unroll=5)
    rows(3200, 112)


def gather_rows(idx_ref, t_ref, g_ref, t):
    t3 = t_ref.reshape(3328, 1, 128)
    for s in range(144):
        i = idx_ref.at[pl.ds(s, 20736 - 143)][t * 144]
        g_ref[pl.ds(s, 1), :] = t3[i]


def spread(g_ref, bm, bt, t, lane):
    tr = g_ref[:128, :].T
    for r in range(9):
        for b, x in enumerate(unpacked(tr[r * 8 : r * 8 + 8])):
            bm[b, pl.ds(r * 8 * PITCH + t, 8, stride=PITCH), :] = x
    tt = jnp.concatenate([g_ref[128:144, :]] * 8, 0).T
    for li in range(3):
        v = [tt[(li * 3 + n) * 8 : (li * 3 + n) * 8 + 8] for n in range(3)]
        acc = jnp.where(lane < 2, v[0], jnp.where(lane < 4, v[1], v[2]))
        acc = jnp.where(lane % 2 == 0, acc, jnp.concatenate([acc[4:], acc[:4]], 0))
        for b, x in enumerate(unpacked(acc)):
            bt[b, pl.ds(li * 8 * PITCH + t, 8, stride=PITCH), :] = x


UN = 8


def expand_bias(idx_ref, tb_ref, t_ref, piece, ga, gb, bm, bt):
    build_table(tb_ref, t_ref, piece)
    lane8 = lax.broadcasted_iota(jnp.int32, (8, 128), 1) // 16
    gather_rows(idx_ref, t_ref, ga, 0)
    gs = [ga, gb]

    def step(u, carry):
        t = UN * u
        for k in range(UN):
            spread(gs[k % 2], bm, bt, t + k, lane8)
            nxt = t + k + 1
            gather_rows(idx_ref, t_ref, gs[(k + 1) % 2], jnp.minimum(nxt, 143) if k == UN - 1 else nxt)
        return carry

    lax.fori_loop(0, 144 // UN, step, 0)


def mask_bias(bm, bt, last_lat):
    tok = lax.broadcasted_iota(jnp.int32, (144, 128), 0)
    key = lax.broadcasted_iota(jnp.int32, (144, 128), 1)
    key_t = 128 + key % 16

    def level(t):
        return t // 72

    def row(t):
        return ((t // 12) % 6) // 3

    def cut(lo, hi, window, code):
        differ = code(tok) != code(key)
        differ_t = code(tok) != code(key_t)

        def step(n, carry):
            li, a = window(n)
            for h in range(6):
                at = pl.ds(pl.multiple_of((li * 24 + h * 4 + a) * PITCH, 8), 144)
                bm[1, at, :] = jnp.where(differ, -1e30, bm[1, at, :])
            at = pl.ds(pl.multiple_of((li * 8 + a) * PITCH, 8), 144)
            bt[1, at, :] = jnp.where(differ_t, -1e30, bt[1, at, :])
            return carry

        lax.fori_loop(lo, hi, step, 0)

    cut(0, 3, lambda n: (n, 3), level)

    @pl.when(last_lat)
    def _():
        cut(0, 4, lambda n: (2, n), row)


def block_rows(b, li, cur, ws, gains, bm, bt, qkv, att, k_tail, v_tail, v_pair):
    wq, wo, wu, wd = ws

    def first(g, carry):
        x = cur[b, pl.ds(4 * li + 2 * g, 2)].reshape(288, 192)
        qkv[pl.ds(pl.multiple_of(g * 288, 288), 288), :] = qkv_rows(x, gains[b, 0:1, :], wq[b])
        return carry

    lax.fori_loop(0, 2, first, 0, unroll=2)

    def second(a, carry):
        def main(h):
            return bm[b, pl.ds(pl.multiple_of((li * 24 + h * 4 + a) * PITCH, 8), 144), :]

        start = pl.multiple_of(a * 144, 144)
        tail = bt[b, pl.ds(pl.multiple_of((li * 8 + a) * PITCH, 8), 144), :]
        att[pl.ds(start, 144), :] = attend(qkv, start, main, tail, k_tail, v_tail, v_pair)
        return carry

    lax.fori_loop(0, 4, second, 0, unroll=4)

    def third(g, carry):
        x = cur[b, pl.ds(4 * li + 2 * g, 2)].reshape(288, 192)
        rows = pl.ds(pl.multiple_of(g * 288, 288), 288)
        out = ffn_rows(x, att[rows, :], wo[b], gains[b, 1:2, :], wu[b], wd[b])
        cur[b, pl.ds(4 * li + 2 * g, 2)] = out.reshape(2, 144, 192)
        return carry

    lax.fori_loop(0, 2, third, 0, unroll=2)


PARTS = ((0, 1, 2, 3, 8), (4, 5, 6, 7))
FAR_FIRST = (8, 7, 9, 6, 10, 5, 11, 4, 12, 3, 13, 2, 14, 1, 15)


def less(a, b, axis):
    return jnp.sum(jnp.where(a < b, 1.0, 0.0), axis=axis, keepdims=True)


def thirds(rank):
    peer = jnp.floor((rank + 0.5) * (1.0 / 3))
    return 13.0 * peer + rank


def column_places(order_ref, lon, send_ref, place_ref):
    order = order_ref[...].astype(f32).reshape(1, 768)
    row = lax.broadcasted_iota(jnp.int32, (128, 1), 0)
    lane = lax.broadcasted_iota(jnp.int32, (128, 768), 1)
    level, col = (row % 64) // 8, row % 8
    wide = lon * 6 + col + 3
    ids = level * 96 + jnp.where(wide >= 96, wide - 96, wide)
    hit = order == ids.astype(f32)
    place = jnp.sum(jnp.where(hit, lane.astype(f32), 0.0), axis=1, keepdims=True)
    place = jnp.where(col < 6, place, 1e6)
    across = jnp.broadcast_to(place, (128, 128))
    send_ref[...] = jnp.broadcast_to(thirds(less(across[:64], across.T[:1], 0)), (8, 128))
    mine = jnp.sum(jnp.where(lane == lon * 48 + row, order, 0.0), axis=1, keepdims=True)
    east = mine - 96.0 * jnp.floor((mine + 0.5) * (1.0 / 96)) - 3.0
    east = jnp.where(east < 0.0, east + 96.0, east)
    key = jnp.floor((east + 0.5) * (1.0 / 6)) * 48.0 + row.astype(f32)
    key = jnp.where(row < 48, key, 1e6)
    across = jnp.broadcast_to(key, (128, 128))
    at = thirds(less(across.T[:1], key, 1))
    place_ref[...] = jnp.broadcast_to(at[:48], (48, 128))


def split(ref, rows, x):
    ref[0, rows, :] = x[:, :128]
    ref[1, rows, :64] = x[:, 128:]


def kernel(
    idx, tb, gains, mgain, order, x_hbm, wq_hbm, wo_hbm, wu_hbm, wd_hbm, wm_hbm,
    out,
    table, piece, ga, gb, bm, bt, xin, xf, xy, qkv, att, k_tail, v_tail, v_pair, wq, wo, wu, wd, wm,
    stage, half_out, half_in, north_out, north_in, lines, back_out, back_in, back, cells, merged, fan_out, fan_in, send_at, place_at,
    load, half_s, half_r, north_s, north_r, back_s, back_r, fan_s, fan_r,
):
    lats, lons = lax.axis_size("lat"), lax.axis_size("lon")
    lat, lon = lax.axis_index("lat"), lax.axis_index("lon")
    up, down = lax.rem(lat + lats - 1, lats), lax.rem(lat + 1, lats)
    west, east = lax.rem(lon + lons - 1, lons), lax.rem(lon + 1, lons)

    barrier = pltpu.get_barrier_semaphore()
    greet = [(lat, lax.rem(lon + k, lons)) for k in range(1, 16)] + [(down, lon), (down, east), (up, lon)]
    for where in greet:
        pl.semaphore_signal(barrier, inc=1, device_id=where, device_id_type=MESH)

    pairs = [(x_hbm, xin), (wq_hbm, wq), (wo_hbm, wo), (wu_hbm, wu), (wd_hbm, wd), (wm_hbm, wm)]
    loads = [pltpu.make_async_copy(s, d, load.at[n]) for n, (s, d) in enumerate(pairs)]
    for c in loads:
        c.start()
    column_places(order, lon, send_at, place_at)
    expand_bias(idx, tb, table, piece, ga, gb, bm, bt)
    mask_bias(bm, bt, lat == lats - 1)
    for c in loads:
        c.wait()
    pl.semaphore_wait(barrier, 18)
    ws = (wq, wo, wu, wd)
    x3, y3 = xy.at[0], xy.at[1]

    split(xf, pl.ds(0, 1728), xin[...].reshape(1728, 192).astype(f32))
    def window(w, carry):
        for zz in range(2):
            for r in range(6):
                i = zz * 6 + r
                at = pl.ds((6 * (w // 4) + r) * 96 + 2 * (w % 4) + zz, 16, stride=8)
                x3[w, 12 * i : 12 * i + 12, :128] = xf[0, at, :][:12]
                x3[w, 12 * i : 12 * i + 12, 128:] = xf[1, at, :][:12, :64]
        return carry

    lax.fori_loop(0, 12, window, 0, unroll=2)
    stage[...] = jnp.zeros_like(stage)
    k_tail[...] = jnp.zeros_like(k_tail)
    v_tail[...] = jnp.zeros_like(v_tail)

    def half_copy(li, a, rh):
        target = jnp.where(li + rh == 0, up, lat)
        n = (li * 4 + a) * 2 + rh
        return pltpu.make_async_remote_copy(
            src_ref=half_out.at[n], dst_ref=half_in.at[n], send_sem=half_s.at[n], recv_sem=half_r.at[n],
            device_id=(target, west), device_id_type=MESH,
        )

    def north_copy(a):
        return pltpu.make_async_remote_copy(
            src_ref=north_out.at[a], dst_ref=north_in.at[a], send_sem=north_s.at[a], recv_sem=north_r.at[a],
            device_id=(up, lon), device_id_type=MESH,
        )

    def moved(a, zz):
        return (a, 0) if zz == 1 else ((a + 3) % 4, 1)

    def send_row_of_windows(li):
        for a in range(4):
            w = li * 4 + a
            for rh in range(2):
                for rr in range(3):
                    for zz in range(2):
                        at = 12 * (zz * 6 + 3 * rh + rr)
                        to = 6 * (rr * 2 + zz)
                        stage[a * 2 + rh, to : to + 6, :] = x3[w, at : at + 6, :]
                half_out[w * 2 + rh] = stage[a * 2 + rh].astype(bf16)
                half_copy(li, a, rh).start()

        @pl.when(li == 0)
        def _():
            for a in range(4):
                for rr in range(3):
                    for zz in range(2):
                        at = 12 * (zz * 6 + rr) + 6
                        to = 6 * (rr * 2 + zz)
                        stage[a, to : to + 6, :] = x3[a, at : at + 6, :]
                north_out[a] = stage[a].astype(bf16)
                north_copy(a).start()

        for a in range(4):
            for zz in range(2):
                a2, z2 = moved(a, zz)
                for r in range(3, 6):
                    at, to = 12 * (zz * 6 + r) + 6, 12 * (z2 * 6 + r - 3)
                    y3[li * 4 + a2, to : to + 6, :] = x3[li * 4 + a, at : at + 6, :]

        @pl.when(li > 0)
        def _():
            for a in range(4):
                for zz in range(2):
                    a2, z2 = moved(a, zz)
                    for r in range(3):
                        at, to = 12 * (zz * 6 + r) + 6, 12 * (z2 * 6 + r + 3)
                        y3[(li - 1) * 4 + a2, to : to + 6, :] = x3[li * 4 + a, at : at + 6, :]

    def place_half(li, block, a, rh, col):
        for rr in range(3):
            for zz in range(2):
                a2, z2 = moved(a, zz)
                to = 12 * (z2 * 6 + (rr if rh == 1 else rr + 3)) + col
                y3[li * 4 + a2, to : to + 6, :] = stage[block, 6 * (rr * 2 + zz) : 6 * (rr * 2 + zz) + 6, :]

    def receive_row_of_windows(li):
        nxt = lax.rem(li + 1, 3)
        for rh, source in ((1, li), (0, nxt)):
            for a in range(4):
                half_copy(source, a, rh).wait_recv()
                stage[a * 2 + rh] = half_in[(source * 4 + a) * 2 + rh].astype(f32)
                place_half(li, a * 2 + rh, a, rh, 6)

        @pl.when(li == 2)
        def _():
            for a in range(4):
                north_copy(a).wait_recv()
                stage[a] = north_in[a].astype(f32)
                place_half(li, a, a, 0, 0)

    back_copy = pltpu.make_async_remote_copy(
        src_ref=back_out, dst_ref=back_in, send_sem=back_s.at[0], recv_sem=back_r.at[0],
        device_id=(down, lon), device_id_type=MESH,
    )

    def step(k, carry):
        li = lax.rem(k + 2, 3)
        b = k // 3

        @pl.when(b == 1)
        def _():
            receive_row_of_windows(li)

        block_rows(b, li, xy, ws, gains, bm, bt, qkv, att, k_tail, v_tail, v_pair)

        @pl.when(b == 0)
        def _():
            send_row_of_windows(li)

        @pl.when(b == 1)
        def _():
            finish(li)

        return carry

    def finish(li):
        @pl.when(li == 2)
        def _():
            for rr in range(3):
                for a in range(4):
                    for zz in range(2):
                        to = 12 * (rr * 8 + 2 * a + zz)
                        at = 12 * (zz * 6 + rr + 3)
                        lines[to : to + 12, :] = y3[8 + a, at : at + 12, :]
            back_out[...] = lines[...].astype(bf16)
            back_copy.start()

        for a in range(4):
            w = li * 4 + a
            split(xf, pl.ds(pl.multiple_of(w * 144, 144), 144), y3[w])

        @pl.when(li == 0)
        def _():
            back_copy.wait_recv()
            split(back, pl.ds(0, 288), back_in[...].astype(f32))
            flush(0)

    def line(rho, lev, par):
        if rho < 0:
            return back, pl.ds(12 * ((rho + 3) * 8 + lev) + par, 8, stride=2)
        at = ((rho // 6) * 4 + lev // 2) * 144 + 12 * ((lev % 2) * 6 + rho % 6)
        return xf, pl.ds(at + par, 8, stride=2)

    def fan_copy(part, k):
        peer = lax.rem(lon + k, lons)
        return pltpu.make_async_remote_copy(
            src_ref=fan_out.at[part, peer], dst_ref=fan_in.at[part, lon],
            send_sem=fan_s.at[part, k], recv_sem=fan_r.at[part, k],
            device_id=(lat, peer), device_id_type=MESH,
        )

    def flush(part):
        ready = PARTS[part]
        base, size = 64 * 5 * part, 64 * len(ready)

        def level(z, carry):
            lev = lax.rem(z + 7, 8)
            for n, i in enumerate(ready):
                to = pl.ds(pl.multiple_of(base + (n * 8 + z) * 8, 8), 8)
                for q in range(4):
                    ref, at = line(2 * i - 3 + q % 2, lev, q // 2)
                    cells[q, to, :128] = ref[0, at, :]
                    cells[q, to, 128:] = ref[1, at, :][:, :64]
            return carry

        lax.fori_loop(0, 8, level, 0, unroll=2)

        def merge(g, carry):
            rows = pl.ds(pl.multiple_of(base + g * (size // 2), 16), size // 2)
            xs = [cells[q, rows, :] for q in range(4)]
            mean = sum(jnp.sum(x, axis=-1, keepdims=True) for x in xs) * (1.0 / 768)
            cs = [x - mean for x in xs]
            var = sum(jnp.sum(c * c, axis=-1, keepdims=True) for c in cs) * (1.0 / 768)
            scale = lax.rsqrt(var + epsilon)
            gain = mgain[...].reshape(1, 768)
            total = None
            for q in range(4):
                piece_gain = gain[:, 192 * q : 192 * q + 192]
                part_sum = dot((cs[q] * scale * piece_gain).astype(bf16), wm[q])
                total = part_sum if total is None else total + part_sum
            merged[rows, :] = total.astype(bf16)
            return carry

        lax.fori_loop(0, 2, merge, 0, unroll=2)
        lane = lax.broadcasted_iota(jnp.int32, (1, 128), 1)
        blocks = [send_at[0:1, :] + (3 * (2 * m + lane // 64)).astype(f32) for m in range((len(ready) + 1) // 2)]
        where = jnp.concatenate(blocks, axis=1)[:, :size]
        pick = lax.broadcasted_iota(jnp.int32, (256, size), 0).astype(f32) == where
        fan = dot(jnp.where(pick, 1.0, 0.0).astype(bf16), merged[base : base + size, :])
        fan_out[part] = fan.astype(bf16).reshape(16, 16, 384)
        for k in FAR_FIRST:
            fan_copy(part, k).start()
        fan_in[part, lon] = fan_out[part, lon]

    xf[:, 1728:, :] = jnp.zeros((2, 32, 128), f32)
    back[:, 288:, :] = jnp.zeros((2, 8, 128), f32)
    lax.fori_loop(0, 6, step, 0)
    flush(1)

    for part in range(2):
        for k in FAR_FIRST:
            fan_copy(part, k).wait_recv()
        arrived = fan_in[part].reshape(256, 384)
        slot = lax.broadcasted_iota(jnp.int32, (48, 256), 1).astype(f32)
        picks = [
            jnp.where(slot == place_at[...][:, :1] + 3.0 * n, 1.0, 0.0).astype(bf16) for n in range(len(PARTS[part]))
        ]
        rows = dot(jnp.concatenate(picks, axis=0), arrived).astype(bf16)
        for n, i in enumerate(PARTS[part]):
            out[i] = rows[48 * n : 48 * n + 48]

    for n in range(24):
        half_copy(n // 8, (n // 2) % 4, n % 2).wait_send()
    for a in range(4):
        north_copy(a).wait_send()
    back_copy.wait_send()
    for part in range(2):
        for k in FAR_FIRST:
            fan_copy(part, k).wait_send()


VM = pl.BlockSpec(memory_space=pltpu.VMEM)
HB = pl.BlockSpec(memory_space=pl.ANY)
SM = pl.BlockSpec(memory_space=pltpu.SMEM)


def whole(idx, tables, gains, mgain, order, x, wq, wo, wu, wd, wm):
    v = pltpu.VMEM
    dma = pltpu.SemaphoreType.DMA
    return pl.pallas_call(
        kernel,
        out_shape=jax.ShapeDtypeStruct((9, 48, 384), bf16),
        in_specs=[SM] + [VM] * 4 + [HB] * 6,
        out_specs=VM,
        scratch_shapes=[
            v((3328, 128), jnp.int32),
            v((2, 128, 128), f32),
            v((144, 128), jnp.int32),
            v((144, 128), jnp.int32),
            v((2, 72 * PITCH, 128), f32),
            v((2, 24 * PITCH, 128), f32),
            v(x.shape, bf16),
            v((2, 1760, 128), f32),
            v((2, 12, 144, 192), f32),
            v((576, 576), bf16),
            v((576, 192), bf16),
            v((128, 192), bf16),
            v((128, 192), bf16),
            v((768, 192), bf16),
            v(wq.shape, bf16),
            v(wo.shape, bf16),
            v(wu.shape, bf16),
            v(wd.shape, bf16),
            v(wm.shape, bf16),
            v((8, 48, 192), f32),
            v((24, 48, 192), bf16),
            v((24, 48, 192), bf16),
            v((4, 48, 192), bf16),
            v((4, 48, 192), bf16),
            v((288, 192), f32),
            v((288, 192), bf16),
            v((288, 192), bf16),
            v((2, 296, 128), f32),
            v((4, 576, 192), f32),
            v((576, 384), bf16),
            v((2, 16, 16, 384), bf16),
            v((2, 16, 16, 384), bf16),
            v((8, 128), f32),
            v((48, 128), f32),
            dma((6,)),
            dma((24,)),
            dma((24,)),
            dma((4,)),
            dma((4,)),
            dma((1,)),
            dma((1,)),
            dma((2, 16)),
            dma((2, 16)),
        ],
        compiler_params=pltpu.CompilerParams(vmem_limit_bytes=60 << 20, collective_id=0, has_side_effects=True),
        name="whole_pair",
    )(idx, tables, gains, mgain, order, x, wq, wo, wu, wd, wm)


def body(
    fine_field,
    qkv_weight,
    out_weight,
    up_weight,
    down_weight,
    norm_gain,
    bias_table,
    bias_index,
    merge_gain,
    merge_weight,
    column_order,
):
    result = whole(
        bias_index.reshape(-1),
        bias_table.transpose(0, 1, 3, 2, 4),
        norm_gain,
        merge_gain,
        column_order,
        fine_field.transpose(1, 2, 0, 3),
        qkv_weight,
        out_weight,
        up_weight,
        down_weight.transpose(0, 2, 1),
        merge_weight.reshape(4, 192, 384),
    )
    return result.transpose(1, 0, 2)


def solution(mesh):
    in_specs = (
        P(None, "lat", "lon", None),
        P(),
        P(),
        P(),
        P(),
        P(),
        P(None, "lat", None, None, None),
        P(),
        P(),
        P(),
        P(),
    )
    out_specs = P("lon", "lat", None)
    return jax.shard_map(body, mesh=mesh, in_specs=in_specs, out_specs=out_specs, check_vma=False)
```
